128 devices in a mesh: dp: 64 (over x, y, z), seq: 2 (over core).
Axes of the slice: x: 4, y: 4, z: 4, core: 2. Of those that a mesh axis runs over, the one named last changes fastest.
Arguments:
- images: float32 [256, 48, 256], P('dp', None, 'seq'), may hold values from -6 to 6
- labels: int32 [256], P('dp'), may hold values from 0 to 999
- crop_sizes: int32 [256, 2], P('dp'), may hold values from 4 to 16, as said below
- latent_cotangent: float32 [256, 48, 256], P('dp', None, 'seq'), may hold values from -6 to 6
- logdet_cotangent: float32 [256], P('dp'), may hold values from -6 to 6
- weight_in: float32 [48, 768], P(None, ('dp', 'seq')), may hold values from -0.875 to 0.875
- moment_in: float32 [48, 768], P(None, ('dp', 'seq')), may hold values from -0.00024414062 to 0.00024414062
- second_in: float32 [48, 768], P(None, ('dp', 'seq')), may hold values from 3.768329e-09 to 5.0244388e-08
- class_table: float32 [1000, 768], P(None, ('dp', 'seq')), may hold values from -3 to 3
- moment_table: float32 [1000, 768], P(None, ('dp', 'seq')), may hold values from -0.00024414062 to 0.00024414062
- second_table: float32 [1000, 768], P(None, ('dp', 'seq')), may hold values from 3.768329e-09 to 5.0244388e-08
- weight_qkv: float32 [1, 768, 2304], P(None, ('dp', 'seq')), may hold values from -0.21875 to 0.21875
- moment_qkv: float32 [1, 768, 2304], P(None, ('dp', 'seq')), may hold values from -0.00024414062 to 0.00024414062
- second_qkv: float32 [1, 768, 2304], P(None, ('dp', 'seq')), may hold values from 3.768329e-09 to 5.0244388e-08
- weight_attn: float32 [1, 768, 768], P(None, ('dp', 'seq')), may hold values from -1.25 to 1.25
- moment_attn: float32 [1, 768, 768], P(None, ('dp', 'seq')), may hold values from -0.00024414062 to 0.00024414062
- second_attn: float32 [1, 768, 768], P(None, ('dp', 'seq')), may hold values from 3.768329e-09 to 5.0244388e-08
- weight_up: float32 [1, 768, 3072], P(None, ('dp', 'seq')), may hold values from -0.21875 to 0.21875
- moment_up: float32 [1, 768, 3072], P(None, ('dp', 'seq')), may hold values from -0.00024414062 to 0.00024414062
- second_up: float32 [1, 768, 3072], P(None, ('dp', 'seq')), may hold values from 3.768329e-09 to 5.0244388e-08
- weight_down: float32 [1, 3072, 768], P(None, None, ('dp', 'seq')), may hold values from -0.109375 to 0.109375
- moment_down: float32 [1, 3072, 768], P(None, None, ('dp', 'seq')), may hold values from -0.00024414062 to 0.00024414062
- second_down: float32 [1, 3072, 768], P(None, None, ('dp', 'seq')), may hold values from 3.768329e-09 to 5.0244388e-08
- weight_out: float32 [768, 96], P(('dp', 'seq')), may hold values from -0.109375 to 0.109375
- moment_out: float32 [768, 96], P(('dp', 'seq')), may hold values from -0.00024414062 to 0.00024414062
- second_out: float32 [768, 96], P(('dp', 'seq')), may hold values from 3.768329e-09 to 5.0244388e-08
- vectors: float32 [6, 768], P(None, ('dp', 'seq')), may hold values from -0.6 to 1.25
- moment_vectors: float32 [6, 768], P(None, ('dp', 'seq')), may hold values from -0.0009765625 to 0.0009765625
- second_vectors: float32 [6, 768], P(None, ('dp', 'seq')), may hold values from 6.280548e-08 to 8.039102e-07
Outputs:
- latents: float32 [256, 48, 256], P('dp', None, 'seq')
- logdet: float32 [256], P('dp')
- image_grad: float32 [256, 48, 256], P('dp', None, 'seq')
- grad_norm: float32 [], replicated
- moment_in_next: float32 [48, 768], P(None, ('dp', 'seq'))
- second_in_next: float32 [48, 768], P(None, ('dp', 'seq'))
- weight_in_next: float32 [48, 768], P(None, ('dp', 'seq'))
- moment_table_next: float32 [1000, 768], P(None, ('dp', 'seq'))
- second_table_next: float32 [1000, 768], P(None, ('dp', 'seq'))
- class_table_next: float32 [1000, 768], P(None, ('dp', 'seq'))
- moment_qkv_next: float32 [1, 768, 2304], P(None, ('dp', 'seq'))
- second_qkv_next: float32 [1, 768, 2304], P(None, ('dp', 'seq'))
- weight_qkv_next: float32 [1, 768, 2304], P(None, ('dp', 'seq'))
- moment_attn_next: float32 [1, 768, 768], P(None, ('dp', 'seq'))
- second_attn_next: float32 [1, 768, 768], P(None, ('dp', 'seq'))
- weight_attn_next: float32 [1, 768, 768], P(None, ('dp', 'seq'))
- moment_up_next: float32 [1, 768, 3072], P(None, ('dp', 'seq'))
- second_up_next: float32 [1, 768, 3072], P(None, ('dp', 'seq'))
- weight_up_next: float32 [1, 768, 3072], P(None, ('dp', 'seq'))
- moment_down_next: float32 [1, 3072, 768], P(None, None, ('dp', 'seq'))
- second_down_next: float32 [1, 3072, 768], P(None, None, ('dp', 'seq'))
- weight_down_next: float32 [1, 3072, 768], P(None, None, ('dp', 'seq'))
- moment_out_next: float32 [768, 96], P(('dp', 'seq'))
- second_out_next: float32 [768, 96], P(('dp', 'seq'))
- weight_out_next: float32 [768, 96], P(('dp', 'seq'))
- moment_vectors_next: float32 [6, 768], P(None, ('dp', 'seq'))
- second_vectors_next: float32 [6, 768], P(None, ('dp', 'seq'))
- vectors_next: float32 [6, 768], P(None, ('dp', 'seq'))
The draws below stay inside these ranges and needn't reach their ends.
Inputs may be any that keep to these rules, and one draw needn't show every extreme that they name: `crop_sizes`: in each aligned block of 4 crops one crop is 16 by 16.
All inputs are finite; a program needn't handle non-finite values.
Results may differ from the reference program's by a relative error of at most 0.0096.
Values may be sent and summed in bfloat16 or wider, within the bound.
No kernel may reach another device: no remote copies, remote signals or barrier semaphores. Data moves between devices by JAX's collectives and lax.ppermute only.
A program may use at most 192 MiB of HBM per device.

```python
import math
import jax
import jax.numpy as jnp
from jax import lax

D = 768
HEADS = 12
HEAD = 64
FF = 3072
CH = 48
CLASSES = 1000
SIDE = 16
LAYERS = 1
STEP = 5
ITEMS_DEV = 4
PATCHES = 256
ITEMS = 256
NVEC = 6
NPARAMS = 7961088


def draw_crop_sizes(key, part):
    key = jax.random.fold_in(key, 11)
    key_list = jax.random.split(key, 2)
    size_draw = jax.random.randint(key_list[0], (ITEMS, 2), SIDE // 4, SIDE + 1)
    block_count = ITEMS // ITEMS_DEV
    chosen = jax.random.randint(key_list[1], (block_count,), 0, ITEMS_DEV)
    full_item = jnp.arange(ITEMS) % ITEMS_DEV == jnp.repeat(chosen, ITEMS_DEV)
    return jnp.where(full_item[:, None], SIDE, size_draw).astype(jnp.int32)


def vector_rows(key, start_gain, rough_low, rough_high, bias_bound):
    key_list = jax.random.split(key, 2)
    column = jnp.arange(D, dtype=jnp.float32) / D
    rough = jax.random.uniform(key_list[0], (NVEC, D), jnp.float32, rough_low, rough_high)
    gains = (start_gain + (1.0 - start_gain) * column)[None, :] * rough
    biases = jax.random.uniform(key_list[1], (NVEC, D), jnp.float32, -bias_bound, bias_bound)
    gain_row = (jnp.arange(NVEC) % 2 == 1)[:, None]
    return jnp.where(gain_row, gains, biases)


def draw_vectors(key, part):
    key = jax.random.fold_in(key, 23)
    return vector_rows(key, 0.6, 0.8, 1.2, 0.5)


def with_ends(array, rng, low, top_value):
    spot = [jax.random.randint(jax.random.fold_in(rng, axis), (), 0, length) for axis, length in enumerate(array.shape)]
    widest = array.shape.index(max(array.shape))
    beside = spot[:widest] + [(spot[widest] + 1) % array.shape[widest]] + spot[widest + 1:]
    return array.at[tuple(spot)].set(low).at[tuple(beside)].set(top_value)


def block_levels(rng, dims, cuts, least, high):
    gain = 1.0
    for position, parts in cuts:
        draws = jax.random.uniform(jax.random.fold_in(jax.random.fold_in(rng, 6), position), (parts,), jnp.float32, least / len(cuts), high / len(cuts))
        gain = gain * jnp.repeat(jnp.exp(draws), dims[position] // parts).reshape((-1,) + (1,) * (len(dims) - 1 - position))
    return gain


def noise(own_key, extent, width, reach, shards=(), kind=jnp.bfloat16):
    gain = block_levels(own_key, extent, shards, -0.22, 0.18) if shards else 1.0
    entries = jax.random.normal(own_key, extent, jnp.float32) * width * gain
    return jnp.minimum(jnp.maximum(entries, -reach), reach).astype(kind)


def setup_inputs(seed: int = 0) -> dict:
    keys = jax.random.split(jax.random.key(seed), 30)
    images = noise(keys[0], (ITEMS, CH, PATCHES), 1.0, 6.0, ((0, 64), (2, 2)), jnp.float32)
    labels = with_ends(jax.random.randint(keys[1], (ITEMS,), 0, CLASSES), jax.random.fold_in(keys[1], 1), 0, CLASSES - 1).astype(jnp.int32)
    crop_sizes = draw_crop_sizes(jax.random.fold_in(keys[29], 71), 0)
    latent_cotangent = noise(keys[3], (ITEMS, CH, PATCHES), 1.0, 6.0, ((0, 64), (2, 2)), jnp.float32)
    logdet_cotangent = noise(keys[4], (ITEMS,), 1.0, 6.0, ((0, 64),), jnp.float32)
    weight_in = noise(keys[5], (CH, D), CH ** -0.5, 0.875, ((1, 128),), jnp.float32)
    moment_in = noise(keys[6], (CH, D), (0.11 / NPARAMS ** 0.5), 0.00024414062, ((1, 128),), jnp.float32)
    second_in = jnp.clip(jnp.exp(math.log(5.024438820555588e-08) - 2.5902671 * jax.random.uniform(keys[7], (CH, D), jnp.float32) ** block_levels(keys[7], (CH, D), ((1, 128),), -0.2, 0.2)), 3.768329204234533e-09, 5.024438820555588e-08)
    class_table = noise(keys[8], (CLASSES, D), 0.5, 3.0, ((1, 128),), jnp.float32)
    moment_table = noise(keys[9], (CLASSES, D), (0.11 / NPARAMS ** 0.5), 0.00024414062, ((1, 128),), jnp.float32)
    second_table = jnp.clip(jnp.exp(math.log(5.024438820555588e-08) - 2.5902671 * jax.random.uniform(keys[10], (CLASSES, D), jnp.float32) ** block_levels(keys[10], (CLASSES, D), ((1, 128),), -0.2, 0.2)), 3.768329204234533e-09, 5.024438820555588e-08)
    weight_qkv = noise(keys[11], (LAYERS, D, 3 * D), D ** -0.5, 0.21875, ((1, 128),), jnp.float32)
    moment_qkv = noise(keys[12], (LAYERS, D, 3 * D), (0.11 / NPARAMS ** 0.5), 0.00024414062, ((1, 128),), jnp.float32)
    second_qkv = jnp.clip(jnp.exp(math.log(5.024438820555588e-08) - 2.5902671 * jax.random.uniform(keys[13], (LAYERS, D, 3 * D), jnp.float32) ** block_levels(keys[13], (LAYERS, D, 3 * D), ((1, 128),), -0.2, 0.2)), 3.768329204234533e-09, 5.024438820555588e-08)
    weight_attn = noise(keys[14], (LAYERS, D, D), (D // 32) ** -0.5, 1.25, ((1, 128),), jnp.float32)
    moment_attn = noise(keys[15], (LAYERS, D, D), (0.11 / NPARAMS ** 0.5), 0.00024414062, ((1, 128),), jnp.float32)
    second_attn = jnp.clip(jnp.exp(math.log(5.024438820555588e-08) - 2.5902671 * jax.random.uniform(keys[16], (LAYERS, D, D), jnp.float32) ** block_levels(keys[16], (LAYERS, D, D), ((1, 128),), -0.2, 0.2)), 3.768329204234533e-09, 5.024438820555588e-08)
    weight_up = noise(keys[17], (LAYERS, D, FF), D ** -0.5, 0.21875, ((1, 128),), jnp.float32)
    moment_up = noise(keys[18], (LAYERS, D, FF), (0.11 / NPARAMS ** 0.5), 0.00024414062, ((1, 128),), jnp.float32)
    second_up = jnp.clip(jnp.exp(math.log(5.024438820555588e-08) - 2.5902671 * jax.random.uniform(keys[19], (LAYERS, D, FF), jnp.float32) ** block_levels(keys[19], (LAYERS, D, FF), ((1, 128),), -0.2, 0.2)), 3.768329204234533e-09, 5.024438820555588e-08)
    weight_down = noise(keys[20], (LAYERS, FF, D), FF ** -0.5, 0.109375, ((2, 128),), jnp.float32)
    moment_down = noise(keys[21], (LAYERS, FF, D), (0.11 / NPARAMS ** 0.5), 0.00024414062, ((2, 128),), jnp.float32)
    second_down = jnp.clip(jnp.exp(math.log(5.024438820555588e-08) - 2.5902671 * jax.random.uniform(keys[22], (LAYERS, FF, D), jnp.float32) ** block_levels(keys[22], (LAYERS, FF, D), ((2, 128),), -0.2, 0.2)), 3.768329204234533e-09, 5.024438820555588e-08)
    weight_out = noise(keys[23], (D, 2 * CH), (4 * D) ** -0.5, 0.109375, ((0, 128),), jnp.float32)
    moment_out = noise(keys[24], (D, 2 * CH), (0.11 / NPARAMS ** 0.5), 0.00024414062, ((0, 128),), jnp.float32)
    second_out = jnp.clip(jnp.exp(math.log(5.024438820555588e-08) - 2.5902671 * jax.random.uniform(keys[25], (D, 2 * CH), jnp.float32) ** block_levels(keys[25], (D, 2 * CH), ((0, 128),), -0.2, 0.2)), 3.768329204234533e-09, 5.024438820555588e-08)
    vectors = draw_vectors(jax.random.fold_in(keys[29], 71), 0)
    moment_vectors = noise(keys[27], (NVEC, D), (0.44 / NPARAMS ** 0.5), 0.0009765625, ((1, 128),), jnp.float32)
    second_vectors = jnp.clip(jnp.exp(math.log(8.039102112888941e-07) - 2.5494452 * jax.random.uniform(keys[28], (NVEC, D), jnp.float32) ** block_levels(keys[28], (NVEC, D), ((1, 128),), -0.2, 0.2)), 6.280548348058801e-08, 8.039102112888941e-07)
    return dict(images=images, labels=labels, crop_sizes=crop_sizes, latent_cotangent=latent_cotangent, logdet_cotangent=logdet_cotangent, weight_in=weight_in, moment_in=moment_in, second_in=second_in, class_table=class_table, moment_table=moment_table, second_table=second_table, weight_qkv=weight_qkv, moment_qkv=moment_qkv, second_qkv=second_qkv, weight_attn=weight_attn, moment_attn=moment_attn, second_attn=second_attn, weight_up=weight_up, moment_up=moment_up, second_up=second_up, weight_down=weight_down, moment_down=moment_down, second_down=second_down, weight_out=weight_out, moment_out=moment_out, second_out=second_out, vectors=vectors, moment_vectors=moment_vectors, second_vectors=second_vectors)


@jax.custom_vjp
def low(v):
    return lax.optimization_barrier(v.astype(jnp.bfloat16)).astype(jnp.float32)

@jax.custom_vjp
def low_back(v):
    return v

def low_keep(v):
    return (low(v), None)

def low_pass(kept, grad):
    return (grad,)

def back_keep(v):
    return (v, None)

def back_low(kept, grad):
    return (low(grad),)
low.defvjp(low_keep, low_pass)
low_back.defvjp(back_keep, back_low)
highest = lax.Precision.HIGHEST
beta_one = 0.9
beta_two = 0.95
adam_eps = 1e-08
step_rates = (0.02, 0.3, 0.02, 0.1, 0.02, 0.02, 0.02, 0.2)
decay_factors = (0.1, 0.1, 0.1, 0.1, 0.1, 0.1, 0.1, 0.0)
clip_norm = 1.0
norm_eps = 1e-06

def product(pattern, left_side, right_side):
    return jnp.einsum(pattern, left_side, right_side, precision=highest, preferred_element_type=jnp.float32)

def layer_norm(hidden, gain_row):
    row_mean = lax.optimization_barrier(jnp.mean(hidden, axis=-1, keepdims=True))
    centered = hidden - row_mean
    variance = lax.optimization_barrier(jnp.mean(centered * centered, axis=-1, keepdims=True))
    return centered * lax.rsqrt(variance + norm_eps) * gain_row

def valid_mask(positions, crop_sizes):
    natural = PATCHES - 1 - positions
    row_ok = (natural // SIDE)[None, :] < crop_sizes[:, 0:1]
    column_ok = (natural % SIDE)[None, :] < crop_sizes[:, 1:2]
    return row_ok & column_ok & (positions >= 0)[None, :]

def group_forward(parameters, images, labels, crop_sizes):
    weight_in, class_table, weight_qkv, weight_attn, weight_up, weight_down, weight_out, vectors = parameters
    item_count = images.shape[0]
    flow_in = jnp.transpose(images[:, :, ::-1], (0, 2, 1))
    shifted = jnp.concatenate([jnp.zeros_like(flow_in[:, :1]), flow_in[:, :-1]], axis=1)
    positions = jnp.arange(PATCHES, dtype=jnp.int32)
    valid = valid_mask(positions, crop_sizes)
    causal = positions[None, :] <= positions[:, None]
    diagonal = positions[None, :] == positions[:, None]
    allowed = causal[None] & (valid[:, None, :] | diagonal[None])
    hidden = low_back(product('ipc,cd->ipd', low(shifted), weight_in) + vectors[0] + class_table[labels][:, None, :])
    split_shape = (item_count, PATCHES, HEADS, HEAD)
    for layer_index in range(LAYERS):
        normed_one = low(layer_norm(hidden, vectors[1 + 4 * layer_index]))
        packed_qkv = low(low_back(product('ipd,de->ipe', normed_one, weight_qkv[layer_index])))
        queries = packed_qkv[..., :D].reshape(split_shape)
        key_all = packed_qkv[..., D:2 * D].reshape(split_shape)
        value_all = packed_qkv[..., 2 * D:].reshape(split_shape)
        scores = low_back(product('iqhe,ikhe->ihqk', queries, key_all) * HEAD ** (-0.5))
        scores = jnp.where(allowed[:, None], scores, -jnp.inf)
        row_max = lax.optimization_barrier(jnp.max(scores, axis=-1, keepdims=True))
        exponent = jnp.exp(scores - row_max)
        soft = low(exponent / lax.optimization_barrier(jnp.sum(exponent, axis=-1, keepdims=True)))
        mixed_out = low(low_back(product('ihqk,ikhe->iqhe', soft, value_all).reshape(item_count, PATCHES, D)))
        hidden = hidden + low_back(product('ipd,de->ipe', mixed_out, weight_attn[layer_index]) + vectors[2 + 4 * layer_index])
        normed_two = low(layer_norm(hidden, vectors[3 + 4 * layer_index]))
        up_proj = low_back(product('ipd,df->ipf', normed_two, weight_up[layer_index]))
        activated = low(jax.nn.gelu(up_proj))
        hidden = hidden + low_back(product('ipf,fd->ipd', activated, weight_down[layer_index]) + vectors[4 + 4 * layer_index])
    final_low = low(layer_norm(hidden, vectors[NVEC - 1]))
    output = low_back(product('ipd,de->ipe', final_low, weight_out))
    shift_mean = output[..., :CH]
    log_scale = output[..., CH:]
    latent = (flow_in - shift_mean) * jnp.exp(-log_scale)
    valid_float = valid.astype(jnp.float32)[..., None]
    latents = jnp.transpose(latent * valid_float, (0, 2, 1))
    logdet = -lax.optimization_barrier(jnp.sum(log_scale * valid_float, axis=(1, 2)))
    return (latents, logdet)

def forward(parameters, images, labels, crop_sizes):
    lowered = tuple((low(entry) for entry in parameters))
    group_size = 16
    group_count = ITEMS // group_size
    pieces = (images.reshape(group_count, group_size, CH, PATCHES), labels.reshape(group_count, group_size), crop_sizes.reshape(group_count, group_size, 2))

    def scan_step(carried, piece):
        return (carried, jax.checkpoint(group_forward)(lowered, piece[0], piece[1], piece[2]))
    carried, results = lax.scan(scan_step, jnp.zeros((), jnp.float32), pieces)
    return (results[0].reshape(ITEMS, CH, PATCHES), results[1].reshape(ITEMS))

def adam_update(weight, first_moment, second, gradient, factor, step_rate, decay_factor):
    clipped = gradient * factor
    first_new = beta_one * first_moment + (1.0 - beta_one) * clipped
    second_new = beta_two * second + (1.0 - beta_two) * clipped * clipped
    first_hat = first_new / (1.0 - beta_one ** STEP)
    second_hat = second_new / (1.0 - beta_two ** STEP)
    weight_new = weight - step_rate * (first_hat / (jnp.sqrt(second_hat) + adam_eps) + decay_factor * weight)
    return (first_new, second_new, weight_new)

def reference(images, labels, crop_sizes, latent_cotangent, logdet_cotangent, weight_in, moment_in, second_in, class_table, moment_table, second_table, weight_qkv, moment_qkv, second_qkv, weight_attn, moment_attn, second_attn, weight_up, moment_up, second_up, weight_down, moment_down, second_down, weight_out, moment_out, second_out, vectors, moment_vectors, second_vectors):
    parameters = (weight_in, class_table, weight_qkv, weight_attn, weight_up, weight_down, weight_out, vectors)
    firsts = (moment_in, moment_table, moment_qkv, moment_attn, moment_up, moment_down, moment_out, moment_vectors)
    seconds = (second_in, second_table, second_qkv, second_attn, second_up, second_down, second_out, second_vectors)

    def run(params_now, images_now):
        return forward(params_now, images_now, labels, crop_sizes)
    outputs, pullback = jax.vjp(run, parameters, images)
    latents, logdet = outputs
    gradients, image_grad = pullback((latent_cotangent, logdet_cotangent))
    squares = jnp.stack([jnp.sum(entry * entry) for entry in gradients])
    grad_norm = jnp.sqrt(jnp.sum(squares))
    factor = jnp.minimum(1.0, clip_norm / grad_norm)
    updated = []
    for index in range(8):
        updated.append(adam_update(parameters[index], firsts[index], seconds[index], gradients[index], factor, step_rates[index], decay_factors[index]))
    return (latents, logdet, image_grad, grad_norm, updated[0][0], updated[0][1], updated[0][2], updated[1][0], updated[1][1], updated[1][2], updated[2][0], updated[2][1], updated[2][2], updated[3][0], updated[3][1], updated[3][2], updated[4][0], updated[4][1], updated[4][2], updated[5][0], updated[5][1], updated[5][2], updated[6][0], updated[6][1], updated[6][2], updated[7][0], updated[7][1], updated[7][2])
```

```python
import functools

import jax
import jax.numpy as jnp
import numpy as np
from jax import lax
from jax.experimental import pallas as pl
from jax.experimental.pallas import tpu as pltpu
from jax.sharding import Mesh, PartitionSpec as P

D = 768
HEADS = 12
HEAD = 64
CH = 48
CLASSES = 1000
SIDE = 16
STEP = 5
PATCHES = 256
ITEMS = 256
FF = 3072
NVEC = 6
ROWS = 6
CROPS = 2

beta_one = 0.9
beta_two = 0.95
adam_eps = 1e-08
step_rates = (0.02, 0.3, 0.02, 0.1, 0.02, 0.02, 0.02, 0.2)
decay_factors = (0.1, 0.1, 0.1, 0.1, 0.1, 0.1, 0.1, 0.0)
clip_norm = 1.0
norm_eps = 1e-06

QKV = 3 * D
A_IN = QKV
A_VEC = A_IN + CH
A_LAB = A_VEC + NVEC
A_TABLE = QKV + 128
A_COLS = A_TABLE + 1024
B_UP = D
B_DOWN = B_UP + FF
B_OUT = B_DOWN + FF
B_END = B_OUT + 2 * CH
B_COLS = B_OUT + 128
G_VEC = QKV + CH
G_ITEM = QKV + 128
G_COLS = G_ITEM + ITEMS
G_CUT = 1152
B_CUT = 3584
B_REST = B_COLS - B_CUT

low = jnp.bfloat16
wide = jnp.float32


together = lax.optimization_barrier


def swap(value, axis, distance):
    size = lax.axis_size(axis)
    return lax.ppermute(value, axis, [(i, i ^ distance) for i in range(size)])


def gather_four(value, axis, dim):
    place = lax.axis_index(axis)
    parts = [value] + [swap(value, axis, k) for k in (1, 2, 3)]
    shape = value.shape[:dim] + (4,) + value.shape[dim:]
    result = jnp.zeros(shape, value.dtype)
    for k, part in enumerate(parts):
        result = lax.dynamic_update_index_in_dim(result, part, place ^ k, dim)
    return result


def scatter_four(piece, axis):
    place = lax.axis_index(axis)
    total = piece(place).astype(wide)
    for k in (1, 2, 3):
        total = total + swap(piece(place ^ k).astype(low), axis, k).astype(wide)
    return total


def order_matrix():
    natural = np.arange(D)
    place = (natural // ROWS) % 2 * (D // 2) + natural // (2 * ROWS) * ROWS + natural % ROWS
    return (place[:, None] == natural[None, :]).astype(low)


NN = (((1,), (0,)), ((), ()))
NT = (((1,), (1,)), ((), ()))
HALF = D // 2
TOKENS = CROPS * PATCHES
P_COLS = 1792
Q_COLS = 1664
Q_X = QKV - P_COLS
Q_TABLE = Q_X + 128
MASKED = -1e30
SCALE = HEAD ** (-0.5)
VMEM_BYTES = 58 * 1024 * 1024
COST = pl.CostEstimate(flops=1000, bytes_accessed=1000, transcendentals=0)


def dot(left_side, right_side, how=NN):
    return lax.dot_general(left_side, right_side, how, preferred_element_type=wide)


def iota(shape, axis):
    return lax.broadcasted_iota(jnp.int32, shape, axis)


def crop_valid(place, height, width):
    natural = PATCHES - 1 - place
    return ((natural >> 4) < height) & ((natural & 15) < width)


def norm_parts(value):
    mean = jnp.mean(value, axis=-1, keepdims=True)
    centered = value - mean
    scale = lax.rsqrt(jnp.mean(centered * centered, axis=-1, keepdims=True) + norm_eps)
    return centered * scale, scale


def norm_pull(normed, scale, gain, upstream):
    inner = upstream * gain
    to_input = scale * (
        inner
        - jnp.mean(inner, axis=-1, keepdims=True)
        - normed * jnp.mean(inner * normed, axis=-1, keepdims=True)
    )
    return to_input, jnp.sum(upstream * normed, axis=0, keepdims=True)


GELU_ROOT = 0.7978845608028654
GELU_CUBE = 0.044715


def gelu_tanh(value):
    return jnp.tanh(GELU_ROOT * (value + GELU_CUBE * (value * value * value)))


def front_kernel(
    labels, flow, p_own, p_far, q_own, q_far, hidden, normed, qkv, gains, entered, weights, sem
):
    copies = []
    for k, (source, row, start, width) in enumerate(
        ((q_own, 0, P_COLS, Q_COLS), (q_far, HALF, P_COLS, Q_COLS), (p_own, 0, 0, P_COLS), (p_far, HALF, 0, P_COLS))
    ):
        copies.append(
            pltpu.make_async_copy(source, weights.at[pl.ds(row, HALF), pl.ds(start, width)], sem.at[k])
        )
        copies[k].start()
    lane = iota((CH, PATCHES), 1)
    for i in range(CROPS):
        moved = jnp.where(lane == 0, 0.0, pltpu.roll(flow[i], 1, 1))
        below = jnp.where(iota((128 - CH, PATCHES), 0) == 0, 1.0, 0.0)
        both = jnp.concatenate([moved, below], axis=0)
        entered[i * PATCHES : (i + 1) * PATCHES, :] = both.T.astype(low)
    pick = (iota((8, 128), 1) == iota((8, 128), 0) + CH).astype(low)
    chosen = iota((8, 1024), 1) == jnp.where(iota((8, 1024), 0) == 0, labels[0], labels[1])
    chosen = chosen.astype(low)
    copies[0].wait()
    copies[1].wait()
    block = weights[:, QKV:A_TABLE]
    gains[...] = dot(pick, block, NT)
    class_rows = dot(chosen, weights[:, A_TABLE:], NT)
    for i in range(CROPS):
        rows = slice(i * PATCHES, (i + 1) * PATCHES)
        value = dot(entered[rows, :], block, NT) + class_rows[i : i + 1, :]
        hidden[rows, :] = value
        value, _ = norm_parts(value)
        normed[rows, :] = (value * gains[1:2, :]).astype(low)
    copies[2].wait()
    copies[3].wait()
    for start in range(0, QKV, 256):
        qkv[:, start : start + 256] = dot(normed[...], weights[:, start : start + 256]).astype(low)


def front(labels, flow, p_own, p_far, q_own, q_far):
    near, far = pl.BlockSpec(memory_space=pltpu.VMEM), pl.BlockSpec(memory_space=pl.ANY)
    return pl.pallas_call(
        front_kernel,
        out_shape=(
            jax.ShapeDtypeStruct((TOKENS, D), wide),
            jax.ShapeDtypeStruct((TOKENS, D), low),
            jax.ShapeDtypeStruct((TOKENS, QKV), low),
            jax.ShapeDtypeStruct((8, D), wide),
            jax.ShapeDtypeStruct((TOKENS, 128), low),
        ),
        in_specs=[pl.BlockSpec(memory_space=pltpu.SMEM), near] + [far] * 4,
        out_specs=(near,) * 5,
        scratch_shapes=[pltpu.VMEM((D, A_COLS), low), pltpu.SemaphoreType.DMA((4,))],
        compiler_params=pltpu.CompilerParams(vmem_limit_bytes=VMEM_BYTES),
        cost_estimate=COST,
        name="front",
    )(labels, flow, p_own, p_far, q_own, q_far)


HEAD_PAIRS = HEADS // 2
STEP_PAIRS = 3


def pair_blocks(pair):
    return slice(pair * 128, (pair + 1) * 128)


def head_masks():
    first = iota((PATCHES, 128), 1) < HEAD
    return first, jnp.logical_not(first)


def attend_kernel(sizes, queries, keys, values, mixed):
    crop = pl.program_id(0)
    shape = (PATCHES, PATCHES)
    place, key_place = iota(shape, 0), iota(shape, 1)
    valid = crop_valid(key_place, sizes[crop, 0], sizes[crop, 1])
    allowed = (key_place == place) | ((key_place < place) & valid)
    masks = head_masks()
    heads = [(pair, mine) for pair in range(STEP_PAIRS) for mine in masks]
    exponents, inverses = [], []
    for pair, mine in heads:
        block = pair_blocks(pair)
        scores = dot(queries[:, block] * low(SCALE), jnp.where(mine, keys[:, block], 0), NT)
        scores = jnp.where(allowed, scores, MASKED)
        exponent = jnp.exp(scores - jnp.max(scores, axis=-1, keepdims=True))
        exponents.append(exponent)
        inverses.append(1.0 / jnp.sum(exponent, axis=-1, keepdims=True))
    for pair in range(STEP_PAIRS):
        block = pair_blocks(pair)
        total = jnp.zeros((PATCHES, 128), wide)
        for k, mine in enumerate(masks):
            soft = (exponents[2 * pair + k] * inverses[2 * pair + k]).astype(low)
            total = total + dot(soft, jnp.where(mine, values[:, block], 0))
        mixed[:, block] = total.astype(low)


def attend(sizes, qkv):
    steps = HEAD_PAIRS // STEP_PAIRS
    shape = (PATCHES, STEP_PAIRS * 128)
    return pl.pallas_call(
        attend_kernel,
        grid=(CROPS, steps),
        out_shape=jax.ShapeDtypeStruct((TOKENS, D), low),
        in_specs=[pl.BlockSpec(memory_space=pltpu.SMEM)]
        + [pl.BlockSpec(shape, lambda i, h, s=s: (i, s * steps + h)) for s in range(3)],
        out_specs=pl.BlockSpec(shape, lambda i, h: (i, h)),
        compiler_params=pltpu.CompilerParams(vmem_limit_bytes=VMEM_BYTES),
        cost_estimate=COST,
        name="attend",
    )(sizes, qkv, qkv, qkv)


def attend_back_kernel(crop, sizes, queries, keys, values, d_mixed, d_queries, d_keys, d_values):
    shape = (PATCHES, PATCHES)
    key_place, place = iota(shape, 0), iota(shape, 1)
    valid = crop_valid(key_place, sizes[crop, 0], sizes[crop, 1])
    allowed = (key_place == place) | ((key_place < place) & valid)
    masks = head_masks()
    heads = [(pair, mine) for pair in range(STEP_PAIRS) for mine in masks]
    softs = []
    for pair, mine in heads:
        block = pair_blocks(pair)
        scores = dot(jnp.where(mine, keys[:, block], 0), queries[:, block] * low(SCALE), NT)
        scores = jnp.where(allowed, scores, MASKED)
        exponent = jnp.exp(scores - jnp.max(scores, axis=0, keepdims=True))
        softs.append(exponent * (1.0 / jnp.sum(exponent, axis=0, keepdims=True)))
    slopes = []
    for soft, (pair, mine) in zip(softs, heads):
        block = pair_blocks(pair)
        d_soft = dot(jnp.where(mine, values[:, block], 0), d_mixed[:, block], NT)
        d_scores = soft * (d_soft - jnp.sum(d_soft * soft, axis=0, keepdims=True))
        slopes.append(d_scores.astype(low))
    for pair in range(STEP_PAIRS):
        block = pair_blocks(pair)
        to_queries = jnp.zeros((PATCHES, 128), wide)
        to_keys = jnp.zeros((PATCHES, 128), wide)
        to_values = jnp.zeros((PATCHES, 128), wide)
        for k, mine in enumerate(masks):
            soft, slope = softs[2 * pair + k], slopes[2 * pair + k]
            to_values = to_values + dot(soft.astype(low), jnp.where(mine, d_mixed[:, block], 0))
            to_keys = to_keys + dot(slope, jnp.where(mine, queries[:, block] * low(SCALE), 0))
            to_queries = to_queries + dot(slope.T, jnp.where(mine, keys[:, block], 0))
        d_queries[:, block] = (to_queries * SCALE).astype(low)
        d_keys[:, block] = to_keys.astype(low)
        d_values[:, block] = to_values.astype(low)


def attend_back(crop, sizes, qkv, d_mixed):
    steps = HEAD_PAIRS // STEP_PAIRS
    shape = (PATCHES, STEP_PAIRS * 128)
    block = pl.BlockSpec(shape, lambda h: (0, h))
    return pl.pallas_call(
        functools.partial(attend_back_kernel, crop),
        grid=(steps,),
        out_shape=(jax.ShapeDtypeStruct((PATCHES, D), low),) * 3,
        in_specs=[pl.BlockSpec(memory_space=pltpu.SMEM)]
        + [pl.BlockSpec(shape, lambda h, s=s: (crop, s * steps + h)) for s in range(3)]
        + [pl.BlockSpec(shape, lambda h: (crop, h))],
        out_specs=(block,) * 3,
        compiler_params=pltpu.CompilerParams(vmem_limit_bytes=VMEM_BYTES),
        cost_estimate=COST,
        name="attend_back",
    )(sizes, qkv, qkv, qkv, d_mixed)


SECTIONS = ((0, D), (B_UP, FF), (B_DOWN, FF), (B_OUT, 128))
STEP_COLS = 512


def middle_kernel(
    core_ref, sizes, logdet_cot, hidden_in, mixed, gains, order, flow, latent_cot, b_own, b_far,
    latents, d_flow, logdet, d_hidden, d_mixed, vectors_out, keep_p, keep_q, send_p, send_q,
    weights, grads, up_proj, active, hidden, normed_two, branch, d_head, sem_in, sem_out,
):
    core = core_ref[0]
    keep, send = (keep_p, keep_q), (send_p, send_q)
    loads = []
    for k, (start, width) in enumerate(SECTIONS):
        pair = []
        for j, source in enumerate((b_own, b_far)):
            columns = pl.ds(start, width)
            target = weights.at[pl.ds(j * HALF, HALF), columns]
            copy = pltpu.make_async_copy(source.at[:, columns], target, sem_in.at[k, j])
            copy.start()
            pair.append(copy)
        loads.append(pair)
    stores = []

    def store(section):
        start, width = SECTIONS[section]
        for part, (low_end, high_end) in enumerate(((0, B_CUT), (B_CUT, B_COLS))):
            first, last = max(start, low_end), min(start + width, high_end)
            if first >= last:
                continue
            for j, target in enumerate((keep[part], send[part])):
                copy = pltpu.make_async_copy(
                    grads.at[pl.ds(j * HALF, HALF), pl.ds(first, last - first)],
                    target.at[:, pl.ds(first - low_end, last - first)],
                    sem_out.at[section, 2 * part + j],
                )
                copy.start()
                stores.append(copy)

    def arrived(section):
        for copy in loads[section]:
            copy.wait()

    def half_at(k):
        return pl.ds(pl.multiple_of((k ^ core) * HALF, 128), HALF)

    gain = lambda row: gains[row : row + 1, :]
    halves = (slice(0, HALF), slice(HALF, D))

    mixed_here = jnp.concatenate([dot(mixed[...], order[:, half_at(k)]) for k in range(2)], axis=1).astype(low)
    mixed_rows = mixed_here.T
    arrived(0)
    for k, columns in enumerate(halves):
        value = dot(mixed_here, weights[:, half_at(k)])
        hidden[:, columns] = hidden_in[:, columns] + value + gains[2:3, columns]

    value, _ = norm_parts(hidden[...])
    normed_two[...] = (value * gain(3)).astype(low)
    arrived(1)
    for step in range(0, FF, STEP_COLS):
        columns = slice(B_UP + step, B_UP + step + STEP_COLS)
        value = dot(normed_two[...], weights[:, columns])
        up_proj[:, step : step + STEP_COLS] = value
        active[:, step : step + STEP_COLS] = (0.5 * value * (1.0 + gelu_tanh(value))).astype(low)
    arrived(2)
    d_hidden[...] = hidden[...] + dot(active[...], weights[:, B_DOWN:B_OUT], NT) + gain(4)

    last, last_scale = norm_parts(d_hidden[...])
    final_rows = (last * gain(5)).astype(low).T
    arrived(3)
    head_rows = weights[:, B_OUT:].T
    output = dot(head_rows, final_rows)
    place = iota((CH, PATCHES), 1)
    for i in range(CROPS):
        columns = slice(i * PATCHES, (i + 1) * PATCHES)
        valid = crop_valid(place, sizes[i, 0], sizes[i, 1]).astype(wide)
        log_scale = output[CH : 2 * CH, columns]
        inverse = jnp.exp(-log_scale)
        latent = (flow[i] - output[:CH, columns]) * inverse
        latents[i] = latent * valid
        terms = jnp.sum(jnp.sum(log_scale * valid, axis=1, keepdims=True), axis=0, keepdims=True)
        logdet[8 * i : 8 * i + 8, :] = jnp.broadcast_to(-terms, (8, 128))
        d_latent = latent_cot[i] * valid
        to_flow = d_latent * inverse
        d_flow[i] = to_flow
        d_head[:CH, columns] = -to_flow
        d_head[CH : 2 * CH, columns] = -d_latent * latent - valid * logdet_cot[i]
        d_head[2 * CH :, columns] = jnp.zeros((128 - 2 * CH, PATCHES), wide)
    d_output = d_head[...].astype(low)
    d_output_rows = d_head[...].T.astype(low)
    grads[:, B_OUT:] = dot(final_rows, d_output, NT).astype(low)
    store(3)
    upstream = dot(d_output_rows, head_rows)
    to_input, to_gain = norm_pull(last, last_scale, gain(5), upstream)
    vectors_out[5:6, :] = to_gain
    d_hidden[...] = to_input

    edge = d_hidden[...].astype(low)
    vectors_out[4:5, :] = jnp.sum(edge.astype(wide), axis=0, keepdims=True)
    edge_rows = edge.T
    normed_rows = normed_two[...].T
    for step in range(0, FF, STEP_COLS):
        columns = slice(B_DOWN + step, B_DOWN + step + STEP_COLS)
        up_columns = slice(B_UP + step, B_UP + step + STEP_COLS)
        chunk = slice(step, step + STEP_COLS)
        d_active = dot(edge, weights[:, columns])
        grads[:, columns] = dot(edge_rows, active[:, chunk]).astype(low)
        value = up_proj[:, chunk]
        tanh = gelu_tanh(value)
        slope = 0.5 * (1.0 + tanh) + 0.5 * value * (1.0 - tanh * tanh) * GELU_ROOT * (
            1.0 + 3.0 * GELU_CUBE * value * value
        )
        d_up = (d_active * slope).astype(low)
        active[:, chunk] = d_up
        grads[:, up_columns] = dot(normed_rows, d_up).astype(low)
    store(2)
    store(1)
    upstream = dot(active[...], weights[:, B_UP:B_DOWN], NT)
    value, scale = norm_parts(hidden[...])
    to_input, to_gain = norm_pull(value, scale, gain(3), upstream)
    vectors_out[3:4, :] = to_gain
    d_hidden[...] = d_hidden[...] + to_input

    edge = d_hidden[...].astype(low)
    vectors_out[2:3, :] = jnp.sum(edge.astype(wide), axis=0, keepdims=True)
    vectors_out[0:2, :] = jnp.zeros((2, D), wide)
    vectors_out[6:8, :] = jnp.zeros((2, D), wide)
    branch[...] = edge
    parts = [branch[:, half_at(k)] for k in range(2)]
    natural = jnp.concatenate(parts, axis=1)
    grads[:, :D] = dot(mixed_rows, natural).astype(low)
    store(0)
    d_here = dot(natural, weights[:, :D], NT).astype(low)
    branch[...] = d_here
    natural = jnp.concatenate([branch[:, half_at(k)] for k in range(2)], axis=1)
    d_mixed[...] = dot(natural, order[...], NT).astype(low)
    for copy in stores:
        copy.wait()


def middle(core, sizes, logdet_cot, hidden, mixed, gains, order, flow, latent_cot, b_own, b_far):
    small = pl.BlockSpec(memory_space=pltpu.SMEM)
    near = pl.BlockSpec(memory_space=pltpu.VMEM)
    far = pl.BlockSpec(memory_space=pl.ANY)
    return pl.pallas_call(
        middle_kernel,
        out_shape=(
            jax.ShapeDtypeStruct((CROPS, CH, PATCHES), wide),
            jax.ShapeDtypeStruct((CROPS, CH, PATCHES), wide),
            jax.ShapeDtypeStruct((8 * CROPS, 128), wide),
            jax.ShapeDtypeStruct((TOKENS, D), wide),
            jax.ShapeDtypeStruct((TOKENS, D), low),
            jax.ShapeDtypeStruct((8, D), wide),
            jax.ShapeDtypeStruct((HALF, B_CUT), low),
            jax.ShapeDtypeStruct((HALF, B_REST), low),
            jax.ShapeDtypeStruct((HALF, B_CUT), low),
            jax.ShapeDtypeStruct((HALF, B_REST), low),
        ),
        in_specs=[small] * 3 + [near] * 6 + [far] * 2,
        out_specs=(near,) * 6 + (far,) * 4,
        scratch_shapes=[pltpu.VMEM((D, B_COLS), low)] * 2
        + [
            pltpu.VMEM((TOKENS, FF), wide),
            pltpu.VMEM((TOKENS, FF), low),
            pltpu.VMEM((TOKENS, D), wide),
            pltpu.VMEM((TOKENS, D), low),
            pltpu.VMEM((TOKENS, D), low),
            pltpu.VMEM((128, TOKENS), wide),
            pltpu.SemaphoreType.DMA((4, 2)),
            pltpu.SemaphoreType.DMA((4, 4)),
        ],
        compiler_params=pltpu.CompilerParams(vmem_limit_bytes=VMEM_BYTES),
        cost_estimate=COST,
        name="middle",
    )(core, sizes, logdet_cot, hidden, mixed, gains, order, flow, latent_cot, b_own, b_far)


def back_kernel(
    first_crop, dq0, dk0, dv0, dq1, dk1, dv1, normed, hidden, d_hidden, gains, vectors, entered, d_flow,
    p_own, p_far, q_own, q_far, keep, send, d_image, d_qkv, sums, weights, sem,
):
    copies = []
    for k, (source, row, start, width) in enumerate(
        ((p_own, 0, 0, P_COLS), (p_far, HALF, 0, P_COLS), (q_own, 0, P_COLS, Q_TABLE), (q_far, HALF, P_COLS, Q_TABLE))
    ):
        target = weights.at[pl.ds(row, HALF), pl.ds(start, width)]
        copies.append(pltpu.make_async_copy(source.at[:, pl.ds(0, width)], target, sem.at[k]))
        copies[k].start()
    for i, parts in enumerate(((dq0, dk0, dv0), (dq1, dk1, dv1))):
        for s, part in enumerate(parts):
            d_qkv[i * PATCHES : (i + 1) * PATCHES, s * D : (s + 1) * D] = part[...]
    normed_rows = normed[...].T
    for start in range(0, QKV, 256):
        columns = slice(start, start + 256)
        value = dot(normed_rows, d_qkv[:, columns]).astype(low)
        keep[:, columns] = value[:HALF]
        send[:, columns] = value[HALF:]
    for copy in copies:
        copy.wait()
    upstream = dot(d_qkv[...], weights[:, :QKV], NT)
    value, scale = norm_parts(hidden[...])
    to_input, to_gain = norm_pull(value, scale, gains[1:2, :], upstream)
    edge_rows = (d_hidden[...] + to_input).astype(low).T
    sums[...] = jnp.zeros((128, D), wide)
    sums[CH : CH + 8, :] = jnp.where(iota((8, D), 0) == 1, to_gain, vectors[...])
    owner = iota((TOKENS, ITEMS), 1) == first_crop[0] + (iota((TOKENS, ITEMS), 0) >> 8)
    value = (dot(edge_rows, entered[...]) + sums[...].T).astype(low)
    keep[:, QKV : QKV + 128] = value[:HALF]
    send[:, QKV : QKV + 128] = value[HALF:]
    value = dot(edge_rows, owner.astype(low)).astype(low)
    keep[:, QKV + 128 :] = value[:HALF]
    send[:, QKV + 128 :] = value[HALF:]
    d_shifted = dot(weights[:, QKV:].T, edge_rows)
    lane = iota((CH, PATCHES), 1)
    for i in range(CROPS):
        moved = pltpu.roll(d_shifted[:CH, i * PATCHES : (i + 1) * PATCHES], PATCHES - 1, 1)
        d_image[i] = d_flow[i] + jnp.where(lane == PATCHES - 1, 0.0, moved)


def back(first_crop, d_parts, normed, hidden, d_hidden, gains, vectors, entered, p_own, p_far, q_own, q_far, d_flow):
    near = pl.BlockSpec(memory_space=pltpu.VMEM)
    return pl.pallas_call(
        back_kernel,
        out_shape=(
            jax.ShapeDtypeStruct((HALF, G_COLS), low),
            jax.ShapeDtypeStruct((HALF, G_COLS), low),
            jax.ShapeDtypeStruct((CROPS, CH, PATCHES), wide),
        ),
        in_specs=[pl.BlockSpec(memory_space=pltpu.SMEM)] + [near] * 13 + [pl.BlockSpec(memory_space=pl.ANY)] * 4,
        out_specs=(near,) * 3,
        scratch_shapes=[
            pltpu.VMEM((TOKENS, QKV), low),
            pltpu.VMEM((128, D), wide),
            pltpu.VMEM((D, QKV + 128), low),
            pltpu.SemaphoreType.DMA((4,)),
        ],
        compiler_params=pltpu.CompilerParams(vmem_limit_bytes=VMEM_BYTES),
        cost_estimate=COST,
        name="back",
    )(first_crop, *d_parts, normed, hidden, d_hidden, gains, vectors, entered, d_flow, p_own, p_far, q_own, q_far)


WIDTHS = (QKV, D, FF, FF)
PACK_STARTS = (0, A_COLS, A_COLS + B_UP, A_COLS + B_DOWN)


def pack_kernel(labels, qkv, attn, up, down, entry, vectors, table, out, order, packed, wide_rows):
    wide_rows[...] = jnp.zeros(wide_rows.shape, wide)
    for source, start, width in zip((qkv, attn, up, down), PACK_STARTS, WIDTHS):
        for row in range(ROWS):
            wide_rows[row : row + 1, start : start + width] = source[row]
    start = A_COLS
    attn_rows = dot(wide_rows[:, start : start + D].astype(low), order[...])
    wide_rows[:, start : start + D] = attn_rows
    wide_rows[:ROWS, A_IN:A_VEC] = entry[...]
    lane = iota((8, 128), 1)
    marks = jnp.zeros((8, 128), wide)
    for i in range(2 * CROPS):
        first = (labels[i] >> 5).astype(wide)
        second = (labels[i] & 31).astype(wide)
        marks = jnp.where(lane == CH + NVEC + i, first, marks)
        marks = jnp.where(lane == CH + NVEC + 2 * CROPS + i, second, marks)
    wide_rows[:, A_IN:A_TABLE] = wide_rows[:, A_IN:A_TABLE] + marks
    same = iota((ROWS, ROWS), 0) == iota((ROWS, ROWS), 1)
    lane = iota((ROWS, 128), 1)
    for k in range(NVEC):
        across = jnp.broadcast_to(vectors[k : k + 1, :], (ROWS, ROWS))
        down_rows = jnp.sum(jnp.where(same, across, 0.0), axis=1, keepdims=True)
        wide_rows[:ROWS, A_IN:A_TABLE] = jnp.where(lane == CH + k, down_rows, wide_rows[:ROWS, A_IN:A_TABLE])
    wide_rows[:ROWS, A_TABLE : A_TABLE + CLASSES] = table[...]
    wide_rows[:ROWS, A_COLS + B_OUT : A_COLS + B_END] = out[...]
    packed[...] = wide_rows[:ROWS, :].astype(low)


def pack(labels, qkv, attn, up, down, entry, vectors, table, out, order):
    near = pl.BlockSpec(memory_space=pltpu.VMEM)
    return pl.pallas_call(
        pack_kernel,
        out_shape=jax.ShapeDtypeStruct((ROWS, A_COLS + B_COLS), low),
        in_specs=[pl.BlockSpec(memory_space=pltpu.SMEM)] + [near] * 9,
        out_specs=near,
        scratch_shapes=[pltpu.VMEM((8, A_COLS + B_COLS), wide)],
        compiler_params=pltpu.CompilerParams(vmem_limit_bytes=VMEM_BYTES),
        cost_estimate=COST,
        name="pack",
    )(labels, qkv, attn, up, down, entry, vectors, table, out, order)


R_UP = D
R_QKV = B_CUT
R_UP_REST = R_QKV + G_CUT
R_DOWN = R_UP_REST + B_DOWN - B_CUT
R_OUT = R_DOWN + FF
R_REST = R_OUT + 128
R_ENTRY = R_REST + QKV - G_CUT
R_ITEM = R_ENTRY + 128
R_COLS = R_ITEM + ITEMS


def finish_kernel(
    own, one, two, three, places, order, qkv, attn, up, down, entry, table, out, vectors, square, rows
):
    rows[...] = jnp.zeros(rows.shape, wide)
    total = own[...].astype(wide) + one[...].astype(wide) + two[...].astype(wide) + three[...].astype(wide)
    rows[:ROWS, :] = total
    rest = rows[:, :R_UP]
    swapped = jnp.zeros((8, D), wide)
    for _ in range(3):
        part = rest.astype(low)
        swapped = swapped + dot(part, order[...], NT)
        rest = rest - part.astype(wide)
    rows[:, :R_UP] = swapped
    pieces = (
        (qkv, 0, R_QKV, G_CUT),
        (qkv, G_CUT, R_REST, QKV - G_CUT),
        (attn, 0, 0, D),
        (up, 0, R_UP, B_CUT - D),
        (up, B_CUT - D, R_UP_REST, B_DOWN - B_CUT),
        (down, 0, R_DOWN, FF),
    )
    for target, first, start, width in pieces:
        for row in range(ROWS):
            target[row, :, first : first + width] = rows[row : row + 1, start : start + width]
    same = iota((ROWS, ROWS), 0) == iota((ROWS, ROWS), 1)
    for k in range(NVEC):
        at = R_ENTRY + CH + k
        down_rows = jnp.broadcast_to(rows[:ROWS, at : at + 1], (ROWS, ROWS))
        vectors[k : k + 1, :] = jnp.sum(jnp.where(same, down_rows, 0.0), axis=0, keepdims=True)
    entry[...] = rows[:ROWS, R_ENTRY : R_ENTRY + CH]
    out[...] = rows[:ROWS, R_OUT : R_OUT + 2 * CH]
    by_class = dot(rows[:, R_ITEM:].astype(low), places[...])
    table[...] = by_class[:ROWS, :]
    total = jnp.sum(jnp.square(by_class), axis=1, keepdims=True)
    for start in range(0, R_ITEM, 1216):
        total = total + jnp.sum(jnp.square(rows[:, start : start + 1216]), axis=1, keepdims=True)
    square[...] = jnp.broadcast_to(jnp.sum(total, axis=0, keepdims=True), (8, 128))


def finish(own, one, two, three, places, order):
    near = pl.BlockSpec(memory_space=pltpu.VMEM)
    flats = tuple(jax.ShapeDtypeStruct((ROWS, 1, width), wide) for width in WIDTHS)
    return pl.pallas_call(
        finish_kernel,
        out_shape=flats
        + (
            jax.ShapeDtypeStruct((ROWS, CH), wide),
            jax.ShapeDtypeStruct((ROWS, CLASSES), wide),
            jax.ShapeDtypeStruct((ROWS, 2 * CH), wide),
            jax.ShapeDtypeStruct((NVEC, ROWS), wide),
            jax.ShapeDtypeStruct((8, 128), wide),
        ),
        in_specs=[near] * 6,
        out_specs=(near,) * 9,
        scratch_shapes=[pltpu.VMEM((8, R_COLS), wide)],
        compiler_params=pltpu.CompilerParams(vmem_limit_bytes=VMEM_BYTES),
        cost_estimate=COST,
        name="finish",
    )(own, one, two, three, places, order)


def adam_kernel(*refs):
    squares, gradients, states = refs[:4], refs[4:12], refs[12:36]
    results, norm_out = refs[36:60], refs[60]
    norm = jnp.sqrt(squares[0][...] + squares[1][...] + squares[2][...] + squares[3][...])
    norm_out[...] = norm[0:1, 0:1]
    factor = jnp.minimum(1.0, clip_norm / norm)[0:1, 0:1]
    for index in range(8):
        weight, first, second = (ref[...] for ref in states[3 * index : 3 * index + 3])
        gradient = gradients[index][...]
        clipped = gradient * factor.reshape((1,) * gradient.ndim)
        first_new = beta_one * first + (1.0 - beta_one) * clipped
        second_new = beta_two * second + (1.0 - beta_two) * clipped * clipped
        first_hat = first_new / (1.0 - beta_one**STEP)
        second_hat = second_new / (1.0 - beta_two**STEP)
        weight_new = weight - step_rates[index] * (
            first_hat / (jnp.sqrt(second_hat) + adam_eps) + decay_factors[index] * weight
        )
        for k, value in enumerate((first_new, second_new, weight_new)):
            results[3 * index + k][...] = value


def adam(squares, gradients, states):
    near = pl.BlockSpec(memory_space=pltpu.VMEM)
    shapes = tuple(jax.ShapeDtypeStruct(value.shape, wide) for value in states)
    return pl.pallas_call(
        adam_kernel,
        out_shape=shapes + (jax.ShapeDtypeStruct((1, 1), wide),),
        in_specs=[near] * 36,
        out_specs=(near,) * 25,
        compiler_params=pltpu.CompilerParams(vmem_limit_bytes=VMEM_BYTES),
        cost_estimate=COST,
        name="adam",
    )(*squares, *gradients, *states)


P_SPLIT = (0, 1792, B_CUT)
Q_SPLIT = (0, 1792, B_REST)


def fold_kernel(places, keep_p, came_p, keep_q, came_q, *outs):
    distance = pl.program_id(0)
    for axis, (kept, came, split) in enumerate(((keep_p, came_p, P_SPLIT), (keep_q, came_q, Q_SPLIT))):
        for part in range(2):
            columns = slice(split[part], split[part + 1])
            own, other, sent = outs[6 * axis + 3 * part : 6 * axis + 3 * part + 3]
            first, second = (1, 3) if part == 0 else (3, 1)

            def total():
                return kept[..., columns].astype(wide) + came[..., columns].astype(wide)

            @pl.when(distance == 0)
            def _(own=own, total=total):
                own[...] = total().reshape(own.shape)

            @pl.when(distance == second)
            def _(other=other, total=total):
                other[...] = total().reshape(other.shape)

            @pl.when((distance == first) | (distance == 2))
            def _(sent=sent, total=total):
                sent[...] = total().reshape(sent.shape).astype(low)


def fold(places, keep_p, came_p, keep_q, came_q):
    by_x = lambda value: value.reshape(4, 4, 24, value.shape[1])
    in_x = pl.BlockSpec((1, 4, 24, B_CUT), lambda k, places: (places[0] ^ k, 0, 0, 0))
    in_y = pl.BlockSpec((4, 1, 24, B_REST), lambda k, places: (0, places[1] ^ k, 0, 0))
    shapes, specs = [], []
    for split in (P_SPLIT, Q_SPLIT):
        for part in range(2):
            width = split[part + 1] - split[part]
            shapes += [jax.ShapeDtypeStruct((4, 24, width), wide)] * 2
            specs += [pl.BlockSpec((4, 24, width), lambda k, places: (0, 0, 0))] * 2
            shapes.append(jax.ShapeDtypeStruct((2, 4, 24, width), low))
            slot = (lambda k, places: (k // 2, 0, 0, 0)) if part == 0 else (lambda k, places: (k // 3, 0, 0, 0))
            specs.append(pl.BlockSpec((1, 4, 24, width), slot))
    return pl.pallas_call(
        fold_kernel,
        grid_spec=pltpu.PrefetchScalarGridSpec(
            num_scalar_prefetch=1, grid=(4,), in_specs=[in_x, in_x, in_y, in_y], out_specs=specs
        ),
        out_shape=shapes,
        compiler_params=pltpu.CompilerParams(vmem_limit_bytes=VMEM_BYTES),
        cost_estimate=COST,
        name="fold",
    )(places, by_x(keep_p), by_x(came_p), by_x(keep_q), by_x(came_q))


def per_device(
    images,
    labels,
    crop_sizes,
    latent_cotangent,
    logdet_cotangent,
    weight_in,
    moment_in,
    second_in,
    class_table,
    moment_table,
    second_table,
    weight_qkv,
    moment_qkv,
    second_qkv,
    weight_attn,
    moment_attn,
    second_attn,
    weight_up,
    moment_up,
    second_up,
    weight_down,
    moment_down,
    second_down,
    weight_out,
    moment_out,
    second_out,
    vectors,
    moment_vectors,
    second_vectors,
):
    core = lax.axis_index("c")
    chip = lax.axis_index(("x", "y", "z"))
    half = PATCHES // 2

    order = order_matrix()
    rows_of = lambda value: jnp.transpose(value, (1, 0, 2))
    rows_down = lambda value: jnp.transpose(value, (2, 0, 1))
    packed = pack(
        labels, rows_of(weight_qkv), rows_of(weight_attn), rows_of(weight_up), rows_down(weight_down),
        weight_in.T, vectors, class_table.T, weight_out, order,
    )

    inputs = jnp.stack([images, latent_cotangent])
    mine = lax.dynamic_slice_in_dim(inputs, core * CROPS, CROPS, 1)
    theirs = swap(lax.dynamic_slice_in_dim(inputs, (1 - core) * CROPS, CROPS, 1), "c", 1)
    whole = jnp.where(
        core == 0,
        jnp.concatenate([mine, theirs], axis=-1),
        jnp.concatenate([theirs, mine], axis=-1),
    )
    flow = whole[0][:, :, ::-1]
    latent_cot = whole[1]
    logdet_cot = lax.dynamic_slice_in_dim(logdet_cotangent, core * CROPS, CROPS, 0)
    sizes = lax.dynamic_slice_in_dim(crop_sizes, core * CROPS, CROPS, 0)
    my_labels = lax.dynamic_slice_in_dim(labels, core * CROPS, CROPS, 0)

    gathered = gather_four(packed, "z", 0).reshape(4 * ROWS, A_COLS + B_COLS)
    b_own = lax.all_gather(gathered[:, A_COLS:], ("x", "y"), axis=0, tiled=True)
    p_own = gather_four(gather_four(gathered[:, :P_COLS], "y", 0), "x", 0).reshape(HALF, P_COLS)
    q_own = gather_four(gather_four(gathered[:, P_COLS:A_COLS], "x", 0), "y", 1).reshape(HALF, Q_COLS)
    p_far = swap(p_own, "c", 1)
    q_far = swap(q_own, "c", 1)

    hidden, normed, qkv, gains, entered = front(my_labels, flow, p_own, p_far, q_own, q_far)
    b_own, qkv = together((b_own, qkv))
    b_far = swap(b_own, "c", 1)
    mixed = attend(sizes, qkv)
    masked_latent, d_flow, logdet_rows, d_hidden, d_mixed, vector_rows, keep_p, keep_q, send_p, send_q = middle(
        core[None], sizes, logdet_cot, hidden, mixed, gains, order, flow, latent_cot, b_own, b_far
    )
    came_p, came_q = swap(send_p, "c", 1), swap(send_q, "c", 1)
    d_first = attend_back(0, sizes, qkv, d_mixed)
    came_p, came_q, d_first = together((came_p, came_q, d_first))
    places = jnp.stack([lax.axis_index("x"), lax.axis_index("y")])
    folded = fold(places, keep_p, came_p, keep_q, came_q)
    routes = (("x", 1), ("x", 3), ("y", 1), ("y", 3))
    sent, qkv_late = together((folded[2::3], qkv))
    came = [swap(value, axis, first) for value, (axis, first) in zip(sent, routes)]
    d_second = attend_back(1, sizes, qkv_late, d_mixed)
    came, d_second = together((came, d_second))
    mine, sent = [], []
    for k, (axis, first) in enumerate(routes):
        here, there = (0, 1) if first == 1 else (1, 0)
        mine.append(folded[3 * k] + came[k][here].astype(wide))
        sent.append((folded[3 * k + 1] + came[k][there].astype(wide)).astype(low))
    sent, mine, normed_late = together((sent, mine, normed))
    came = [swap(value, axis, first ^ 2) for value, (axis, first) in zip(sent, routes)]
    first_crop = (chip * 4 + core * CROPS)[None]
    keep_a, send_a, d_image = back(
        first_crop, (*d_first, *d_second), normed_late, hidden, d_hidden, gains, vector_rows, entered,
        p_own, p_far, q_own, q_far, d_flow,
    )
    came, send_a = together((came, send_a))
    came_a = swap(send_a, "c", 1)
    total_b = [(value + other.astype(wide)).astype(low) for value, other in zip(mine, came)]
    left_b = [value.reshape(96, -1) for value in total_b[:2]]
    right_b = total_b[2:]

    def of_x(kept, came, start, stop):
        def piece(place):
            part = lambda value: lax.dynamic_slice(value, (place * 96, start), (96, stop - start)).astype(wide)
            return part(kept) + part(came)

        return piece

    def of_y(kept, came, start, stop):
        def piece(place):
            part = lambda value: lax.dynamic_slice(
                value.reshape(4, 4, 24, value.shape[1]), (0, place, 0, start), (4, 1, 24, stop - start)
            )[:, 0].astype(wide)
            return part(kept) + part(came)

        return piece

    left_a = scatter_four(of_x(keep_a, came_a, 0, G_CUT), "x").astype(low)
    right_a = scatter_four(of_y(keep_a, came_a, G_CUT, G_COLS), "y").astype(low)
    left = jnp.concatenate([*left_b, left_a], axis=1).reshape(4, 24, B_CUT + G_CUT)
    right = jnp.concatenate([*right_b, right_a], axis=2)
    pick = lambda value: lambda place: lax.dynamic_index_in_dim(value, place, 0, keepdims=False)
    left = scatter_four(pick(left), "y").astype(low)
    right = scatter_four(pick(right), "x").astype(low)
    last = jnp.concatenate([left, right], axis=1).reshape(4, ROWS, R_COLS)
    level = lax.axis_index("z")
    parts = [lax.dynamic_index_in_dim(last, level ^ k, 0, keepdims=False) for k in range(4)]
    parts = [parts[0]] + [swap(parts[k], "z", k) for k in (1, 2, 3)]

    image_back = d_image[:, :, ::-1]
    logdet_own = logdet_rows[::8, 0]

    def to_places(value):
        kept = lax.dynamic_slice_in_dim(value, core * half, half, 2)
        came = swap(lax.dynamic_slice_in_dim(value, (1 - core) * half, half, 2), "c", 1)
        return jnp.where(
            core == 0, jnp.concatenate([kept, came], axis=0), jnp.concatenate([came, kept], axis=0)
        )

    latents = to_places(masked_latent)
    image_grad = to_places(image_back)
    came_logdet = swap(logdet_rows, "c", 1)[::8, 0]
    logdet = jnp.where(
        core == 0,
        jnp.concatenate([logdet_own, came_logdet]),
        jnp.concatenate([came_logdet, logdet_own]),
    )

    label_parts = q_own[::ROWS, Q_X + CH + NVEC : Q_X + CH + NVEC + 8].astype(wide).astype(jnp.int32)
    all_labels = (label_parts[:, :4] * 32 + label_parts[:, 4:]).reshape(ITEMS)
    class_places = (all_labels[:, None] == jnp.arange(CLASSES, dtype=jnp.int32)[None, :]).astype(low)
    *grads, grad_entry, grad_table, grad_out, grad_vectors, square = finish(*parts, class_places, order)
    square = square + swap(square, "c", 1)
    for axis in ("z", "y"):
        square = square + swap(square, axis, 1) + swap(square, axis, 2) + swap(square, axis, 3)
    squares = [square] + [swap(square, "x", k) for k in (1, 2, 3)]

    rows_back = lambda value: jnp.transpose(value, (1, 0, 2))
    turned = lambda value: value.T
    same = lambda value: value
    views = (
        (turned, turned, grad_entry),
        (turned, turned, grad_table),
        (rows_of, rows_back, grads[0]),
        (rows_of, rows_back, grads[1]),
        (rows_of, rows_back, grads[2]),
        (rows_down, lambda value: jnp.transpose(value, (1, 2, 0)), grads[3]),
        (same, same, grad_out),
        (same, same, grad_vectors),
    )
    states = (
        (weight_in, moment_in, second_in),
        (class_table, moment_table, second_table),
        (weight_qkv, moment_qkv, second_qkv),
        (weight_attn, moment_attn, second_attn),
        (weight_up, moment_up, second_up),
        (weight_down, moment_down, second_down),
        (weight_out, moment_out, second_out),
        (vectors, moment_vectors, second_vectors),
    )
    entered_states = [view[0](value) for view, group in zip(views, states) for value in group]
    *results, norm = adam(squares, [view[2] for view in views], entered_states)
    updated = [views[k // 3][1](value) for k, value in enumerate(results)]
    return (latents, logdet, image_grad, norm.reshape(()), *updated)


def solution(mesh):
    chips = Mesh(mesh.devices.reshape(4, 4, 4, 2), ("x", "y", "z", "c"))
    dp, every = ("x", "y", "z"), ("x", "y", "z", "c")
    patches = P(dp, None, "c")
    columns, rows, last = P(None, every), P(None, every, None), P(None, None, every)
    parameters = (columns,) * 6 + (rows,) * 9 + (last,) * 3 + (P(every, None),) * 3 + (columns,) * 3
    return jax.shard_map(
        per_device,
        mesh=chips,
        in_specs=(patches, P(dp), P(dp, None), patches, P(dp)) + parameters,
        out_specs=(patches, P(dp), patches, P()) + parameters,
        check_vma=False,
    )
```

```python
import functools

import jax
import jax.numpy as jnp
import numpy as np
from jax import lax
from jax.experimental import pallas as pl
from jax.experimental.pallas import tpu as pltpu
from jax.sharding import Mesh, PartitionSpec as P

D = 768
HEADS = 12
HEAD = 64
CH = 48
CLASSES = 1000
SIDE = 16
STEP = 5
PATCHES = 256
ITEMS = 256
FF = 3072
NVEC = 6
ROWS = 6
CROPS = 2

beta_one = 0.9
beta_two = 0.95
adam_eps = 1e-08
step_rates = (0.02, 0.3, 0.02, 0.1, 0.02, 0.02, 0.02, 0.2)
decay_factors = (0.1, 0.1, 0.1, 0.1, 0.1, 0.1, 0.1, 0.0)
clip_norm = 1.0
norm_eps = 1e-06

QKV = 3 * D
A_IN = QKV
A_VEC = A_IN + CH
A_LAB = A_VEC + NVEC
A_TABLE = QKV + 128
A_OUT = A_TABLE + 1024
A_COLS = A_OUT + 128
M_ATTN = 2 * FF
M_COLS = M_ATTN + D
B_UP = D
B_DOWN = B_UP + FF
B_OUT = B_DOWN + FF
B_END = B_OUT + 2 * CH
B_COLS = B_OUT + 128
G_VEC = QKV + CH
G_ITEM = QKV + 128
G_COLS = G_ITEM + ITEMS
G_CUT = 1408
B_CUT = 3584
B_REST = B_COLS - B_CUT

low = jnp.bfloat16
wide = jnp.float32


together = lax.optimization_barrier


def swap(value, axis, distance):
    size = lax.axis_size(axis)
    return lax.ppermute(value, axis, [(i, i ^ distance) for i in range(size)])


def gather_four(value, axis, dim):
    place = lax.axis_index(axis)
    parts = [value] + [swap(value, axis, k) for k in (1, 2, 3)]
    shape = value.shape[:dim] + (4,) + value.shape[dim:]
    result = jnp.zeros(shape, value.dtype)
    for k, part in enumerate(parts):
        result = lax.dynamic_update_index_in_dim(result, part, place ^ k, dim)
    return result


def scatter_four(piece, axis):
    place = lax.axis_index(axis)
    total = piece(place).astype(wide)
    for k in (1, 2, 3):
        total = total + swap(piece(place ^ k).astype(low), axis, k).astype(wide)
    return total


def order_matrix():
    natural = np.arange(D)
    place = (natural // ROWS) % 2 * (D // 2) + natural // (2 * ROWS) * ROWS + natural % ROWS
    return (place[:, None] == natural[None, :]).astype(low)


NN = (((1,), (0,)), ((), ()))
NT = (((1,), (1,)), ((), ()))
HALF = D // 2
TOKENS = CROPS * PATCHES
P_COLS = A_COLS // 2
Q_COLS = A_COLS // 2
Q_X = QKV - P_COLS
Q_TABLE = Q_X + 128
Q_OUT = Q_TABLE + 1024
MASKED = -1e30
SCALE = HEAD ** (-0.5)
MIB = 1024 * 1024
VMEM_BYTES = 58 * MIB
COST = pl.CostEstimate(flops=1000, bytes_accessed=1000, transcendentals=0)


def dot(left_side, right_side, how=NN):
    return lax.dot_general(left_side, right_side, how, preferred_element_type=wide)


def iota(shape, axis):
    return lax.broadcasted_iota(jnp.int32, shape, axis)


def crop_valid(place, height, width):
    natural = PATCHES - 1 - place
    return ((natural >> 4) < height) & ((natural & 15) < width)


def norm_parts(value):
    mean = jnp.mean(value, axis=-1, keepdims=True)
    centered = value - mean
    scale = lax.rsqrt(jnp.mean(centered * centered, axis=-1, keepdims=True) + norm_eps)
    return centered * scale, scale


def norm_pull(normed, scale, gain, upstream):
    inner = upstream * gain
    to_input = scale * (
        inner
        - jnp.mean(inner, axis=-1, keepdims=True)
        - normed * jnp.mean(inner * normed, axis=-1, keepdims=True)
    )
    return to_input, jnp.sum(upstream * normed, axis=0, keepdims=True)


GELU_ROOT = 0.7978845608028654
GELU_CUBE = 0.044715


def gelu_tanh(value):
    return jnp.tanh(GELU_ROOT * (value + GELU_CUBE * (value * value * value)))


def front_kernel(
    labels, flow, p_own, p_far, q_own, q_far, hidden, normed, qkv, gains, entered, weights, sem
):
    copies = []
    for k, (source, row, start, width) in enumerate(
        ((q_own, 0, P_COLS, Q_OUT), (q_far, HALF, P_COLS, Q_OUT), (p_own, 0, 0, P_COLS), (p_far, HALF, 0, P_COLS))
    ):
        copies.append(
            pltpu.make_async_copy(
                source.at[:, pl.ds(0, width)], weights.at[pl.ds(row, HALF), pl.ds(start, width)], sem.at[k]
            )
        )
        copies[k].start()
    lane = iota((CH, PATCHES), 1)
    for i in range(CROPS):
        moved = jnp.where(lane == 0, 0.0, pltpu.roll(flow[i], 1, 1))
        below = jnp.where(iota((128 - CH, PATCHES), 0) == 0, 1.0, 0.0)
        both = jnp.concatenate([moved, below], axis=0)
        entered[i * PATCHES : (i + 1) * PATCHES, :] = both.T.astype(low)
    pick = (iota((8, 128), 1) == iota((8, 128), 0) + CH).astype(low)
    chosen = iota((8, 1024), 1) == jnp.where(iota((8, 1024), 0) == 0, labels[0], labels[1])
    chosen = chosen.astype(low)
    copies[0].wait()
    copies[1].wait()
    block = weights[:, QKV:A_TABLE]
    gains[...] = dot(pick, block, NT)
    class_rows = dot(chosen, weights[:, A_TABLE:], NT)
    for i in range(CROPS):
        rows = slice(i * PATCHES, (i + 1) * PATCHES)
        value = dot(entered[rows, :], block, NT) + class_rows[i : i + 1, :]
        hidden[rows, :] = value
        value, _ = norm_parts(value)
        normed[rows, :] = (value * gains[1:2, :]).astype(low)
    copies[2].wait()
    copies[3].wait()
    for start in range(0, QKV, 256):
        qkv[:, start : start + 256] = dot(normed[...], weights[:, start : start + 256]).astype(low)


def front(labels, flow, p_own, p_far, q_own, q_far):
    near, far = pl.BlockSpec(memory_space=pltpu.VMEM), pl.BlockSpec(memory_space=pl.ANY)
    return pl.pallas_call(
        front_kernel,
        out_shape=(
            jax.ShapeDtypeStruct((TOKENS, D), wide),
            jax.ShapeDtypeStruct((TOKENS, D), low),
            jax.ShapeDtypeStruct((TOKENS, QKV), low),
            jax.ShapeDtypeStruct((8, D), wide),
            jax.ShapeDtypeStruct((TOKENS, 128), low),
        ),
        in_specs=[pl.BlockSpec(memory_space=pltpu.SMEM), near] + [far] * 4,
        out_specs=(near,) * 5,
        scratch_shapes=[pltpu.VMEM((D, A_OUT), low), pltpu.SemaphoreType.DMA((4,))],
        compiler_params=pltpu.CompilerParams(vmem_limit_bytes=VMEM_BYTES),
        cost_estimate=COST,
        name="front",
    )(labels, flow, p_own, p_far, q_own, q_far)


HEAD_PAIRS = HEADS // 2
STEP_PAIRS = 3


def pair_blocks(pair):
    return slice(pair * 128, (pair + 1) * 128)


def head_masks():
    first = iota((PATCHES, 128), 1) < HEAD
    return first, jnp.logical_not(first)


def attend_kernel(sizes, queries, keys, values, mixed):
    crop = pl.program_id(0)
    shape = (PATCHES, PATCHES)
    place, key_place = iota(shape, 0), iota(shape, 1)
    valid = crop_valid(key_place, sizes[crop, 0], sizes[crop, 1])
    allowed = (key_place == place) | ((key_place < place) & valid)
    masks = head_masks()
    heads = [(pair, mine) for pair in range(STEP_PAIRS) for mine in masks]
    exponents, inverses = [], []
    for pair, mine in heads:
        block = pair_blocks(pair)
        scores = dot(queries[:, block] * low(SCALE), jnp.where(mine, keys[:, block], 0), NT)
        scores = jnp.where(allowed, scores, MASKED)
        exponent = jnp.exp(scores - jnp.max(scores, axis=-1, keepdims=True))
        exponents.append(exponent)
        inverses.append(1.0 / jnp.sum(exponent, axis=-1, keepdims=True))
    for pair in range(STEP_PAIRS):
        block = pair_blocks(pair)
        total = jnp.zeros((PATCHES, 128), wide)
        for k, mine in enumerate(masks):
            soft = (exponents[2 * pair + k] * inverses[2 * pair + k]).astype(low)
            total = total + dot(soft, jnp.where(mine, values[:, block], 0))
        mixed[:, block] = total.astype(low)


def attend(sizes, qkv):
    steps = HEAD_PAIRS // STEP_PAIRS
    shape = (PATCHES, STEP_PAIRS * 128)
    return pl.pallas_call(
        attend_kernel,
        grid=(CROPS, steps),
        out_shape=jax.ShapeDtypeStruct((TOKENS, D), low),
        in_specs=[pl.BlockSpec(memory_space=pltpu.SMEM)]
        + [pl.BlockSpec(shape, lambda i, h, s=s: (i, s * steps + h)) for s in range(3)],
        out_specs=pl.BlockSpec(shape, lambda i, h: (i, h)),
        compiler_params=pltpu.CompilerParams(vmem_limit_bytes=16 * MIB),
        cost_estimate=COST,
        name="attend",
    )(sizes, qkv, qkv, qkv)


def attend_back_kernel(crop, sizes, queries, keys, values, d_mixed, d_queries, d_keys, d_values):
    shape = (PATCHES, PATCHES)
    key_place, place = iota(shape, 0), iota(shape, 1)
    valid = crop_valid(key_place, sizes[crop, 0], sizes[crop, 1])
    allowed = (key_place == place) | ((key_place < place) & valid)
    masks = head_masks()
    heads = [(pair, mine) for pair in range(STEP_PAIRS) for mine in masks]
    softs = []
    for pair, mine in heads:
        block = pair_blocks(pair)
        scores = dot(jnp.where(mine, keys[:, block], 0), queries[:, block] * low(SCALE), NT)
        scores = jnp.where(allowed, scores, MASKED)
        exponent = jnp.exp(scores - jnp.max(scores, axis=0, keepdims=True))
        softs.append(exponent * (1.0 / jnp.sum(exponent, axis=0, keepdims=True)))
    slopes = []
    for soft, (pair, mine) in zip(softs, heads):
        block = pair_blocks(pair)
        d_soft = dot(jnp.where(mine, values[:, block], 0), d_mixed[:, block], NT)
        d_scores = soft * (d_soft - jnp.sum(d_soft * soft, axis=0, keepdims=True))
        slopes.append(d_scores.astype(low))
    for pair in range(STEP_PAIRS):
        block = pair_blocks(pair)
        to_queries = jnp.zeros((PATCHES, 128), wide)
        to_keys = jnp.zeros((PATCHES, 128), wide)
        to_values = jnp.zeros((PATCHES, 128), wide)
        for k, mine in enumerate(masks):
            soft, slope = softs[2 * pair + k], slopes[2 * pair + k]
            to_values = to_values + dot(soft.astype(low), jnp.where(mine, d_mixed[:, block], 0))
            to_keys = to_keys + dot(slope, jnp.where(mine, queries[:, block] * low(SCALE), 0))
            to_queries = to_queries + dot(slope.T, jnp.where(mine, keys[:, block], 0))
        d_queries[:, block] = (to_queries * SCALE).astype(low)
        d_keys[:, block] = to_keys.astype(low)
        d_values[:, block] = to_values.astype(low)


def attend_back(crop, sizes, qkv, d_mixed):
    steps = HEAD_PAIRS // STEP_PAIRS
    shape = (PATCHES, STEP_PAIRS * 128)
    block = pl.BlockSpec(shape, lambda h: (0, h))
    return pl.pallas_call(
        functools.partial(attend_back_kernel, crop),
        grid=(steps,),
        out_shape=(jax.ShapeDtypeStruct((PATCHES, D), low),) * 3,
        in_specs=[pl.BlockSpec(memory_space=pltpu.SMEM)]
        + [pl.BlockSpec(shape, lambda h, s=s: (crop, s * steps + h)) for s in range(3)]
        + [pl.BlockSpec(shape, lambda h: (crop, h))],
        out_specs=(block,) * 3,
        compiler_params=pltpu.CompilerParams(vmem_limit_bytes=16 * MIB),
        cost_estimate=COST,
        name="attend_back",
    )(sizes, qkv, qkv, qkv, d_mixed)


SECTIONS = ((0, D), (B_UP, FF), (B_DOWN, FF), (B_OUT, 128))
STEP_COLS = 512


def middle_kernel(
    core_ref, sizes, logdet_cot, hidden_in, mixed, gains, order, flow, latent_cot, q_own, q_far, b_own, b_far,
    latents, d_flow, logdet, d_hidden, d_mixed, vectors_out, keep_p, keep_q, send_p, send_q,
    weights, grads, up_proj, active, hidden, normed_two, branch, d_head, sem_in, sem_out,
):
    core = core_ref[0]
    keep, send = (keep_p, keep_q), (send_p, send_q)
    loads = []
    for k, (start, width) in enumerate(SECTIONS):
        pair = []
        for j, (first, second) in enumerate(((q_own, b_own), (q_far, b_far))):
            source, at = ((second, M_ATTN), (second, 0), (second, FF), (first, Q_OUT))[k]
            target = weights.at[pl.ds(j * HALF, HALF), pl.ds(start, width)]
            copy = pltpu.make_async_copy(source.at[:, pl.ds(at, width)], target, sem_in.at[k, j])
            copy.start()
            pair.append(copy)
        loads.append(pair)
    stores = []

    def store(section):
        start, width = SECTIONS[section]
        for part, (low_end, high_end) in enumerate(((0, B_CUT), (B_CUT, B_COLS))):
            first, last = max(start, low_end), min(start + width, high_end)
            if first >= last:
                continue
            for j, target in enumerate((keep[part], send[part])):
                copy = pltpu.make_async_copy(
                    grads.at[pl.ds(j * HALF, HALF), pl.ds(first, last - first)],
                    target.at[:, pl.ds(first - low_end, last - first)],
                    sem_out.at[section, 2 * part + j],
                )
                copy.start()
                stores.append(copy)

    def arrived(section):
        for copy in loads[section]:
            copy.wait()

    def half_at(k):
        return pl.ds(pl.multiple_of((k ^ core) * HALF, 128), HALF)

    gain = lambda row: gains[row : row + 1, :]
    halves = (slice(0, HALF), slice(HALF, D))

    mixed_here = jnp.concatenate([dot(mixed[...], order[:, half_at(k)]) for k in range(2)], axis=1).astype(low)
    mixed_rows = mixed_here.T
    arrived(0)
    for k, columns in enumerate(halves):
        value = dot(mixed_here, weights[:, half_at(k)])
        hidden[:, columns] = hidden_in[:, columns] + value + gains[2:3, columns]

    value, _ = norm_parts(hidden[...])
    normed_two[...] = (value * gain(3)).astype(low)
    arrived(1)
    for step in range(0, FF, STEP_COLS):
        columns = slice(B_UP + step, B_UP + step + STEP_COLS)
        value = dot(normed_two[...], weights[:, columns])
        up_proj[:, step : step + STEP_COLS] = value
        active[:, step : step + STEP_COLS] = (0.5 * value * (1.0 + gelu_tanh(value))).astype(low)
    arrived(2)
    d_hidden[...] = hidden[...] + dot(active[...], weights[:, B_DOWN:B_OUT], NT) + gain(4)

    last, last_scale = norm_parts(d_hidden[...])
    final_rows = (last * gain(5)).astype(low).T
    arrived(3)
    head_rows = weights[:, B_OUT:].T
    output = dot(head_rows, final_rows)
    place = iota((CH, PATCHES), 1)
    for i in range(CROPS):
        columns = slice(i * PATCHES, (i + 1) * PATCHES)
        valid = crop_valid(place, sizes[i, 0], sizes[i, 1]).astype(wide)
        log_scale = output[CH : 2 * CH, columns]
        inverse = jnp.exp(-log_scale)
        latent = (flow[i] - output[:CH, columns]) * inverse
        latents[i] = latent * valid
        terms = jnp.sum(jnp.sum(log_scale * valid, axis=1, keepdims=True), axis=0, keepdims=True)
        logdet[8 * i : 8 * i + 8, :] = jnp.broadcast_to(-terms, (8, 128))
        d_latent = latent_cot[i] * valid
        to_flow = d_latent * inverse
        d_flow[i] = to_flow
        d_head[:CH, columns] = -to_flow
        d_head[CH : 2 * CH, columns] = -d_latent * latent - valid * logdet_cot[i]
        d_head[2 * CH :, columns] = jnp.zeros((128 - 2 * CH, PATCHES), wide)
    d_output = d_head[...].astype(low)
    d_output_rows = d_head[...].T.astype(low)
    grads[:, B_OUT:] = dot(final_rows, d_output, NT).astype(low)
    store(3)
    upstream = dot(d_output_rows, head_rows)
    to_input, to_gain = norm_pull(last, last_scale, gain(5), upstream)
    vectors_out[5:6, :] = to_gain
    d_hidden[...] = to_input

    edge = d_hidden[...].astype(low)
    vectors_out[4:5, :] = jnp.sum(edge.astype(wide), axis=0, keepdims=True)
    edge_rows = edge.T
    normed_rows = normed_two[...].T
    for step in range(0, FF, STEP_COLS):
        columns = slice(B_DOWN + step, B_DOWN + step + STEP_COLS)
        up_columns = slice(B_UP + step, B_UP + step + STEP_COLS)
        chunk = slice(step, step + STEP_COLS)
        d_active = dot(edge, weights[:, columns])
        grads[:, columns] = dot(edge_rows, active[:, chunk]).astype(low)
        value = up_proj[:, chunk]
        tanh = gelu_tanh(value)
        slope = 0.5 * (1.0 + tanh) + 0.5 * value * (1.0 - tanh * tanh) * GELU_ROOT * (
            1.0 + 3.0 * GELU_CUBE * value * value
        )
        d_up = (d_active * slope).astype(low)
        active[:, chunk] = d_up
        grads[:, up_columns] = dot(normed_rows, d_up).astype(low)
    store(2)
    store(1)
    upstream = dot(active[...], weights[:, B_UP:B_DOWN], NT)
    value, scale = norm_parts(hidden[...])
    to_input, to_gain = norm_pull(value, scale, gain(3), upstream)
    vectors_out[3:4, :] = to_gain
    d_hidden[...] = d_hidden[...] + to_input

    edge = d_hidden[...].astype(low)
    vectors_out[2:3, :] = jnp.sum(edge.astype(wide), axis=0, keepdims=True)
    vectors_out[0:2, :] = jnp.zeros((2, D), wide)
    vectors_out[6:8, :] = jnp.zeros((2, D), wide)
    branch[...] = edge
    parts = [branch[:, half_at(k)] for k in range(2)]
    natural = jnp.concatenate(parts, axis=1)
    grads[:, :D] = dot(mixed_rows, natural).astype(low)
    store(0)
    d_here = dot(natural, weights[:, :D], NT).astype(low)
    branch[...] = d_here
    natural = jnp.concatenate([branch[:, half_at(k)] for k in range(2)], axis=1)
    d_mixed[...] = dot(natural, order[...], NT).astype(low)
    for copy in stores:
        copy.wait()


def middle(core, sizes, logdet_cot, hidden, mixed, gains, order, flow, latent_cot, *parts):
    small = pl.BlockSpec(memory_space=pltpu.SMEM)
    near = pl.BlockSpec(memory_space=pltpu.VMEM)
    far = pl.BlockSpec(memory_space=pl.ANY)
    return pl.pallas_call(
        middle_kernel,
        out_shape=(
            jax.ShapeDtypeStruct((CROPS, CH, PATCHES), wide),
            jax.ShapeDtypeStruct((CROPS, CH, PATCHES), wide),
            jax.ShapeDtypeStruct((8 * CROPS, 128), wide),
            jax.ShapeDtypeStruct((TOKENS, D), wide),
            jax.ShapeDtypeStruct((TOKENS, D), low),
            jax.ShapeDtypeStruct((8, D), wide),
            jax.ShapeDtypeStruct((HALF, B_CUT), low),
            jax.ShapeDtypeStruct((HALF, B_REST), low),
            jax.ShapeDtypeStruct((HALF, B_CUT), low),
            jax.ShapeDtypeStruct((HALF, B_REST), low),
        ),
        in_specs=[small] * 3 + [near] * 6 + [far] * 4,
        out_specs=(near,) * 6 + (far,) * 4,
        scratch_shapes=[pltpu.VMEM((D, B_COLS), low)] * 2
        + [
            pltpu.VMEM((TOKENS, FF), wide),
            pltpu.VMEM((TOKENS, FF), low),
            pltpu.VMEM((TOKENS, D), wide),
            pltpu.VMEM((TOKENS, D), low),
            pltpu.VMEM((TOKENS, D), low),
            pltpu.VMEM((128, TOKENS), wide),
            pltpu.SemaphoreType.DMA((4, 2)),
            pltpu.SemaphoreType.DMA((4, 4)),
        ],
        compiler_params=pltpu.CompilerParams(vmem_limit_bytes=50 * MIB),
        cost_estimate=COST,
        name="middle",
    )(core, sizes, logdet_cot, hidden, mixed, gains, order, flow, latent_cot, *parts)


def back_weights_kernel(dq0, dk0, dv0, dq1, dk1, dv1, normed, keep, send):
    rows = normed[...].T
    crops = (rows[:, :PATCHES], rows[:, PATCHES:])
    for s, (first, second) in enumerate(((dq0, dq1), (dk0, dk1), (dv0, dv1))):
        for start in range(0, D, 256):
            columns = slice(start, start + 256)
            value = (dot(crops[0], first[:, columns]) + dot(crops[1], second[:, columns])).astype(low)
            columns = slice(s * D + start, s * D + start + 256)
            keep[:, columns] = value[:HALF]
            send[:, columns] = value[HALF:]


def back_weights(d_parts, normed):
    near = pl.BlockSpec(memory_space=pltpu.VMEM)
    return pl.pallas_call(
        back_weights_kernel,
        out_shape=(jax.ShapeDtypeStruct((HALF, QKV), low),) * 2,
        in_specs=[near] * 7,
        out_specs=(near,) * 2,
        compiler_params=pltpu.CompilerParams(vmem_limit_bytes=16 * MIB),
        cost_estimate=COST,
        name="back_weights",
    )(*d_parts, normed)


REST_COLS = 128 + ITEMS


def back_kernel(
    first_crop, dq0, dk0, dv0, dq1, dk1, dv1, hidden, d_hidden, gains, vectors, entered, d_flow,
    p_own, p_far, q_own, q_far, keep, send, d_image, sums, weights, sem,
):
    copies = []
    for k, (source, row, start, width) in enumerate(
        ((p_own, 0, 0, P_COLS), (p_far, HALF, 0, P_COLS), (q_own, 0, P_COLS, Q_TABLE), (q_far, HALF, P_COLS, Q_TABLE))
    ):
        target = weights.at[pl.ds(row, HALF), pl.ds(start, width)]
        copies.append(pltpu.make_async_copy(source.at[:, pl.ds(0, width)], target, sem.at[k]))
        copies[k].start()
    for copy in copies:
        copy.wait()
    edges, to_gain = [], jnp.zeros((1, D), wide)
    for i, parts in enumerate(((dq0, dk0, dv0), (dq1, dk1, dv1))):
        rows = slice(i * PATCHES, (i + 1) * PATCHES)
        upstream = jnp.zeros((PATCHES, D), wide)
        for s, part in enumerate(parts):
            upstream = upstream + dot(part[...], weights[:, s * D : (s + 1) * D], NT)
        value, scale = norm_parts(hidden[rows, :])
        to_input, gain_part = norm_pull(value, scale, gains[1:2, :], upstream)
        to_gain = to_gain + gain_part
        edges.append((d_hidden[rows, :] + to_input).astype(low).T)
    edge_rows = jnp.concatenate(edges, axis=1)
    sums[...] = jnp.zeros((128, D), wide)
    sums[CH : CH + 8, :] = jnp.where(iota((8, D), 0) == 1, to_gain, vectors[...])
    owner = iota((TOKENS, ITEMS), 1) == first_crop[0] + (iota((TOKENS, ITEMS), 0) >> 8)
    value = (dot(edge_rows, entered[...]) + sums[...].T).astype(low)
    keep[:, :128] = value[:HALF]
    send[:, :128] = value[HALF:]
    value = dot(edge_rows, owner.astype(low)).astype(low)
    keep[:, 128:] = value[:HALF]
    send[:, 128:] = value[HALF:]
    d_shifted = dot(weights[:, QKV:].T, edge_rows)
    lane = iota((CH, PATCHES), 1)
    for i in range(CROPS):
        moved = pltpu.roll(d_shifted[:CH, i * PATCHES : (i + 1) * PATCHES], PATCHES - 1, 1)
        d_image[i] = d_flow[i] + jnp.where(lane == PATCHES - 1, 0.0, moved)


def back(first_crop, d_parts, hidden, d_hidden, gains, vectors, entered, p_own, p_far, q_own, q_far, d_flow):
    near = pl.BlockSpec(memory_space=pltpu.VMEM)
    return pl.pallas_call(
        back_kernel,
        out_shape=(
            jax.ShapeDtypeStruct((HALF, REST_COLS), low),
            jax.ShapeDtypeStruct((HALF, REST_COLS), low),
            jax.ShapeDtypeStruct((CROPS, CH, PATCHES), wide),
        ),
        in_specs=[pl.BlockSpec(memory_space=pltpu.SMEM)] + [near] * 12 + [pl.BlockSpec(memory_space=pl.ANY)] * 4,
        out_specs=(near,) * 3,
        scratch_shapes=[
            pltpu.VMEM((128, D), wide),
            pltpu.VMEM((D, QKV + 128), low),
            pltpu.SemaphoreType.DMA((4,)),
        ],
        compiler_params=pltpu.CompilerParams(vmem_limit_bytes=VMEM_BYTES),
        cost_estimate=COST,
        name="back",
    )(first_crop, *d_parts, hidden, d_hidden, gains, vectors, entered, d_flow, p_own, p_far, q_own, q_far)


WIDTHS = (QKV, D, FF, FF)
PACK_STARTS = (0, A_COLS + M_ATTN, A_COLS, A_COLS + FF)


def pack_kernel(labels, qkv, attn, up, down, entry, vectors, table, out, order, packed, wide_rows):
    wide_rows[...] = jnp.zeros(wide_rows.shape, wide)
    for source, start, width in zip((qkv, attn, up, down), PACK_STARTS, WIDTHS):
        for row in range(ROWS):
            wide_rows[row : row + 1, start : start + width] = source[row]
    start = A_COLS + M_ATTN
    attn_rows = dot(wide_rows[:, start : start + D].astype(low), order[...])
    wide_rows[:, start : start + D] = attn_rows
    wide_rows[:ROWS, A_IN:A_VEC] = entry[...]
    lane = iota((8, 128), 1)
    marks = jnp.zeros((8, 128), wide)
    for i in range(2 * CROPS):
        first = (labels[i] >> 5).astype(wide)
        second = (labels[i] & 31).astype(wide)
        marks = jnp.where(lane == CH + NVEC + i, first, marks)
        marks = jnp.where(lane == CH + NVEC + 2 * CROPS + i, second, marks)
    wide_rows[:, A_IN:A_TABLE] = wide_rows[:, A_IN:A_TABLE] + marks
    same = iota((ROWS, ROWS), 0) == iota((ROWS, ROWS), 1)
    lane = iota((ROWS, 128), 1)
    for k in range(NVEC):
        across = jnp.broadcast_to(vectors[k : k + 1, :], (ROWS, ROWS))
        down_rows = jnp.sum(jnp.where(same, across, 0.0), axis=1, keepdims=True)
        wide_rows[:ROWS, A_IN:A_TABLE] = jnp.where(lane == CH + k, down_rows, wide_rows[:ROWS, A_IN:A_TABLE])
    wide_rows[:ROWS, A_TABLE : A_TABLE + CLASSES] = table[...]
    wide_rows[:ROWS, A_OUT : A_OUT + 2 * CH] = out[...]
    packed[...] = wide_rows[:ROWS, :].astype(low)


def pack(labels, qkv, attn, up, down, entry, vectors, table, out, order):
    near = pl.BlockSpec(memory_space=pltpu.VMEM)
    return pl.pallas_call(
        pack_kernel,
        out_shape=jax.ShapeDtypeStruct((ROWS, A_COLS + M_COLS), low),
        in_specs=[pl.BlockSpec(memory_space=pltpu.SMEM)] + [near] * 9,
        out_specs=near,
        scratch_shapes=[pltpu.VMEM((8, A_COLS + M_COLS), wide)],
        compiler_params=pltpu.CompilerParams(vmem_limit_bytes=VMEM_BYTES),
        cost_estimate=COST,
        name="pack",
    )(labels, qkv, attn, up, down, entry, vectors, table, out, order)


R_ENTRY = 4736
R_ITEM = R_ENTRY + 128
R_RIGHT = R_ITEM + ITEMS
R_OUT = 8832
R_COLS = 9728
R_PIECES = (
    (1, 0, 0, 768),
    (2, 0, 768, 1024),
    (0, 0, 1792, 768),
    (2, 1024, 2560, 1792),
    (0, 768, 4352, 384),
    (2, 2816, 5120, 256),
    (3, 0, 5376, 1536),
    (0, 1152, 6912, 384),
    (3, 1536, 7296, 1536),
    (0, 1536, 8960, 768),
)


def finish_kernel(
    own, one, two, three, places, order, qkv, attn, up, down, entry, table, out, vectors, square, rows
):
    rows[...] = jnp.zeros(rows.shape, wide)
    total = own[...].astype(wide) + one[...].astype(wide) + two[...].astype(wide) + three[...].astype(wide)
    rows[:ROWS, :] = total
    rest = rows[:, :D]
    swapped = jnp.zeros((8, D), wide)
    for _ in range(3):
        part = rest.astype(low)
        swapped = swapped + dot(part, order[...], NT)
        rest = rest - part.astype(wide)
    rows[:, :D] = swapped
    targets = (qkv, attn, up, down)
    for index, first, start, width in R_PIECES:
        for row in range(ROWS):
            targets[index][row, :, first : first + width] = rows[row : row + 1, start : start + width]
    same = iota((ROWS, ROWS), 0) == iota((ROWS, ROWS), 1)
    for k in range(NVEC):
        at = R_ENTRY + CH + k
        down_rows = jnp.broadcast_to(rows[:ROWS, at : at + 1], (ROWS, ROWS))
        vectors[k : k + 1, :] = jnp.sum(jnp.where(same, down_rows, 0.0), axis=0, keepdims=True)
    entry[...] = rows[:ROWS, R_ENTRY : R_ENTRY + CH]
    out[...] = rows[:ROWS, R_OUT : R_OUT + 2 * CH]
    by_class = dot(rows[:, R_ITEM:R_RIGHT].astype(low), places[...])
    table[...] = by_class[:ROWS, :]
    total = jnp.sum(jnp.square(by_class), axis=1, keepdims=True)
    for columns in (slice(0, R_ITEM), slice(R_RIGHT, R_COLS)):
        total = total + jnp.sum(jnp.square(rows[:, columns]), axis=1, keepdims=True)
    square[...] = jnp.broadcast_to(jnp.sum(total, axis=0, keepdims=True), (8, 128))


def finish(own, one, two, three, places, order):
    near = pl.BlockSpec(memory_space=pltpu.VMEM)
    flats = tuple(jax.ShapeDtypeStruct((ROWS, 1, width), wide) for width in WIDTHS)
    return pl.pallas_call(
        finish_kernel,
        out_shape=flats
        + (
            jax.ShapeDtypeStruct((ROWS, CH), wide),
            jax.ShapeDtypeStruct((ROWS, CLASSES), wide),
            jax.ShapeDtypeStruct((ROWS, 2 * CH), wide),
            jax.ShapeDtypeStruct((NVEC, ROWS), wide),
            jax.ShapeDtypeStruct((8, 128), wide),
        ),
        in_specs=[near] * 6,
        out_specs=(near,) * 9,
        scratch_shapes=[pltpu.VMEM((8, R_COLS), wide)],
        compiler_params=pltpu.CompilerParams(vmem_limit_bytes=16 * MIB),
        cost_estimate=COST,
        name="finish",
    )(own, one, two, three, places, order)


def adam_kernel(*refs):
    squares, gradients, states = refs[:4], refs[4:12], refs[12:36]
    results, norm_out = refs[36:60], refs[60]
    norm = jnp.sqrt(squares[0][...] + squares[1][...] + squares[2][...] + squares[3][...])
    norm_out[...] = norm[0:1, 0:1]
    factor = jnp.minimum(1.0, clip_norm / norm)[0:1, 0:1]
    for index in range(8):
        weight, first, second = (ref[...] for ref in states[3 * index : 3 * index + 3])
        gradient = gradients[index][...]
        clipped = gradient * factor.reshape((1,) * gradient.ndim)
        first_new = beta_one * first + (1.0 - beta_one) * clipped
        second_new = beta_two * second + (1.0 - beta_two) * clipped * clipped
        first_hat = first_new / (1.0 - beta_one**STEP)
        second_hat = second_new / (1.0 - beta_two**STEP)
        weight_new = weight - step_rates[index] * (
            first_hat / (jnp.sqrt(second_hat) + adam_eps) + decay_factors[index] * weight
        )
        for k, value in enumerate((first_new, second_new, weight_new)):
            results[3 * index + k][...] = value


def adam(squares, gradients, states):
    near = pl.BlockSpec(memory_space=pltpu.VMEM)
    shapes = tuple(jax.ShapeDtypeStruct(value.shape, wide) for value in states)
    return pl.pallas_call(
        adam_kernel,
        out_shape=shapes + (jax.ShapeDtypeStruct((1, 1), wide),),
        in_specs=[near] * 36,
        out_specs=(near,) * 25,
        compiler_params=pltpu.CompilerParams(vmem_limit_bytes=24 * MIB),
        cost_estimate=COST,
        name="adam",
    )(*squares, *gradients, *states)


ROUTES = (
    ("x", 1, 0, (0, 1792), (0, 768)),
    ("x", 3, 0, (1792, B_CUT), (768, 1152)),
    ("y", 1, 1, (0, 1792), (0, 384)),
    ("y", 3, 1, (1792, B_REST), (384, 1152)),
)
SIDE_QKV = QKV // 2
WIDTHS_OUT = tuple(b[1] - b[0] + a[1] - a[0] for _, _, _, b, a in ROUTES)


def by_place(value):
    return value.reshape(4, 4, 24, value.shape[1])


def both_cores(refs, columns):
    return refs[0][..., columns[0] : columns[1]].astype(wide) + refs[1][..., columns[0] : columns[1]].astype(wide)


def fold_send_kernel(places, *refs):
    distance = pl.program_id(0) + 1
    for m, (axis, first, side, columns, of_qkv) in enumerate(ROUTES):
        block, block_qkv, sent = refs[4 * side : 4 * side + 2], refs[4 * side + 2 : 4 * side + 4], refs[8 + m]
        width = columns[1] - columns[0]

        @pl.when((distance == first) | (distance == 2))
        def _(block=block, block_qkv=block_qkv, sent=sent, columns=columns, of_qkv=of_qkv, width=width):
            value = both_cores(block, columns)
            sent[..., :width] = value.reshape(sent.shape[:-1] + (width,)).astype(low)
            value = both_cores(block_qkv, of_qkv)
            sent[..., width:] = value.reshape(sent.shape[:-1] + (value.shape[-1],)).astype(low)


def fold_send(places, left, right, qkv):
    views_left, views_right, views_qkv = ([by_place(value) for value in pair] for pair in (left, right, qkv))
    x_index = lambda at: lambda k, places: (places[0] ^ (k + 1), 0, 0, at)
    y_index = lambda at: lambda k, places: (0, places[1] ^ (k + 1), 0, at)
    in_specs = (
        [pl.BlockSpec((1, 4, 24, B_CUT), x_index(0))] * 2
        + [pl.BlockSpec((1, 4, 24, SIDE_QKV), x_index(0))] * 2
        + [pl.BlockSpec((4, 1, 24, B_REST), y_index(0))] * 2
        + [pl.BlockSpec((4, 1, 24, SIDE_QKV), y_index(1))] * 2
    )
    shapes, specs = [], []
    for m, route in enumerate(ROUTES):
        shapes.append(jax.ShapeDtypeStruct((2, 4, 24, WIDTHS_OUT[m]), low))
        slot = (lambda k, places: ((k + 1) // 2, 0, 0, 0)) if route[1] == 1 else (lambda k, places: (k // 2, 0, 0, 0))
        specs.append(pl.BlockSpec((1, 4, 24, WIDTHS_OUT[m]), slot))
    return pl.pallas_call(
        fold_send_kernel,
        grid_spec=pltpu.PrefetchScalarGridSpec(num_scalar_prefetch=1, grid=(3,), in_specs=in_specs, out_specs=specs),
        out_shape=shapes,
        compiler_params=pltpu.CompilerParams(vmem_limit_bytes=20 * MIB),
        cost_estimate=COST,
        name="fold_send",
    )(places, *views_left, *views_qkv, *views_right, *views_qkv)


def route_specs(m, distance):
    axis, _, side, columns, of_qkv = ROUTES[m]
    if axis == "x":
        index = lambda at: lambda g, places: (places[0] ^ distance, g, 0, at)
    else:
        index = lambda at: lambda g, places: (g, places[1] ^ distance, 0, at)
    step = of_qkv[1] - of_qkv[0]
    at = (side * SIDE_QKV + of_qkv[0]) // step
    return [pl.BlockSpec((1, 1, 24, 1792), index(columns[0] // 1792))] * 2 + [pl.BlockSpec((1, 1, 24, step), index(at))] * 2


def own_sum(refs, m):
    columns, of_qkv = ROUTES[m][3:]
    width, step = columns[1] - columns[0], of_qkv[1] - of_qkv[0]
    return both_cores(refs[:2], (0, width))[0], both_cores(refs[2:4], (0, step))[0]


def second_send_kernel(places, *refs):
    for m in range(4):
        came, sent = refs[5 * m + 4], refs[20 + m]
        value, of_qkv = own_sum(refs[5 * m : 5 * m + 4], m)
        width = value.shape[-1]
        sent[:, :, :width] = (value + came[0, :, :, :width].astype(wide)).astype(low)
        sent[:, :, width:] = (of_qkv + came[0, :, :, width:].astype(wide)).astype(low)


def slot_spec(m, here):
    slot = (0 if ROUTES[m][1] == 1 else 1) if here else (1 if ROUTES[m][1] == 1 else 0)
    return pl.BlockSpec((1, 1, 24, WIDTHS_OUT[m]), lambda g, places: (slot, g, 0, 0))


def row_spec(width):
    return pl.BlockSpec((1, 24, width), lambda g, places: (g, 0, 0))


def route_operands(m, left, right, qkv):
    return [by_place(value) for value in ((left, right)[ROUTES[m][2]] + qkv)]


def second_send(places, left, right, qkv, came):
    operands, specs = [], []
    for m in range(4):
        operands += [*route_operands(m, left, right, qkv), came[m]]
        specs += [*route_specs(m, ROUTES[m][1] ^ 2), slot_spec(m, False)]
    return pl.pallas_call(
        second_send_kernel,
        grid_spec=pltpu.PrefetchScalarGridSpec(
            num_scalar_prefetch=1, grid=(4,), in_specs=specs, out_specs=[row_spec(width) for width in WIDTHS_OUT]
        ),
        out_shape=[jax.ShapeDtypeStruct((4, 24, width), low) for width in WIDTHS_OUT],
        compiler_params=pltpu.CompilerParams(vmem_limit_bytes=VMEM_BYTES),
        cost_estimate=COST,
        name="second_send",
    )(places, *operands)


def line_sum_kernel(places, *refs):
    left, right = refs[-2:]
    for m in range(4):
        came, late = refs[6 * m + 4 : 6 * m + 6]
        value, of_qkv = own_sum(refs[6 * m : 6 * m + 4], m)
        target, start = (left, right)[m // 2], (m % 2) * WIDTHS_OUT[m - m % 2]
        width = value.shape[-1]
        value = value + came[0, :, :, :width].astype(wide) + late[:, :, :width].astype(wide)
        target[:, :, start : start + width] = value.astype(low)
        value = of_qkv + came[0, :, :, width:].astype(wide) + late[:, :, width:].astype(wide)
        target[:, :, start + width : start + WIDTHS_OUT[m]] = value.astype(low)
    kept, other, came, late = refs[24:28]
    value = kept[0].astype(wide) + other[0].astype(wide) + came[0].astype(wide) + late[...].astype(wide)
    left[:, :, WIDTHS_OUT[0] + WIDTHS_OUT[1] :] = value.astype(low)


def line_sum(places, left, right, qkv, came, late, rest, came_rest, late_rest):
    operands, specs = [], []
    for m in range(4):
        operands += [*route_operands(m, left, right, qkv), came[m], late[m]]
        specs += [*route_specs(m, 0), slot_spec(m, True), row_spec(WIDTHS_OUT[m])]
    operands += [by_place(value) for value in rest] + [came_rest, late_rest]
    specs += [pl.BlockSpec((1, 1, 24, REST_COLS), lambda g, places: (places[0], g, 0, 0))] * 2
    specs += [pl.BlockSpec((1, 1, 24, REST_COLS), lambda g, places: (0, g, 0, 0)), row_spec(REST_COLS)]
    widths = (R_RIGHT, R_COLS - R_RIGHT)
    return pl.pallas_call(
        line_sum_kernel,
        grid_spec=pltpu.PrefetchScalarGridSpec(
            num_scalar_prefetch=1, grid=(4,), in_specs=specs, out_specs=[row_spec(width) for width in widths]
        ),
        out_shape=[jax.ShapeDtypeStruct((4, 24, width), low) for width in widths],
        compiler_params=pltpu.CompilerParams(vmem_limit_bytes=VMEM_BYTES),
        cost_estimate=COST,
        name="line_sum",
    )(places, *operands)


def per_device(
    images,
    labels,
    crop_sizes,
    latent_cotangent,
    logdet_cotangent,
    weight_in,
    moment_in,
    second_in,
    class_table,
    moment_table,
    second_table,
    weight_qkv,
    moment_qkv,
    second_qkv,
    weight_attn,
    moment_attn,
    second_attn,
    weight_up,
    moment_up,
    second_up,
    weight_down,
    moment_down,
    second_down,
    weight_out,
    moment_out,
    second_out,
    vectors,
    moment_vectors,
    second_vectors,
):
    core = lax.axis_index("c")
    chip = lax.axis_index(("x", "y", "z"))
    half = PATCHES // 2

    order = order_matrix()
    rows_of = lambda value: jnp.transpose(value, (1, 0, 2))
    rows_down = lambda value: jnp.transpose(value, (2, 0, 1))
    packed = pack(
        labels, rows_of(weight_qkv), rows_of(weight_attn), rows_of(weight_up), rows_down(weight_down),
        weight_in.T, vectors, class_table.T, weight_out, order,
    )

    inputs = jnp.stack([images, latent_cotangent])
    mine = lax.dynamic_slice_in_dim(inputs, core * CROPS, CROPS, 1)
    theirs = swap(lax.dynamic_slice_in_dim(inputs, (1 - core) * CROPS, CROPS, 1), "c", 1)
    whole = jnp.where(
        core == 0,
        jnp.concatenate([mine, theirs], axis=-1),
        jnp.concatenate([theirs, mine], axis=-1),
    )
    flow = whole[0][:, :, ::-1]
    latent_cot = whole[1]
    logdet_cot = lax.dynamic_slice_in_dim(logdet_cotangent, core * CROPS, CROPS, 0)
    sizes = lax.dynamic_slice_in_dim(crop_sizes, core * CROPS, CROPS, 0)
    my_labels = lax.dynamic_slice_in_dim(labels, core * CROPS, CROPS, 0)

    rows_a = gather_four(packed, "z", 0).reshape(4 * ROWS, A_COLS + M_COLS)
    b_own = lax.all_gather(rows_a[:, A_COLS:], ("x", "y"), axis=0, tiled=True)
    p_own = gather_four(gather_four(rows_a[:, :P_COLS], "y", 0), "x", 0).reshape(HALF, P_COLS)
    q_own = gather_four(gather_four(rows_a[:, P_COLS:A_COLS], "x", 0), "y", 1).reshape(HALF, Q_COLS)
    p_far = swap(p_own, "c", 1)
    q_far = swap(q_own, "c", 1)

    hidden, normed, qkv, gains, entered = front(my_labels, flow, p_own, p_far, q_own, q_far)
    b_own, qkv = together((b_own, qkv))
    b_far = swap(b_own, "c", 1)
    mixed = attend(sizes, qkv)
    label_parts = q_own[::ROWS, Q_X + CH + NVEC : Q_X + CH + NVEC + 8].astype(wide).astype(jnp.int32)
    all_labels = (label_parts[:, :4] * 32 + label_parts[:, 4:]).reshape(ITEMS)
    class_places = (all_labels[:, None] == jnp.arange(CLASSES, dtype=jnp.int32)[None, :]).astype(low)
    mixed, class_places = together((mixed, class_places))
    masked_latent, d_flow, logdet_rows, d_hidden, d_mixed, vector_rows, keep_p, keep_q, send_p, send_q = middle(
        core[None], sizes, logdet_cot, hidden, mixed, gains, order, flow, latent_cot, q_own, q_far, b_own, b_far
    )
    came_p, came_q = swap(send_p, "c", 1), swap(send_q, "c", 1)
    d_parts = (*attend_back(0, sizes, qkv, d_mixed), *attend_back(1, sizes, qkv, d_mixed))
    keep_a, send_a = back_weights(d_parts, normed)
    came_a = swap(send_a, "c", 1)
    places = jnp.stack([lax.axis_index("x"), lax.axis_index("y")])
    sums = ((keep_p, came_p), (keep_q, came_q), (keep_a, came_a))
    sent = fold_send(places, *sums)
    sent, hidden_late = together((sent, hidden))
    came = [swap(value, route[0], route[1]) for value, route in zip(sent, ROUTES)]
    first_crop = (chip * 4 + core * CROPS)[None]
    keep_r, send_r, d_image = back(
        first_crop, d_parts, hidden_late, d_hidden, gains, vector_rows, entered,
        p_own, p_far, q_own, q_far, d_flow,
    )
    came_r = swap(send_r, "c", 1)
    place_x = lax.axis_index("x")

    def rest_block(distance):
        blocks = [lax.dynamic_index_in_dim(by_place(value), place_x ^ distance, 0, keepdims=False) for value in (keep_r, came_r)]
        return blocks[0].astype(wide) + blocks[1].astype(wide)

    came_rest = swap(jnp.stack([rest_block(1).astype(low), rest_block(2).astype(low)]), "x", 1)
    came, came_rest = together((came, came_rest))
    sent = second_send(places, *sums, came)
    sent_rest = (rest_block(3) + came_rest[1].astype(wide)).astype(low)
    sent, sent_rest = together((sent, sent_rest))
    late = [swap(value, route[0], route[1] ^ 2) for value, route in zip(sent, ROUTES)]
    late_rest = swap(sent_rest, "x", 3)
    left, right = line_sum(places, *sums, came, late, (keep_r, came_r), came_rest, late_rest)
    pick = lambda value: lambda place: lax.dynamic_index_in_dim(value, place, 0, keepdims=False)
    left = scatter_four(pick(left), "y").astype(low)
    right = scatter_four(pick(right), "x").astype(low)
    last = jnp.concatenate([left, right], axis=1).reshape(4, ROWS, R_COLS)
    level = lax.axis_index("z")
    parts = [lax.dynamic_index_in_dim(last, level ^ k, 0, keepdims=False) for k in range(4)]
    parts = [parts[0]] + [swap(parts[k], "z", k) for k in (1, 2, 3)]

    image_back = d_image[:, :, ::-1]
    logdet_own = logdet_rows[::8, 0]

    def to_places(value):
        kept = lax.dynamic_slice_in_dim(value, core * half, half, 2)
        came = swap(lax.dynamic_slice_in_dim(value, (1 - core) * half, half, 2), "c", 1)
        return jnp.where(
            core == 0, jnp.concatenate([kept, came], axis=0), jnp.concatenate([came, kept], axis=0)
        )

    latents = to_places(masked_latent)
    image_grad = to_places(image_back)
    came_logdet = swap(logdet_rows, "c", 1)[::8, 0]
    logdet = jnp.where(
        core == 0,
        jnp.concatenate([logdet_own, came_logdet]),
        jnp.concatenate([came_logdet, logdet_own]),
    )

    *grads, grad_entry, grad_table, grad_out, grad_vectors, square = finish(*parts, class_places, order)
    square = square + swap(square, "c", 1)
    for axis in ("z", "y"):
        square = square + swap(square, axis, 1) + swap(square, axis, 2) + swap(square, axis, 3)
    squares = [square] + [swap(square, "x", k) for k in (1, 2, 3)]

    rows_back = lambda value: jnp.transpose(value, (1, 0, 2))
    turned = lambda value: value.T
    same = lambda value: value
    views = (
        (turned, turned, grad_entry),
        (turned, turned, grad_table),
        (rows_of, rows_back, grads[0]),
        (rows_of, rows_back, grads[1]),
        (rows_of, rows_back, grads[2]),
        (rows_down, lambda value: jnp.transpose(value, (1, 2, 0)), grads[3]),
        (same, same, grad_out),
        (same, same, grad_vectors),
    )
    states = (
        (weight_in, moment_in, second_in),
        (class_table, moment_table, second_table),
        (weight_qkv, moment_qkv, second_qkv),
        (weight_attn, moment_attn, second_attn),
        (weight_up, moment_up, second_up),
        (weight_down, moment_down, second_down),
        (weight_out, moment_out, second_out),
        (vectors, moment_vectors, second_vectors),
    )
    entered_states = [view[0](value) for view, group in zip(views, states) for value in group]
    *results, norm = adam(squares, [view[2] for view in views], entered_states)
    updated = [views[k // 3][1](value) for k, value in enumerate(results)]
    return (latents, logdet, image_grad, norm.reshape(()), *updated)


def solution(mesh):
    chips = Mesh(mesh.devices.reshape(4, 4, 4, 2), ("x", "y", "z", "c"))
    dp, every = ("x", "y", "z"), ("x", "y", "z", "c")
    patches = P(dp, None, "c")
    columns, rows, last = P(None, every), P(None, every, None), P(None, None, every)
    parameters = (columns,) * 6 + (rows,) * 9 + (last,) * 3 + (P(every, None),) * 3 + (columns,) * 3
    return jax.shard_map(
        per_device,
        mesh=chips,
        in_specs=(patches, P(dp), P(dp, None), patches, P(dp)) + parameters,
        out_specs=(patches, P(dp), patches, P()) + parameters,
        check_vma=False,
    )
```

```python
import functools

import jax
import jax.numpy as jnp
import numpy as np
from jax import lax
from jax.experimental import pallas as pl
from jax.experimental.pallas import tpu as pltpu
from jax.sharding import Mesh, PartitionSpec as P

D = 768
HEADS = 12
HEAD = 64
CH = 48
CLASSES = 1000
SIDE = 16
STEP = 5
PATCHES = 256
ITEMS = 256
FF = 3072
NVEC = 6
ROWS = 6
CROPS = 2

beta_one = 0.9
beta_two = 0.95
adam_eps = 1e-08
step_rates = (0.02, 0.3, 0.02, 0.1, 0.02, 0.02, 0.02, 0.2)
decay_factors = (0.1, 0.1, 0.1, 0.1, 0.1, 0.1, 0.1, 0.0)
clip_norm = 1.0
norm_eps = 1e-06

QKV = 3 * D
A_IN = QKV
A_VEC = A_IN + CH
A_LAB = A_VEC + NVEC
A_TABLE = QKV + 128
A_OUT = A_TABLE + 1024
A_COLS = A_OUT + 128
M_ATTN = 2 * FF
M_COLS = M_ATTN + D
B_UP = D
B_DOWN = B_UP + FF
B_OUT = B_DOWN + FF
B_END = B_OUT + 2 * CH
B_COLS = B_OUT + 128
G_VEC = QKV + CH
G_ITEM = QKV + 128
G_COLS = G_ITEM + ITEMS
G_CUT = 1408
B_CUT = 3584
B_REST = B_COLS - B_CUT

low = jnp.bfloat16
wide = jnp.float32


together = lax.optimization_barrier


def swap(value, axis, distance):
    size = lax.axis_size(axis)
    return lax.ppermute(value, axis, [(i, i ^ distance) for i in range(size)])


def gather_four(value, axis, dim):
    place = lax.axis_index(axis)
    parts = [value] + [swap(value, axis, k) for k in (1, 2, 3)]
    shape = value.shape[:dim] + (4,) + value.shape[dim:]
    result = jnp.zeros(shape, value.dtype)
    for k, part in enumerate(parts):
        result = lax.dynamic_update_index_in_dim(result, part, place ^ k, dim)
    return result


def scatter_four(piece, axis):
    place = lax.axis_index(axis)
    total = piece(place).astype(wide)
    for k in (1, 2, 3):
        total = total + swap(piece(place ^ k).astype(low), axis, k).astype(wide)
    return total


def order_matrix():
    natural = np.arange(D)
    place = (natural // ROWS) % 2 * (D // 2) + natural // (2 * ROWS) * ROWS + natural % ROWS
    return (place[:, None] == natural[None, :]).astype(low)


NN = (((1,), (0,)), ((), ()))
NT = (((1,), (1,)), ((), ()))
HALF = D // 2
TOKENS = CROPS * PATCHES
P_COLS = A_COLS // 2
Q_COLS = A_COLS // 2
Q_X = QKV - P_COLS
Q_TABLE = Q_X + 128
Q_OUT = Q_TABLE + 1024
MASKED = -1e30
SCALE = HEAD ** (-0.5)
MIB = 1024 * 1024
VMEM_BYTES = 58 * MIB
COST = pl.CostEstimate(flops=1000, bytes_accessed=1000, transcendentals=0)


def dot(left_side, right_side, how=NN):
    return lax.dot_general(left_side, right_side, how, preferred_element_type=wide)


def iota(shape, axis):
    return lax.broadcasted_iota(jnp.int32, shape, axis)


def crop_valid(place, height, width):
    natural = PATCHES - 1 - place
    return ((natural >> 4) < height) & ((natural & 15) < width)


def norm_parts(value):
    mean = jnp.mean(value, axis=-1, keepdims=True)
    centered = value - mean
    scale = lax.rsqrt(jnp.mean(centered * centered, axis=-1, keepdims=True) + norm_eps)
    return centered * scale, scale


def norm_pull(normed, scale, gain, upstream):
    inner = upstream * gain
    to_input = scale * (
        inner
        - jnp.mean(inner, axis=-1, keepdims=True)
        - normed * jnp.mean(inner * normed, axis=-1, keepdims=True)
    )
    return to_input, jnp.sum(upstream * normed, axis=0, keepdims=True)


GELU_ROOT = 0.7978845608028654
GELU_CUBE = 0.044715


def gelu_tanh(value):
    return jnp.tanh(GELU_ROOT * (value + GELU_CUBE * (value * value * value)))


def front_kernel(
    labels, flow, p_own, p_far, q_own, q_far, hidden, normed, qkv, gains, entered, weights, sem
):
    copies = []
    for k, (source, row, start, width) in enumerate(
        ((q_own, 0, P_COLS, Q_OUT), (q_far, HALF, P_COLS, Q_OUT), (p_own, 0, 0, P_COLS), (p_far, HALF, 0, P_COLS))
    ):
        copies.append(
            pltpu.make_async_copy(
                source.at[:, pl.ds(0, width)], weights.at[pl.ds(row, HALF), pl.ds(start, width)], sem.at[k]
            )
        )
        copies[k].start()
    lane = iota((CH, PATCHES), 1)
    for i in range(CROPS):
        moved = jnp.where(lane == 0, 0.0, pltpu.roll(flow[i], 1, 1))
        below = jnp.where(iota((128 - CH, PATCHES), 0) == 0, 1.0, 0.0)
        both = jnp.concatenate([moved, below], axis=0)
        entered[i * PATCHES : (i + 1) * PATCHES, :] = both.T.astype(low)
    pick = (iota((8, 128), 1) == iota((8, 128), 0) + CH).astype(low)
    chosen = iota((8, 1024), 1) == jnp.where(iota((8, 1024), 0) == 0, labels[0], labels[1])
    chosen = chosen.astype(low)
    copies[0].wait()
    copies[1].wait()
    block = weights[:, QKV:A_TABLE]
    gains[...] = dot(pick, block, NT)
    class_rows = dot(chosen, weights[:, A_TABLE:], NT)
    for i in range(CROPS):
        rows = slice(i * PATCHES, (i + 1) * PATCHES)
        value = dot(entered[rows, :], block, NT) + class_rows[i : i + 1, :]
        hidden[rows, :] = value
        value, _ = norm_parts(value)
        normed[rows, :] = (value * gains[1:2, :]).astype(low)
    copies[2].wait()
    copies[3].wait()
    for start in range(0, QKV, 256):
        qkv[:, start : start + 256] = dot(normed[...], weights[:, start : start + 256]).astype(low)


def front(labels, flow, p_own, p_far, q_own, q_far):
    near, far = pl.BlockSpec(memory_space=pltpu.VMEM), pl.BlockSpec(memory_space=pl.ANY)
    return pl.pallas_call(
        front_kernel,
        out_shape=(
            jax.ShapeDtypeStruct((TOKENS, D), wide),
            jax.ShapeDtypeStruct((TOKENS, D), low),
            jax.ShapeDtypeStruct((TOKENS, QKV), low),
            jax.ShapeDtypeStruct((8, D), wide),
            jax.ShapeDtypeStruct((TOKENS, 128), low),
        ),
        in_specs=[pl.BlockSpec(memory_space=pltpu.SMEM), near] + [far] * 4,
        out_specs=(near,) * 5,
        scratch_shapes=[pltpu.VMEM((D, A_OUT), low), pltpu.SemaphoreType.DMA((4,))],
        compiler_params=pltpu.CompilerParams(vmem_limit_bytes=VMEM_BYTES),
        cost_estimate=COST,
        name="front",
    )(labels, flow, p_own, p_far, q_own, q_far)


HEAD_PAIRS = HEADS // 2
STEP_PAIRS = 3


def pair_blocks(pair):
    return slice(pair * 128, (pair + 1) * 128)


def head_masks():
    first = iota((PATCHES, 128), 1) < HEAD
    return first, jnp.logical_not(first)


def attend_kernel(sizes, queries, keys, values, mixed):
    crop = pl.program_id(0)
    shape = (PATCHES, PATCHES)
    place, key_place = iota(shape, 0), iota(shape, 1)
    valid = crop_valid(key_place, sizes[crop, 0], sizes[crop, 1])
    allowed = (key_place == place) | ((key_place < place) & valid)
    masks = head_masks()
    heads = [(pair, mine) for pair in range(STEP_PAIRS) for mine in masks]
    exponents, inverses = [], []
    for pair, mine in heads:
        block = pair_blocks(pair)
        scores = dot(queries[:, block] * low(SCALE), jnp.where(mine, keys[:, block], 0), NT)
        scores = jnp.where(allowed, scores, MASKED)
        exponent = jnp.exp(scores - jnp.max(scores, axis=-1, keepdims=True))
        exponents.append(exponent)
        inverses.append(1.0 / jnp.sum(exponent, axis=-1, keepdims=True))
    for pair in range(STEP_PAIRS):
        block = pair_blocks(pair)
        total = jnp.zeros((PATCHES, 128), wide)
        for k, mine in enumerate(masks):
            soft = (exponents[2 * pair + k] * inverses[2 * pair + k]).astype(low)
            total = total + dot(soft, jnp.where(mine, values[:, block], 0))
        mixed[:, block] = total.astype(low)


def attend(sizes, qkv):
    steps = HEAD_PAIRS // STEP_PAIRS
    shape = (PATCHES, STEP_PAIRS * 128)
    return pl.pallas_call(
        attend_kernel,
        grid=(CROPS, steps),
        out_shape=jax.ShapeDtypeStruct((TOKENS, D), low),
        in_specs=[pl.BlockSpec(memory_space=pltpu.SMEM)]
        + [pl.BlockSpec(shape, lambda i, h, s=s: (i, s * steps + h)) for s in range(3)],
        out_specs=pl.BlockSpec(shape, lambda i, h: (i, h)),
        compiler_params=pltpu.CompilerParams(vmem_limit_bytes=16 * MIB),
        cost_estimate=COST,
        name="attend",
    )(sizes, qkv, qkv, qkv)


def attend_back_kernel(crop, sizes, queries, keys, values, d_mixed, d_queries, d_keys, d_values):
    shape = (PATCHES, PATCHES)
    key_place, place = iota(shape, 0), iota(shape, 1)
    valid = crop_valid(key_place, sizes[crop, 0], sizes[crop, 1])
    allowed = (key_place == place) | ((key_place < place) & valid)
    masks = head_masks()
    heads = [(pair, mine) for pair in range(STEP_PAIRS) for mine in masks]
    softs = []
    for pair, mine in heads:
        block = pair_blocks(pair)
        scores = dot(jnp.where(mine, keys[:, block], 0), queries[:, block] * low(SCALE), NT)
        scores = jnp.where(allowed, scores, MASKED)
        exponent = jnp.exp(scores - jnp.max(scores, axis=0, keepdims=True))
        softs.append(exponent * (1.0 / jnp.sum(exponent, axis=0, keepdims=True)))
    slopes = []
    for soft, (pair, mine) in zip(softs, heads):
        block = pair_blocks(pair)
        d_soft = dot(jnp.where(mine, values[:, block], 0), d_mixed[:, block], NT)
        d_scores = soft * (d_soft - jnp.sum(d_soft * soft, axis=0, keepdims=True))
        slopes.append(d_scores.astype(low))
    for pair in range(STEP_PAIRS):
        block = pair_blocks(pair)
        to_queries = jnp.zeros((PATCHES, 128), wide)
        to_keys = jnp.zeros((PATCHES, 128), wide)
        to_values = jnp.zeros((PATCHES, 128), wide)
        for k, mine in enumerate(masks):
            soft, slope = softs[2 * pair + k], slopes[2 * pair + k]
            to_values = to_values + dot(soft.astype(low), jnp.where(mine, d_mixed[:, block], 0))
            to_keys = to_keys + dot(slope, jnp.where(mine, queries[:, block] * low(SCALE), 0))
            to_queries = to_queries + dot(slope.T, jnp.where(mine, keys[:, block], 0))
        d_queries[:, block] = (to_queries * SCALE).astype(low)
        d_keys[:, block] = to_keys.astype(low)
        d_values[:, block] = to_values.astype(low)


def attend_back(crop, sizes, qkv, d_mixed):
    steps = HEAD_PAIRS // STEP_PAIRS
    shape = (PATCHES, STEP_PAIRS * 128)
    block = pl.BlockSpec(shape, lambda h: (0, h))
    return pl.pallas_call(
        functools.partial(attend_back_kernel, crop),
        grid=(steps,),
        out_shape=(jax.ShapeDtypeStruct((PATCHES, D), low),) * 3,
        in_specs=[pl.BlockSpec(memory_space=pltpu.SMEM)]
        + [pl.BlockSpec(shape, lambda h, s=s: (crop, s * steps + h)) for s in range(3)]
        + [pl.BlockSpec(shape, lambda h: (crop, h))],
        out_specs=(block,) * 3,
        compiler_params=pltpu.CompilerParams(vmem_limit_bytes=16 * MIB),
        cost_estimate=COST,
        name="attend_back",
    )(sizes, qkv, qkv, qkv, d_mixed)


SECTIONS = ((0, D), (B_UP, FF), (B_DOWN, FF), (B_OUT, 128))
STEP_COLS = 512


def middle_kernel(
    core_ref, sizes, logdet_cot, hidden_in, mixed, gains, order, flow, latent_cot, q_own, q_far, b_own, b_far,
    latents, d_flow, logdet, d_hidden, d_mixed, vectors_out, keep_p, keep_q, send_p, send_q,
    weights, grads, up_proj, active, hidden, normed_two, branch, d_head, sem_in, sem_out,
):
    core = core_ref[0]
    keep, send = (keep_p, keep_q), (send_p, send_q)
    loads = []
    for k, (start, width) in enumerate(SECTIONS):
        pair = []
        for j, (first, second) in enumerate(((q_own, b_own), (q_far, b_far))):
            source, at = ((second, M_ATTN), (second, 0), (second, FF), (first, Q_OUT))[k]
            target = weights.at[pl.ds(j * HALF, HALF), pl.ds(start, width)]
            copy = pltpu.make_async_copy(source.at[:, pl.ds(at, width)], target, sem_in.at[k, j])
            copy.start()
            pair.append(copy)
        loads.append(pair)
    stores = []

    def store(section):
        start, width = SECTIONS[section]
        for part, (low_end, high_end) in enumerate(((0, B_CUT), (B_CUT, B_COLS))):
            first, last = max(start, low_end), min(start + width, high_end)
            if first >= last:
                continue
            for j, target in enumerate((keep[part], send[part])):
                copy = pltpu.make_async_copy(
                    grads.at[pl.ds(j * HALF, HALF), pl.ds(first, last - first)],
                    target.at[:, pl.ds(first - low_end, last - first)],
                    sem_out.at[section, 2 * part + j],
                )
                copy.start()
                stores.append(copy)

    def arrived(section):
        for copy in loads[section]:
            copy.wait()

    def half_at(k):
        return pl.ds(pl.multiple_of((k ^ core) * HALF, 128), HALF)

    gain = lambda row: gains[row : row + 1, :]
    halves = (slice(0, HALF), slice(HALF, D))

    mixed_here = jnp.concatenate([dot(mixed[...], order[:, half_at(k)]) for k in range(2)], axis=1).astype(low)
    mixed_rows = mixed_here.T
    arrived(0)
    for k, columns in enumerate(halves):
        value = dot(mixed_here, weights[:, half_at(k)])
        hidden[:, columns] = hidden_in[:, columns] + value + gains[2:3, columns]

    value, _ = norm_parts(hidden[...])
    normed_two[...] = (value * gain(3)).astype(low)
    arrived(1)
    for step in range(0, FF, STEP_COLS):
        columns = slice(B_UP + step, B_UP + step + STEP_COLS)
        value = dot(normed_two[...], weights[:, columns])
        up_proj[:, step : step + STEP_COLS] = value
        active[:, step : step + STEP_COLS] = (0.5 * value * (1.0 + gelu_tanh(value))).astype(low)
    arrived(2)
    d_hidden[...] = hidden[...] + dot(active[...], weights[:, B_DOWN:B_OUT], NT) + gain(4)

    last, last_scale = norm_parts(d_hidden[...])
    final_rows = (last * gain(5)).astype(low).T
    arrived(3)
    head_rows = weights[:, B_OUT:].T
    output = dot(head_rows, final_rows)
    place = iota((CH, PATCHES), 1)
    for i in range(CROPS):
        columns = slice(i * PATCHES, (i + 1) * PATCHES)
        valid = crop_valid(place, sizes[i, 0], sizes[i, 1]).astype(wide)
        log_scale = output[CH : 2 * CH, columns]
        inverse = jnp.exp(-log_scale)
        latent = (flow[i] - output[:CH, columns]) * inverse
        latents[i] = latent * valid
        terms = jnp.sum(jnp.sum(log_scale * valid, axis=1, keepdims=True), axis=0, keepdims=True)
        logdet[8 * i : 8 * i + 8, :] = jnp.broadcast_to(-terms, (8, 128))
        d_latent = latent_cot[i] * valid
        to_flow = d_latent * inverse
        d_flow[i] = to_flow
        d_head[:CH, columns] = -to_flow
        d_head[CH : 2 * CH, columns] = -d_latent * latent - valid * logdet_cot[i]
        d_head[2 * CH :, columns] = jnp.zeros((128 - 2 * CH, PATCHES), wide)
    d_output = d_head[...].astype(low)
    d_output_rows = d_head[...].T.astype(low)
    grads[:, B_OUT:] = dot(final_rows, d_output, NT).astype(low)
    store(3)
    upstream = dot(d_output_rows, head_rows)
    to_input, to_gain = norm_pull(last, last_scale, gain(5), upstream)
    vectors_out[5:6, :] = to_gain
    d_hidden[...] = to_input

    edge = d_hidden[...].astype(low)
    vectors_out[4:5, :] = jnp.sum(edge.astype(wide), axis=0, keepdims=True)
    edge_rows = edge.T
    normed_rows = normed_two[...].T
    for step in range(0, FF, STEP_COLS):
        columns = slice(B_DOWN + step, B_DOWN + step + STEP_COLS)
        up_columns = slice(B_UP + step, B_UP + step + STEP_COLS)
        chunk = slice(step, step + STEP_COLS)
        d_active = dot(edge, weights[:, columns])
        grads[:, columns] = dot(edge_rows, active[:, chunk]).astype(low)
        value = up_proj[:, chunk]
        tanh = gelu_tanh(value)
        slope = 0.5 * (1.0 + tanh) + 0.5 * value * (1.0 - tanh * tanh) * GELU_ROOT * (
            1.0 + 3.0 * GELU_CUBE * value * value
        )
        d_up = (d_active * slope).astype(low)
        active[:, chunk] = d_up
        grads[:, up_columns] = dot(normed_rows, d_up).astype(low)
    store(2)
    store(1)
    upstream = dot(active[...], weights[:, B_UP:B_DOWN], NT)
    value, scale = norm_parts(hidden[...])
    to_input, to_gain = norm_pull(value, scale, gain(3), upstream)
    vectors_out[3:4, :] = to_gain
    d_hidden[...] = d_hidden[...] + to_input

    edge = d_hidden[...].astype(low)
    vectors_out[2:3, :] = jnp.sum(edge.astype(wide), axis=0, keepdims=True)
    vectors_out[0:2, :] = jnp.zeros((2, D), wide)
    vectors_out[6:8, :] = jnp.zeros((2, D), wide)
    branch[...] = edge
    parts = [branch[:, half_at(k)] for k in range(2)]
    natural = jnp.concatenate(parts, axis=1)
    grads[:, :D] = dot(mixed_rows, natural).astype(low)
    store(0)
    d_here = dot(natural, weights[:, :D], NT).astype(low)
    branch[...] = d_here
    natural = jnp.concatenate([branch[:, half_at(k)] for k in range(2)], axis=1)
    d_mixed[...] = dot(natural, order[...], NT).astype(low)
    for copy in stores:
        copy.wait()


def middle(core, sizes, logdet_cot, hidden, mixed, gains, order, flow, latent_cot, *parts):
    small = pl.BlockSpec(memory_space=pltpu.SMEM)
    near = pl.BlockSpec(memory_space=pltpu.VMEM)
    far = pl.BlockSpec(memory_space=pl.ANY)
    return pl.pallas_call(
        middle_kernel,
        out_shape=(
            jax.ShapeDtypeStruct((CROPS, CH, PATCHES), wide),
            jax.ShapeDtypeStruct((CROPS, CH, PATCHES), wide),
            jax.ShapeDtypeStruct((8 * CROPS, 128), wide),
            jax.ShapeDtypeStruct((TOKENS, D), wide),
            jax.ShapeDtypeStruct((TOKENS, D), low),
            jax.ShapeDtypeStruct((8, D), wide),
            jax.ShapeDtypeStruct((HALF, B_CUT), low),
            jax.ShapeDtypeStruct((HALF, B_REST), low),
            jax.ShapeDtypeStruct((HALF, B_CUT), low),
            jax.ShapeDtypeStruct((HALF, B_REST), low),
        ),
        in_specs=[small] * 3 + [near] * 6 + [far] * 4,
        out_specs=(near,) * 6 + (far,) * 4,
        scratch_shapes=[pltpu.VMEM((D, B_COLS), low)] * 2
        + [
            pltpu.VMEM((TOKENS, FF), wide),
            pltpu.VMEM((TOKENS, FF), low),
            pltpu.VMEM((TOKENS, D), wide),
            pltpu.VMEM((TOKENS, D), low),
            pltpu.VMEM((TOKENS, D), low),
            pltpu.VMEM((128, TOKENS), wide),
            pltpu.SemaphoreType.DMA((4, 2)),
            pltpu.SemaphoreType.DMA((4, 4)),
        ],
        compiler_params=pltpu.CompilerParams(vmem_limit_bytes=50 * MIB),
        cost_estimate=COST,
        name="middle",
    )(core, sizes, logdet_cot, hidden, mixed, gains, order, flow, latent_cot, *parts)


def back_weights_kernel(dq0, dk0, dv0, dq1, dk1, dv1, normed, keep, send):
    rows = normed[...].T
    crops = (rows[:, :PATCHES], rows[:, PATCHES:])
    for s, (first, second) in enumerate(((dq0, dq1), (dk0, dk1), (dv0, dv1))):
        for start in range(0, D, 256):
            columns = slice(start, start + 256)
            value = (dot(crops[0], first[:, columns]) + dot(crops[1], second[:, columns])).astype(low)
            columns = slice(s * D + start, s * D + start + 256)
            keep[:, columns] = value[:HALF]
            send[:, columns] = value[HALF:]


def back_weights(d_parts, normed):
    near = pl.BlockSpec(memory_space=pltpu.VMEM)
    return pl.pallas_call(
        back_weights_kernel,
        out_shape=(jax.ShapeDtypeStruct((HALF, QKV), low),) * 2,
        in_specs=[near] * 7,
        out_specs=(near,) * 2,
        compiler_params=pltpu.CompilerParams(vmem_limit_bytes=16 * MIB),
        cost_estimate=COST,
        name="back_weights",
    )(*d_parts, normed)


REST_COLS = 128 + ITEMS


def back_kernel(
    first_crop, dq0, dk0, dv0, dq1, dk1, dv1, hidden, d_hidden, gains, vectors, entered, d_flow,
    p_own, p_far, q_own, q_far, keep, send, d_image, sums, weights, sem,
):
    copies = []
    for k, (source, row, start, width) in enumerate(
        ((p_own, 0, 0, P_COLS), (p_far, HALF, 0, P_COLS), (q_own, 0, P_COLS, Q_TABLE), (q_far, HALF, P_COLS, Q_TABLE))
    ):
        target = weights.at[pl.ds(row, HALF), pl.ds(start, width)]
        copies.append(pltpu.make_async_copy(source.at[:, pl.ds(0, width)], target, sem.at[k]))
        copies[k].start()
    for copy in copies:
        copy.wait()
    edges, to_gain = [], jnp.zeros((1, D), wide)
    for i, parts in enumerate(((dq0, dk0, dv0), (dq1, dk1, dv1))):
        rows = slice(i * PATCHES, (i + 1) * PATCHES)
        upstream = jnp.zeros((PATCHES, D), wide)
        for s, part in enumerate(parts):
            upstream = upstream + dot(part[...], weights[:, s * D : (s + 1) * D], NT)
        value, scale = norm_parts(hidden[rows, :])
        to_input, gain_part = norm_pull(value, scale, gains[1:2, :], upstream)
        to_gain = to_gain + gain_part
        edges.append((d_hidden[rows, :] + to_input).astype(low).T)
    edge_rows = jnp.concatenate(edges, axis=1)
    sums[...] = jnp.zeros((128, D), wide)
    sums[CH : CH + 8, :] = jnp.where(iota((8, D), 0) == 1, to_gain, vectors[...])
    owner = iota((TOKENS, ITEMS), 1) == first_crop[0] + (iota((TOKENS, ITEMS), 0) >> 8)
    value = (dot(edge_rows, entered[...]) + sums[...].T).astype(low)
    keep[:, :128] = value[:HALF]
    send[:, :128] = value[HALF:]
    value = dot(edge_rows, owner.astype(low)).astype(low)
    keep[:, 128:] = value[:HALF]
    send[:, 128:] = value[HALF:]
    d_shifted = dot(weights[:, QKV:].T, edge_rows)
    lane = iota((CH, PATCHES), 1)
    for i in range(CROPS):
        moved = pltpu.roll(d_shifted[:CH, i * PATCHES : (i + 1) * PATCHES], PATCHES - 1, 1)
        d_image[i] = d_flow[i] + jnp.where(lane == PATCHES - 1, 0.0, moved)


def back(first_crop, d_parts, hidden, d_hidden, gains, vectors, entered, p_own, p_far, q_own, q_far, d_flow):
    near = pl.BlockSpec(memory_space=pltpu.VMEM)
    return pl.pallas_call(
        back_kernel,
        out_shape=(
            jax.ShapeDtypeStruct((HALF, REST_COLS), low),
            jax.ShapeDtypeStruct((HALF, REST_COLS), low),
            jax.ShapeDtypeStruct((CROPS, CH, PATCHES), wide),
        ),
        in_specs=[pl.BlockSpec(memory_space=pltpu.SMEM)] + [near] * 12 + [pl.BlockSpec(memory_space=pl.ANY)] * 4,
        out_specs=(near,) * 3,
        scratch_shapes=[
            pltpu.VMEM((128, D), wide),
            pltpu.VMEM((D, QKV + 128), low),
            pltpu.SemaphoreType.DMA((4,)),
        ],
        compiler_params=pltpu.CompilerParams(vmem_limit_bytes=VMEM_BYTES),
        cost_estimate=COST,
        name="back",
    )(first_crop, *d_parts, hidden, d_hidden, gains, vectors, entered, d_flow, p_own, p_far, q_own, q_far)


WIDTHS = (QKV, D, FF, FF)
PACK_STARTS = (0, A_COLS + M_ATTN, A_COLS, A_COLS + FF)


def pack_kernel(labels, qkv, attn, up, down, entry, vectors, table, out, order, packed, wide_rows):
    wide_rows[...] = jnp.zeros(wide_rows.shape, wide)
    for source, start, width in zip((qkv, attn, up, down), PACK_STARTS, WIDTHS):
        for row in range(ROWS):
            wide_rows[row : row + 1, start : start + width] = source[row]
    start = A_COLS + M_ATTN
    attn_rows = dot(wide_rows[:, start : start + D].astype(low), order[...])
    wide_rows[:, start : start + D] = attn_rows
    wide_rows[:ROWS, A_IN:A_VEC] = entry[...]
    lane = iota((8, 128), 1)
    marks = jnp.zeros((8, 128), wide)
    for i in range(2 * CROPS):
        first = (labels[i] >> 5).astype(wide)
        second = (labels[i] & 31).astype(wide)
        marks = jnp.where(lane == CH + NVEC + i, first, marks)
        marks = jnp.where(lane == CH + NVEC + 2 * CROPS + i, second, marks)
    wide_rows[:, A_IN:A_TABLE] = wide_rows[:, A_IN:A_TABLE] + marks
    same = iota((ROWS, ROWS), 0) == iota((ROWS, ROWS), 1)
    lane = iota((ROWS, 128), 1)
    for k in range(NVEC):
        across = jnp.broadcast_to(vectors[k : k + 1, :], (ROWS, ROWS))
        down_rows = jnp.sum(jnp.where(same, across, 0.0), axis=1, keepdims=True)
        wide_rows[:ROWS, A_IN:A_TABLE] = jnp.where(lane == CH + k, down_rows, wide_rows[:ROWS, A_IN:A_TABLE])
    wide_rows[:ROWS, A_TABLE : A_TABLE + CLASSES] = table[...]
    wide_rows[:ROWS, A_OUT : A_OUT + 2 * CH] = out[...]
    packed[...] = wide_rows[:ROWS, :].astype(low)


def pack(labels, qkv, attn, up, down, entry, vectors, table, out, order):
    near = pl.BlockSpec(memory_space=pltpu.VMEM)
    return pl.pallas_call(
        pack_kernel,
        out_shape=jax.ShapeDtypeStruct((ROWS, A_COLS + M_COLS), low),
        in_specs=[pl.BlockSpec(memory_space=pltpu.SMEM)] + [near] * 9,
        out_specs=near,
        scratch_shapes=[pltpu.VMEM((8, A_COLS + M_COLS), wide)],
        compiler_params=pltpu.CompilerParams(vmem_limit_bytes=VMEM_BYTES),
        cost_estimate=COST,
        name="pack",
    )(labels, qkv, attn, up, down, entry, vectors, table, out, order)


R_ENTRY = 4736
R_ITEM = R_ENTRY + 128
R_RIGHT = R_ITEM + ITEMS
R_OUT = 8832
R_COLS = 9728
R_PIECES = (
    (1, 0, 0, 768),
    (2, 0, 768, 1024),
    (0, 0, 1792, 768),
    (2, 1024, 2560, 1792),
    (0, 768, 4352, 384),
    (2, 2816, 5120, 256),
    (3, 0, 5376, 1536),
    (0, 1152, 6912, 384),
    (3, 1536, 7296, 1536),
    (0, 1536, 8960, 768),
)


def finish_kernel(
    own, one, two, three, places, order, qkv, attn, up, down, entry, table, out, vectors, square, rows
):
    rows[...] = jnp.zeros(rows.shape, wide)
    total = own[...].astype(wide) + one[...].astype(wide) + two[...].astype(wide) + three[...].astype(wide)
    rows[:ROWS, :] = total
    rest = rows[:, :D]
    swapped = jnp.zeros((8, D), wide)
    for _ in range(3):
        part = rest.astype(low)
        swapped = swapped + dot(part, order[...], NT)
        rest = rest - part.astype(wide)
    rows[:, :D] = swapped
    targets = (qkv, attn, up, down)
    for index, first, start, width in R_PIECES:
        for row in range(ROWS):
            targets[index][row, :, first : first + width] = rows[row : row + 1, start : start + width]
    same = iota((ROWS, ROWS), 0) == iota((ROWS, ROWS), 1)
    for k in range(NVEC):
        at = R_ENTRY + CH + k
        down_rows = jnp.broadcast_to(rows[:ROWS, at : at + 1], (ROWS, ROWS))
        vectors[k : k + 1, :] = jnp.sum(jnp.where(same, down_rows, 0.0), axis=0, keepdims=True)
    entry[...] = rows[:ROWS, R_ENTRY : R_ENTRY + CH]
    out[...] = rows[:ROWS, R_OUT : R_OUT + 2 * CH]
    by_class = dot(rows[:, R_ITEM:R_RIGHT].astype(low), places[...])
    table[...] = by_class[:ROWS, :]
    total = jnp.sum(jnp.square(by_class), axis=1, keepdims=True)
    for columns in (slice(0, R_ITEM), slice(R_RIGHT, R_COLS)):
        total = total + jnp.sum(jnp.square(rows[:, columns]), axis=1, keepdims=True)
    square[...] = jnp.broadcast_to(jnp.sum(total, axis=0, keepdims=True), (8, 128))


def finish(own, one, two, three, places, order):
    near = pl.BlockSpec(memory_space=pltpu.VMEM)
    flats = tuple(jax.ShapeDtypeStruct((ROWS, 1, width), wide) for width in WIDTHS)
    return pl.pallas_call(
        finish_kernel,
        out_shape=flats
        + (
            jax.ShapeDtypeStruct((ROWS, CH), wide),
            jax.ShapeDtypeStruct((ROWS, CLASSES), wide),
            jax.ShapeDtypeStruct((ROWS, 2 * CH), wide),
            jax.ShapeDtypeStruct((NVEC, ROWS), wide),
            jax.ShapeDtypeStruct((8, 128), wide),
        ),
        in_specs=[near] * 6,
        out_specs=(near,) * 9,
        scratch_shapes=[pltpu.VMEM((8, R_COLS), wide)],
        compiler_params=pltpu.CompilerParams(vmem_limit_bytes=16 * MIB),
        cost_estimate=COST,
        name="finish",
    )(own, one, two, three, places, order)


def adam_kernel(*refs):
    squares, gradients, states = refs[:4], refs[4:12], refs[12:36]
    results, norm_out = refs[36:60], refs[60]
    norm = jnp.sqrt(squares[0][...] + squares[1][...] + squares[2][...] + squares[3][...])
    norm_out[...] = norm[0:1, 0:1]
    factor = jnp.minimum(1.0, clip_norm / norm)[0:1, 0:1]
    for index in range(8):
        weight, first, second = (ref[...] for ref in states[3 * index : 3 * index + 3])
        gradient = gradients[index][...]
        clipped = gradient * factor.reshape((1,) * gradient.ndim)
        first_new = beta_one * first + (1.0 - beta_one) * clipped
        second_new = beta_two * second + (1.0 - beta_two) * clipped * clipped
        first_hat = first_new / (1.0 - beta_one**STEP)
        second_hat = second_new / (1.0 - beta_two**STEP)
        weight_new = weight - step_rates[index] * (
            first_hat / (jnp.sqrt(second_hat) + adam_eps) + decay_factors[index] * weight
        )
        for k, value in enumerate((first_new, second_new, weight_new)):
            results[3 * index + k][...] = value


def adam(squares, gradients, states):
    near = pl.BlockSpec(memory_space=pltpu.VMEM)
    shapes = tuple(jax.ShapeDtypeStruct(value.shape, wide) for value in states)
    return pl.pallas_call(
        adam_kernel,
        out_shape=shapes + (jax.ShapeDtypeStruct((1, 1), wide),),
        in_specs=[near] * 36,
        out_specs=(near,) * 25,
        compiler_params=pltpu.CompilerParams(vmem_limit_bytes=24 * MIB),
        cost_estimate=COST,
        name="adam",
    )(*squares, *gradients, *states)


ROUTES = (
    ("x", 1, 0, (0, 1792), (0, 768)),
    ("x", 3, 0, (1792, B_CUT), (768, 1152)),
    ("y", 1, 1, (0, 1792), (0, 384)),
    ("y", 3, 1, (1792, B_REST), (384, 1152)),
)
SIDE_QKV = QKV // 2
WIDTHS_OUT = tuple(b[1] - b[0] + a[1] - a[0] for _, _, _, b, a in ROUTES)


def by_place(value):
    return value.reshape(4, 4, 24, value.shape[1])


def both_cores(refs, columns):
    return refs[0][..., columns[0] : columns[1]].astype(wide) + refs[1][..., columns[0] : columns[1]].astype(wide)


def route_specs(m, distance):
    axis, _, side, columns, of_qkv = ROUTES[m]
    if axis == "x":
        index = lambda at: lambda *g: (g[-1][0] ^ distance(g[0]), g[-2], 0, at)
    else:
        index = lambda at: lambda *g: (g[-2], g[-1][1] ^ distance(g[0]), 0, at)
    step = of_qkv[1] - of_qkv[0]
    at = (side * SIDE_QKV + of_qkv[0]) // step
    shape = lambda width: (1, 2, 24, width) if axis == "x" else (2, 1, 24, width)
    return [pl.BlockSpec(shape(1792), index(columns[0] // 1792))] * 2 + [pl.BlockSpec(shape(step), index(at))] * 2


def own_sum(refs, m):
    columns, of_qkv = ROUTES[m][3:]
    width, step = columns[1] - columns[0], of_qkv[1] - of_qkv[0]
    return both_cores(refs[:2], (0, width)).reshape(2, 24, width), both_cores(refs[2:4], (0, step)).reshape(2, 24, step)


def fold_send_kernel(places, *refs):
    for m in range(4):
        sent = refs[16 + m]
        value, of_qkv = own_sum(refs[4 * m : 4 * m + 4], m)
        width = value.shape[-1]
        sent[0, :, :, :width] = value.astype(low)
        sent[0, :, :, width:] = of_qkv.astype(low)


def fold_send(places, left, right, qkv):
    operands, specs, out_specs = [], [], []
    for m in range(4):
        operands += route_operands(m, left, right, qkv)
        start = 1 if ROUTES[m][1] == 1 else 2
        specs += route_specs(m, lambda k, start=start: k + start)
        out_specs.append(pl.BlockSpec((1, 2, 24, WIDTHS_OUT[m]), lambda k, g, places: (k, g, 0, 0)))
    return pl.pallas_call(
        fold_send_kernel,
        grid_spec=pltpu.PrefetchScalarGridSpec(num_scalar_prefetch=1, grid=(2, 2), in_specs=specs, out_specs=out_specs),
        out_shape=[jax.ShapeDtypeStruct((2, 4, 24, width), low) for width in WIDTHS_OUT],
        compiler_params=pltpu.CompilerParams(vmem_limit_bytes=20 * MIB),
        cost_estimate=COST,
        name="fold_send",
    )(places, *operands)


def second_send_kernel(places, *refs):
    for m in range(4):
        came, sent = refs[5 * m + 4], refs[20 + m]
        value, of_qkv = own_sum(refs[5 * m : 5 * m + 4], m)
        width = value.shape[-1]
        sent[:, :, :width] = (value + came[0, :, :, :width].astype(wide)).astype(low)
        sent[:, :, width:] = (of_qkv + came[0, :, :, width:].astype(wide)).astype(low)


def slot_spec(m, here):
    slot = (0 if ROUTES[m][1] == 1 else 1) if here else (1 if ROUTES[m][1] == 1 else 0)
    return pl.BlockSpec((1, 2, 24, WIDTHS_OUT[m]), lambda g, places: (slot, g, 0, 0))


def row_spec(width):
    return pl.BlockSpec((2, 24, width), lambda g, places: (g, 0, 0))


def route_operands(m, left, right, qkv):
    return [by_place(value) for value in ((left, right)[ROUTES[m][2]] + qkv)]


def second_send(places, left, right, qkv, came):
    operands, specs = [], []
    for m in range(4):
        operands += [*route_operands(m, left, right, qkv), came[m]]
        specs += [*route_specs(m, lambda g, d=ROUTES[m][1] ^ 2: d), slot_spec(m, False)]
    return pl.pallas_call(
        second_send_kernel,
        grid_spec=pltpu.PrefetchScalarGridSpec(
            num_scalar_prefetch=1, grid=(2,), in_specs=specs, out_specs=[row_spec(width) for width in WIDTHS_OUT]
        ),
        out_shape=[jax.ShapeDtypeStruct((4, 24, width), low) for width in WIDTHS_OUT],
        compiler_params=pltpu.CompilerParams(vmem_limit_bytes=VMEM_BYTES),
        cost_estimate=COST,
        name="second_send",
    )(places, *operands)


def line_sum_kernel(places, *refs):
    left, right = refs[-2:]
    for m in range(4):
        came, late = refs[6 * m + 4 : 6 * m + 6]
        value, of_qkv = own_sum(refs[6 * m : 6 * m + 4], m)
        target, start = (left, right)[m // 2], (m % 2) * WIDTHS_OUT[m - m % 2]
        width = value.shape[-1]
        value = value + came[0, :, :, :width].astype(wide) + late[:, :, :width].astype(wide)
        target[:, :, start : start + width] = value.astype(low)
        value = of_qkv + came[0, :, :, width:].astype(wide) + late[:, :, width:].astype(wide)
        target[:, :, start + width : start + WIDTHS_OUT[m]] = value.astype(low)
    kept, other, came, late = refs[24:28]
    value = kept[0].astype(wide) + other[0].astype(wide) + came[0].astype(wide) + late[...].astype(wide)
    left[:, :, WIDTHS_OUT[0] + WIDTHS_OUT[1] :] = value.astype(low)


def line_sum(places, left, right, qkv, came, late, rest, came_rest, late_rest):
    operands, specs = [], []
    for m in range(4):
        operands += [*route_operands(m, left, right, qkv), came[m], late[m]]
        specs += [*route_specs(m, lambda g: 0), slot_spec(m, True), row_spec(WIDTHS_OUT[m])]
    operands += [by_place(value) for value in rest] + [came_rest, late_rest]
    specs += [pl.BlockSpec((1, 2, 24, REST_COLS), lambda g, places: (places[0], g, 0, 0))] * 2
    specs += [pl.BlockSpec((1, 2, 24, REST_COLS), lambda g, places: (0, g, 0, 0)), row_spec(REST_COLS)]
    widths = (R_RIGHT, R_COLS - R_RIGHT)
    return pl.pallas_call(
        line_sum_kernel,
        grid_spec=pltpu.PrefetchScalarGridSpec(
            num_scalar_prefetch=1, grid=(2,), in_specs=specs, out_specs=[row_spec(width) for width in widths]
        ),
        out_shape=[jax.ShapeDtypeStruct((4, 24, width), low) for width in widths],
        compiler_params=pltpu.CompilerParams(vmem_limit_bytes=VMEM_BYTES),
        cost_estimate=COST,
        name="line_sum",
    )(places, *operands)


def per_device(
    images,
    labels,
    crop_sizes,
    latent_cotangent,
    logdet_cotangent,
    weight_in,
    moment_in,
    second_in,
    class_table,
    moment_table,
    second_table,
    weight_qkv,
    moment_qkv,
    second_qkv,
    weight_attn,
    moment_attn,
    second_attn,
    weight_up,
    moment_up,
    second_up,
    weight_down,
    moment_down,
    second_down,
    weight_out,
    moment_out,
    second_out,
    vectors,
    moment_vectors,
    second_vectors,
):
    core = lax.axis_index("c")
    chip = lax.axis_index(("x", "y", "z"))
    half = PATCHES // 2

    order = order_matrix()
    rows_of = lambda value: jnp.transpose(value, (1, 0, 2))
    rows_down = lambda value: jnp.transpose(value, (2, 0, 1))
    packed = pack(
        labels, rows_of(weight_qkv), rows_of(weight_attn), rows_of(weight_up), rows_down(weight_down),
        weight_in.T, vectors, class_table.T, weight_out, order,
    )

    inputs = jnp.stack([images, latent_cotangent])
    mine = lax.dynamic_slice_in_dim(inputs, core * CROPS, CROPS, 1)
    theirs = swap(lax.dynamic_slice_in_dim(inputs, (1 - core) * CROPS, CROPS, 1), "c", 1)
    whole = jnp.where(
        core == 0,
        jnp.concatenate([mine, theirs], axis=-1),
        jnp.concatenate([theirs, mine], axis=-1),
    )
    flow = whole[0][:, :, ::-1]
    latent_cot = whole[1]
    logdet_cot = lax.dynamic_slice_in_dim(logdet_cotangent, core * CROPS, CROPS, 0)
    sizes = lax.dynamic_slice_in_dim(crop_sizes, core * CROPS, CROPS, 0)
    my_labels = lax.dynamic_slice_in_dim(labels, core * CROPS, CROPS, 0)

    rows_a = gather_four(packed, "z", 0).reshape(4 * ROWS, A_COLS + M_COLS)
    b_own = lax.all_gather(rows_a[:, A_COLS:], ("x", "y"), axis=0, tiled=True)
    p_own = gather_four(gather_four(rows_a[:, :P_COLS], "y", 0), "x", 0).reshape(HALF, P_COLS)
    q_own = gather_four(gather_four(rows_a[:, P_COLS:A_COLS], "x", 0), "y", 1).reshape(HALF, Q_COLS)
    p_far = swap(p_own, "c", 1)
    q_far = swap(q_own, "c", 1)

    hidden, normed, qkv, gains, entered = front(my_labels, flow, p_own, p_far, q_own, q_far)
    b_own, qkv = together((b_own, qkv))
    b_far = swap(b_own, "c", 1)
    mixed = attend(sizes, qkv)
    label_parts = q_own[::ROWS, Q_X + CH + NVEC : Q_X + CH + NVEC + 8].astype(wide).astype(jnp.int32)
    all_labels = (label_parts[:, :4] * 32 + label_parts[:, 4:]).reshape(ITEMS)
    class_places = (all_labels[:, None] == jnp.arange(CLASSES, dtype=jnp.int32)[None, :]).astype(low)
    mixed, class_places = together((mixed, class_places))
    masked_latent, d_flow, logdet_rows, d_hidden, d_mixed, vector_rows, keep_p, keep_q, send_p, send_q = middle(
        core[None], sizes, logdet_cot, hidden, mixed, gains, order, flow, latent_cot, q_own, q_far, b_own, b_far
    )
    came_p, came_q = swap(send_p, "c", 1), swap(send_q, "c", 1)
    d_parts = (*attend_back(0, sizes, qkv, d_mixed), *attend_back(1, sizes, qkv, d_mixed))
    keep_a, send_a = back_weights(d_parts, normed)
    came_a = swap(send_a, "c", 1)
    places = jnp.stack([lax.axis_index("x"), lax.axis_index("y")])
    sums = ((keep_p, came_p), (keep_q, came_q), (keep_a, came_a))
    sent = fold_send(places, *sums)
    sent, hidden_late = together((sent, hidden))
    came = [swap(value, route[0], route[1]) for value, route in zip(sent, ROUTES)]
    first_crop = (chip * 4 + core * CROPS)[None]
    keep_r, send_r, d_image = back(
        first_crop, d_parts, hidden_late, d_hidden, gains, vector_rows, entered,
        p_own, p_far, q_own, q_far, d_flow,
    )
    came_r = swap(send_r, "c", 1)
    place_x = lax.axis_index("x")

    def rest_block(distance):
        blocks = [lax.dynamic_index_in_dim(by_place(value), place_x ^ distance, 0, keepdims=False) for value in (keep_r, came_r)]
        return blocks[0].astype(wide) + blocks[1].astype(wide)

    came_rest = swap(jnp.stack([rest_block(1).astype(low), rest_block(2).astype(low)]), "x", 1)
    came, came_rest = together((came, came_rest))
    sent = second_send(places, *sums, came)
    sent_rest = (rest_block(3) + came_rest[1].astype(wide)).astype(low)
    sent, sent_rest = together((sent, sent_rest))
    late = [swap(value, route[0], route[1] ^ 2) for value, route in zip(sent, ROUTES)]
    late_rest = swap(sent_rest, "x", 3)
    left, right = line_sum(places, *sums, came, late, (keep_r, came_r), came_rest, late_rest)
    pick = lambda value: lambda place: lax.dynamic_index_in_dim(value, place, 0, keepdims=False)
    left = scatter_four(pick(left), "y").astype(low)
    right = scatter_four(pick(right), "x").astype(low)
    last = jnp.concatenate([left, right], axis=1).reshape(4, ROWS, R_COLS)
    level = lax.axis_index("z")
    parts = [lax.dynamic_index_in_dim(last, level ^ k, 0, keepdims=False) for k in range(4)]
    parts = [parts[0]] + [swap(parts[k], "z", k) for k in (1, 2, 3)]

    image_back = d_image[:, :, ::-1]
    logdet_own = logdet_rows[::8, 0]

    def to_places(value):
        kept = lax.dynamic_slice_in_dim(value, core * half, half, 2)
        came = swap(lax.dynamic_slice_in_dim(value, (1 - core) * half, half, 2), "c", 1)
        return jnp.where(
            core == 0, jnp.concatenate([kept, came], axis=0), jnp.concatenate([came, kept], axis=0)
        )

    latents = to_places(masked_latent)
    image_grad = to_places(image_back)
    came_logdet = swap(logdet_rows, "c", 1)[::8, 0]
    logdet = jnp.where(
        core == 0,
        jnp.concatenate([logdet_own, came_logdet]),
        jnp.concatenate([came_logdet, logdet_own]),
    )

    *grads, grad_entry, grad_table, grad_out, grad_vectors, square = finish(*parts, class_places, order)
    square = square + swap(square, "c", 1)
    for axis in ("z", "y"):
        square = square + swap(square, axis, 1) + swap(square, axis, 2) + swap(square, axis, 3)
    squares = [square] + [swap(square, "x", k) for k in (1, 2, 3)]

    rows_back = lambda value: jnp.transpose(value, (1, 0, 2))
    turned = lambda value: value.T
    same = lambda value: value
    views = (
        (turned, turned, grad_entry),
        (turned, turned, grad_table),
        (rows_of, rows_back, grads[0]),
        (rows_of, rows_back, grads[1]),
        (rows_of, rows_back, grads[2]),
        (rows_down, lambda value: jnp.transpose(value, (1, 2, 0)), grads[3]),
        (same, same, grad_out),
        (same, same, grad_vectors),
    )
    states = (
        (weight_in, moment_in, second_in),
        (class_table, moment_table, second_table),
        (weight_qkv, moment_qkv, second_qkv),
        (weight_attn, moment_attn, second_attn),
        (weight_up, moment_up, second_up),
        (weight_down, moment_down, second_down),
        (weight_out, moment_out, second_out),
        (vectors, moment_vectors, second_vectors),
    )
    entered_states = [view[0](value) for view, group in zip(views, states) for value in group]
    *results, norm = adam(squares, [view[2] for view in views], entered_states)
    updated = [views[k // 3][1](value) for k, value in enumerate(results)]
    return (latents, logdet, image_grad, norm.reshape(()), *updated)


def solution(mesh):
    chips = Mesh(mesh.devices.reshape(4, 4, 4, 2), ("x", "y", "z", "c"))
    dp, every = ("x", "y", "z"), ("x", "y", "z", "c")
    patches = P(dp, None, "c")
    columns, rows, last = P(None, every), P(None, every, None), P(None, None, every)
    parameters = (columns,) * 6 + (rows,) * 9 + (last,) * 3 + (P(every, None),) * 3 + (columns,) * 3
    return jax.shard_map(
        per_device,
        mesh=chips,
        in_specs=(patches, P(dp), P(dp, None), patches, P(dp)) + parameters,
        out_specs=(patches, P(dp), patches, P()) + parameters,
        check_vma=False,
    )
```

```python
import functools

import jax
import jax.numpy as jnp
import numpy as np
from jax import lax
from jax.experimental import pallas as pl
from jax.experimental.pallas import tpu as pltpu
from jax.sharding import Mesh, PartitionSpec as P

D = 768
HEADS = 12
HEAD = 64
CH = 48
CLASSES = 1000
SIDE = 16
STEP = 5
PATCHES = 256
ITEMS = 256
FF = 3072
NVEC = 6
ROWS = 6
CROPS = 2

beta_one = 0.9
beta_two = 0.95
adam_eps = 1e-08
step_rates = (0.02, 0.3, 0.02, 0.1, 0.02, 0.02, 0.02, 0.2)
decay_factors = (0.1, 0.1, 0.1, 0.1, 0.1, 0.1, 0.1, 0.0)
clip_norm = 1.0
norm_eps = 1e-06

QKV = 3 * D
A_IN = QKV
A_VEC = A_IN + CH
A_LAB = A_VEC + NVEC
A_TABLE = QKV + 128
A_OUT = A_TABLE + 1024
A_COLS = A_OUT + 128
M_ATTN = 2 * FF
M_COLS = M_ATTN + D
B_UP = D
B_DOWN = B_UP + FF
B_OUT = B_DOWN + FF
B_END = B_OUT + 2 * CH
B_COLS = B_OUT + 128
G_VEC = QKV + CH
G_ITEM = QKV + 128
G_COLS = G_ITEM + ITEMS
G_CUT = 1408
B_CUT = 3584
B_REST = B_COLS - B_CUT

low = jnp.bfloat16
wide = jnp.float32


together = lax.optimization_barrier


def swap(value, axis, distance):
    size = lax.axis_size(axis)
    return lax.ppermute(value, axis, [(i, i ^ distance) for i in range(size)])


def gather_four(value, axis, dim):
    place = lax.axis_index(axis)
    parts = [value] + [swap(value, axis, k) for k in (1, 2, 3)]
    shape = value.shape[:dim] + (4,) + value.shape[dim:]
    result = jnp.zeros(shape, value.dtype)
    for k, part in enumerate(parts):
        result = lax.dynamic_update_index_in_dim(result, part, place ^ k, dim)
    return result


def scatter_four(piece, axis):
    place = lax.axis_index(axis)
    total = piece(place).astype(wide)
    for k in (1, 2, 3):
        total = total + swap(piece(place ^ k).astype(low), axis, k).astype(wide)
    return total


def order_matrix():
    natural = np.arange(D)
    place = (natural // ROWS) % 2 * (D // 2) + natural // (2 * ROWS) * ROWS + natural % ROWS
    return (place[:, None] == natural[None, :]).astype(low)


NN = (((1,), (0,)), ((), ()))
NT = (((1,), (1,)), ((), ()))
HALF = D // 2
TOKENS = CROPS * PATCHES
P_COLS = A_COLS // 2
Q_COLS = A_COLS // 2
Q_X = QKV - P_COLS
Q_TABLE = Q_X + 128
Q_OUT = Q_TABLE + 1024
MASKED = -1e30
SCALE = HEAD ** (-0.5)
MIB = 1024 * 1024
VMEM_BYTES = 58 * MIB
COST = pl.CostEstimate(flops=1000, bytes_accessed=1000, transcendentals=0)


def dot(left_side, right_side, how=NN):
    return lax.dot_general(left_side, right_side, how, preferred_element_type=wide)


def iota(shape, axis):
    return lax.broadcasted_iota(jnp.int32, shape, axis)


def crop_valid(place, height, width):
    natural = PATCHES - 1 - place
    return ((natural >> 4) < height) & ((natural & 15) < width)


def norm_parts(value):
    mean = jnp.mean(value, axis=-1, keepdims=True)
    centered = value - mean
    scale = lax.rsqrt(jnp.mean(centered * centered, axis=-1, keepdims=True) + norm_eps)
    return centered * scale, scale


def norm_pull(normed, scale, gain, upstream):
    inner = upstream * gain
    to_input = scale * (
        inner
        - jnp.mean(inner, axis=-1, keepdims=True)
        - normed * jnp.mean(inner * normed, axis=-1, keepdims=True)
    )
    return to_input, jnp.sum(upstream * normed, axis=0, keepdims=True)


GELU_ROOT = 0.7978845608028654
GELU_CUBE = 0.044715


def gelu_tanh(value):
    return jnp.tanh(GELU_ROOT * (value + GELU_CUBE * (value * value * value)))


def front_kernel(
    labels, flow, p_own, p_far, q_own, q_far, hidden, normed, qkv, gains, entered, weights, sem
):
    copies = []
    for k, (source, row, start, width) in enumerate(
        ((q_own, 0, P_COLS, Q_OUT), (q_far, HALF, P_COLS, Q_OUT), (p_own, 0, 0, P_COLS), (p_far, HALF, 0, P_COLS))
    ):
        copies.append(
            pltpu.make_async_copy(
                source.at[:, pl.ds(0, width)], weights.at[pl.ds(row, HALF), pl.ds(start, width)], sem.at[k]
            )
        )
        copies[k].start()
    lane = iota((CH, PATCHES), 1)
    for i in range(CROPS):
        moved = jnp.where(lane == 0, 0.0, pltpu.roll(flow[i], 1, 1))
        below = jnp.where(iota((128 - CH, PATCHES), 0) == 0, 1.0, 0.0)
        both = jnp.concatenate([moved, below], axis=0)
        entered[i * PATCHES : (i + 1) * PATCHES, :] = both.T.astype(low)
    pick = (iota((8, 128), 1) == iota((8, 128), 0) + CH).astype(low)
    chosen = iota((8, 1024), 1) == jnp.where(iota((8, 1024), 0) == 0, labels[0], labels[1])
    chosen = chosen.astype(low)
    copies[0].wait()
    copies[1].wait()
    block = weights[:, QKV:A_TABLE]
    gains[...] = dot(pick, block, NT)
    class_rows = dot(chosen, weights[:, A_TABLE:], NT)
    for i in range(CROPS):
        rows = slice(i * PATCHES, (i + 1) * PATCHES)
        value = dot(entered[rows, :], block, NT) + class_rows[i : i + 1, :]
        hidden[rows, :] = value
        value, _ = norm_parts(value)
        normed[rows, :] = (value * gains[1:2, :]).astype(low)
    copies[2].wait()
    copies[3].wait()
    for start in range(0, QKV, 256):
        qkv[:, start : start + 256] = dot(normed[...], weights[:, start : start + 256]).astype(low)


def front(labels, flow, p_own, p_far, q_own, q_far):
    near, far = pl.BlockSpec(memory_space=pltpu.VMEM), pl.BlockSpec(memory_space=pl.ANY)
    return pl.pallas_call(
        front_kernel,
        out_shape=(
            jax.ShapeDtypeStruct((TOKENS, D), wide),
            jax.ShapeDtypeStruct((TOKENS, D), low),
            jax.ShapeDtypeStruct((TOKENS, QKV), low),
            jax.ShapeDtypeStruct((8, D), wide),
            jax.ShapeDtypeStruct((TOKENS, 128), low),
        ),
        in_specs=[pl.BlockSpec(memory_space=pltpu.SMEM), near] + [far] * 4,
        out_specs=(near,) * 5,
        scratch_shapes=[pltpu.VMEM((D, A_OUT), low), pltpu.SemaphoreType.DMA((4,))],
        compiler_params=pltpu.CompilerParams(vmem_limit_bytes=VMEM_BYTES),
        cost_estimate=COST,
        name="front",
    )(labels, flow, p_own, p_far, q_own, q_far)


HEAD_PAIRS = HEADS // 2
STEP_PAIRS = 6


def pair_blocks(pair):
    return slice(pair * 128, (pair + 1) * 128)


def head_masks():
    first = iota((PATCHES, 128), 1) < HEAD
    return first, jnp.logical_not(first)


def attend_kernel(sizes, queries, keys, values, mixed):
    crop = pl.program_id(0)
    shape = (PATCHES, PATCHES)
    place, key_place = iota(shape, 0), iota(shape, 1)
    valid = crop_valid(key_place, sizes[crop, 0], sizes[crop, 1])
    allowed = (key_place == place) | ((key_place < place) & valid)
    masks = head_masks()
    heads = [(pair, mine) for pair in range(STEP_PAIRS) for mine in masks]
    exponents, inverses = [], []
    for pair, mine in heads:
        block = pair_blocks(pair)
        scores = dot(queries[:, block] * low(SCALE), jnp.where(mine, keys[:, block], 0), NT)
        scores = jnp.where(allowed, scores, MASKED)
        exponent = jnp.exp(scores - jnp.max(scores, axis=-1, keepdims=True))
        exponents.append(exponent)
        inverses.append(1.0 / jnp.sum(exponent, axis=-1, keepdims=True))
    for pair in range(STEP_PAIRS):
        block = pair_blocks(pair)
        total = jnp.zeros((PATCHES, 128), wide)
        for k, mine in enumerate(masks):
            soft = (exponents[2 * pair + k] * inverses[2 * pair + k]).astype(low)
            total = total + dot(soft, jnp.where(mine, values[:, block], 0))
        mixed[:, block] = total.astype(low)


def attend(sizes, qkv):
    steps = HEAD_PAIRS // STEP_PAIRS
    shape = (PATCHES, STEP_PAIRS * 128)
    return pl.pallas_call(
        attend_kernel,
        grid=(CROPS, steps),
        out_shape=jax.ShapeDtypeStruct((TOKENS, D), low),
        in_specs=[pl.BlockSpec(memory_space=pltpu.SMEM)]
        + [pl.BlockSpec(shape, lambda i, h, s=s: (i, s * steps + h)) for s in range(3)],
        out_specs=pl.BlockSpec(shape, lambda i, h: (i, h)),
        compiler_params=pltpu.CompilerParams(vmem_limit_bytes=16 * MIB),
        cost_estimate=COST,
        name="attend",
    )(sizes, qkv, qkv, qkv)


def attend_back_kernel(crop, sizes, queries, keys, values, d_mixed, d_queries, d_keys, d_values):
    shape = (PATCHES, PATCHES)
    key_place, place = iota(shape, 0), iota(shape, 1)
    valid = crop_valid(key_place, sizes[crop, 0], sizes[crop, 1])
    allowed = (key_place == place) | ((key_place < place) & valid)
    masks = head_masks()
    heads = [(pair, mine) for pair in range(STEP_PAIRS) for mine in masks]
    softs = []
    for pair, mine in heads:
        block = pair_blocks(pair)
        scores = dot(jnp.where(mine, keys[:, block], 0), queries[:, block] * low(SCALE), NT)
        scores = jnp.where(allowed, scores, MASKED)
        exponent = jnp.exp(scores - jnp.max(scores, axis=0, keepdims=True))
        softs.append(exponent * (1.0 / jnp.sum(exponent, axis=0, keepdims=True)))
    slopes = []
    for soft, (pair, mine) in zip(softs, heads):
        block = pair_blocks(pair)
        d_soft = dot(jnp.where(mine, values[:, block], 0), d_mixed[:, block], NT)
        d_scores = soft * (d_soft - jnp.sum(d_soft * soft, axis=0, keepdims=True))
        slopes.append(d_scores.astype(low))
    for pair in range(STEP_PAIRS):
        block = pair_blocks(pair)
        to_queries = jnp.zeros((PATCHES, 128), wide)
        to_keys = jnp.zeros((PATCHES, 128), wide)
        to_values = jnp.zeros((PATCHES, 128), wide)
        for k, mine in enumerate(masks):
            soft, slope = softs[2 * pair + k], slopes[2 * pair + k]
            to_values = to_values + dot(soft.astype(low), jnp.where(mine, d_mixed[:, block], 0))
            to_keys = to_keys + dot(slope, jnp.where(mine, queries[:, block] * low(SCALE), 0))
            to_queries = to_queries + dot(slope.T, jnp.where(mine, keys[:, block], 0))
        d_queries[:, block] = (to_queries * SCALE).astype(low)
        d_keys[:, block] = to_keys.astype(low)
        d_values[:, block] = to_values.astype(low)


def attend_back(crop, sizes, qkv, d_mixed):
    steps = HEAD_PAIRS // STEP_PAIRS
    shape = (PATCHES, STEP_PAIRS * 128)
    block = pl.BlockSpec(shape, lambda h: (0, h))
    return pl.pallas_call(
        functools.partial(attend_back_kernel, crop),
        grid=(steps,),
        out_shape=(jax.ShapeDtypeStruct((PATCHES, D), low),) * 3,
        in_specs=[pl.BlockSpec(memory_space=pltpu.SMEM)]
        + [pl.BlockSpec(shape, lambda h, s=s: (crop, s * steps + h)) for s in range(3)]
        + [pl.BlockSpec(shape, lambda h: (crop, h))],
        out_specs=(block,) * 3,
        compiler_params=pltpu.CompilerParams(vmem_limit_bytes=16 * MIB),
        cost_estimate=COST,
        name="attend_back",
    )(sizes, qkv, qkv, qkv, d_mixed)


SECTIONS = ((0, D), (B_UP, FF), (B_DOWN, FF), (B_OUT, 128))
STEP_COLS = 512


def middle_kernel(
    core_ref, sizes, logdet_cot, hidden_in, mixed, gains, order, flow, latent_cot, q_own, q_far, b_own, b_far,
    latents, d_flow, logdet, d_hidden, d_mixed, vectors_out, keep_p, keep_q, send_p, send_q,
    weights, grads, up_proj, active, hidden, normed_two, branch, d_head, sem_in, sem_out,
):
    core = core_ref[0]
    keep, send = (keep_p, keep_q), (send_p, send_q)
    loads = []
    for k, (start, width) in enumerate(SECTIONS):
        pair = []
        for j, (first, second) in enumerate(((q_own, b_own), (q_far, b_far))):
            source, at = ((second, M_ATTN), (second, 0), (second, FF), (first, Q_OUT))[k]
            target = weights.at[pl.ds(j * HALF, HALF), pl.ds(start, width)]
            copy = pltpu.make_async_copy(source.at[:, pl.ds(at, width)], target, sem_in.at[k, j])
            copy.start()
            pair.append(copy)
        loads.append(pair)
    stores = []

    def store(section):
        start, width = SECTIONS[section]
        for part, (low_end, high_end) in enumerate(((0, B_CUT), (B_CUT, B_COLS))):
            first, last = max(start, low_end), min(start + width, high_end)
            if first >= last:
                continue
            for j, target in enumerate((keep[part], send[part])):
                copy = pltpu.make_async_copy(
                    grads.at[pl.ds(j * HALF, HALF), pl.ds(first, last - first)],
                    target.at[:, pl.ds(first - low_end, last - first)],
                    sem_out.at[section, 2 * part + j],
                )
                copy.start()
                stores.append(copy)

    def arrived(section):
        for copy in loads[section]:
            copy.wait()

    def half_at(k):
        return pl.ds(pl.multiple_of((k ^ core) * HALF, 128), HALF)

    gain = lambda row: gains[row : row + 1, :]
    halves = (slice(0, HALF), slice(HALF, D))

    mixed_here = jnp.concatenate([dot(mixed[...], order[:, half_at(k)]) for k in range(2)], axis=1).astype(low)
    mixed_rows = mixed_here.T
    arrived(0)
    for k, columns in enumerate(halves):
        value = dot(mixed_here, weights[:, half_at(k)])
        hidden[:, columns] = hidden_in[:, columns] + value + gains[2:3, columns]

    value, _ = norm_parts(hidden[...])
    normed_two[...] = (value * gain(3)).astype(low)
    arrived(1)
    for step in range(0, FF, STEP_COLS):
        columns = slice(B_UP + step, B_UP + step + STEP_COLS)
        value = dot(normed_two[...], weights[:, columns])
        up_proj[:, step : step + STEP_COLS] = value
        active[:, step : step + STEP_COLS] = (0.5 * value * (1.0 + gelu_tanh(value))).astype(low)
    arrived(2)
    d_hidden[...] = hidden[...] + dot(active[...], weights[:, B_DOWN:B_OUT], NT) + gain(4)

    last, last_scale = norm_parts(d_hidden[...])
    final_rows = (last * gain(5)).astype(low).T
    arrived(3)
    head_rows = weights[:, B_OUT:].T
    output = dot(head_rows, final_rows)
    place = iota((CH, PATCHES), 1)
    for i in range(CROPS):
        columns = slice(i * PATCHES, (i + 1) * PATCHES)
        valid = crop_valid(place, sizes[i, 0], sizes[i, 1]).astype(wide)
        log_scale = output[CH : 2 * CH, columns]
        inverse = jnp.exp(-log_scale)
        latent = (flow[i] - output[:CH, columns]) * inverse
        latents[i] = latent * valid
        terms = jnp.sum(jnp.sum(log_scale * valid, axis=1, keepdims=True), axis=0, keepdims=True)
        logdet[8 * i : 8 * i + 8, :] = jnp.broadcast_to(-terms, (8, 128))
        d_latent = latent_cot[i] * valid
        to_flow = d_latent * inverse
        d_flow[i] = to_flow
        d_head[:CH, columns] = -to_flow
        d_head[CH : 2 * CH, columns] = -d_latent * latent - valid * logdet_cot[i]
        d_head[2 * CH :, columns] = jnp.zeros((128 - 2 * CH, PATCHES), wide)
    d_output = d_head[...].astype(low)
    d_output_rows = d_head[...].T.astype(low)
    grads[:, B_OUT:] = dot(final_rows, d_output, NT).astype(low)
    store(3)
    upstream = dot(d_output_rows, head_rows)
    to_input, to_gain = norm_pull(last, last_scale, gain(5), upstream)
    vectors_out[5:6, :] = to_gain
    d_hidden[...] = to_input

    edge = d_hidden[...].astype(low)
    vectors_out[4:5, :] = jnp.sum(edge.astype(wide), axis=0, keepdims=True)
    edge_rows = edge.T
    normed_rows = normed_two[...].T
    for step in range(0, FF, STEP_COLS):
        columns = slice(B_DOWN + step, B_DOWN + step + STEP_COLS)
        up_columns = slice(B_UP + step, B_UP + step + STEP_COLS)
        chunk = slice(step, step + STEP_COLS)
        d_active = dot(edge, weights[:, columns])
        grads[:, columns] = dot(edge_rows, active[:, chunk]).astype(low)
        value = up_proj[:, chunk]
        tanh = gelu_tanh(value)
        slope = 0.5 * (1.0 + tanh) + 0.5 * value * (1.0 - tanh * tanh) * GELU_ROOT * (
            1.0 + 3.0 * GELU_CUBE * value * value
        )
        d_up = (d_active * slope).astype(low)
        active[:, chunk] = d_up
        grads[:, up_columns] = dot(normed_rows, d_up).astype(low)
    store(2)
    store(1)
    upstream = dot(active[...], weights[:, B_UP:B_DOWN], NT)
    value, scale = norm_parts(hidden[...])
    to_input, to_gain = norm_pull(value, scale, gain(3), upstream)
    vectors_out[3:4, :] = to_gain
    d_hidden[...] = d_hidden[...] + to_input

    edge = d_hidden[...].astype(low)
    vectors_out[2:3, :] = jnp.sum(edge.astype(wide), axis=0, keepdims=True)
    vectors_out[0:2, :] = jnp.zeros((2, D), wide)
    vectors_out[6:8, :] = jnp.zeros((2, D), wide)
    branch[...] = edge
    parts = [branch[:, half_at(k)] for k in range(2)]
    natural = jnp.concatenate(parts, axis=1)
    grads[:, :D] = dot(mixed_rows, natural).astype(low)
    store(0)
    d_here = dot(natural, weights[:, :D], NT).astype(low)
    branch[...] = d_here
    natural = jnp.concatenate([branch[:, half_at(k)] for k in range(2)], axis=1)
    d_mixed[...] = dot(natural, order[...], NT).astype(low)
    for copy in stores:
        copy.wait()


def middle(core, sizes, logdet_cot, hidden, mixed, gains, order, flow, latent_cot, *parts):
    small = pl.BlockSpec(memory_space=pltpu.SMEM)
    near = pl.BlockSpec(memory_space=pltpu.VMEM)
    far = pl.BlockSpec(memory_space=pl.ANY)
    return pl.pallas_call(
        middle_kernel,
        out_shape=(
            jax.ShapeDtypeStruct((CROPS, CH, PATCHES), wide),
            jax.ShapeDtypeStruct((CROPS, CH, PATCHES), wide),
            jax.ShapeDtypeStruct((8 * CROPS, 128), wide),
            jax.ShapeDtypeStruct((TOKENS, D), wide),
            jax.ShapeDtypeStruct((TOKENS, D), low),
            jax.ShapeDtypeStruct((8, D), wide),
            jax.ShapeDtypeStruct((HALF, B_CUT), low),
            jax.ShapeDtypeStruct((HALF, B_REST), low),
            jax.ShapeDtypeStruct((HALF, B_CUT), low),
            jax.ShapeDtypeStruct((HALF, B_REST), low),
        ),
        in_specs=[small] * 3 + [near] * 6 + [far] * 4,
        out_specs=(near,) * 6 + (far,) * 4,
        scratch_shapes=[pltpu.VMEM((D, B_COLS), low)] * 2
        + [
            pltpu.VMEM((TOKENS, FF), wide),
            pltpu.VMEM((TOKENS, FF), low),
            pltpu.VMEM((TOKENS, D), wide),
            pltpu.VMEM((TOKENS, D), low),
            pltpu.VMEM((TOKENS, D), low),
            pltpu.VMEM((128, TOKENS), wide),
            pltpu.SemaphoreType.DMA((4, 2)),
            pltpu.SemaphoreType.DMA((4, 4)),
        ],
        compiler_params=pltpu.CompilerParams(vmem_limit_bytes=50 * MIB),
        cost_estimate=COST,
        name="middle",
    )(core, sizes, logdet_cot, hidden, mixed, gains, order, flow, latent_cot, *parts)


def back_weights_kernel(dq0, dk0, dv0, dq1, dk1, dv1, normed, keep, send):
    rows = normed[...].T
    crops = (rows[:, :PATCHES], rows[:, PATCHES:])
    for s, (first, second) in enumerate(((dq0, dq1), (dk0, dk1), (dv0, dv1))):
        for start in range(0, D, 256):
            columns = slice(start, start + 256)
            value = (dot(crops[0], first[:, columns]) + dot(crops[1], second[:, columns])).astype(low)
            columns = slice(s * D + start, s * D + start + 256)
            keep[:, columns] = value[:HALF]
            send[:, columns] = value[HALF:]


def back_weights(d_parts, normed):
    near = pl.BlockSpec(memory_space=pltpu.VMEM)
    return pl.pallas_call(
        back_weights_kernel,
        out_shape=(jax.ShapeDtypeStruct((HALF, QKV), low),) * 2,
        in_specs=[near] * 7,
        out_specs=(near,) * 2,
        compiler_params=pltpu.CompilerParams(vmem_limit_bytes=16 * MIB),
        cost_estimate=COST,
        name="back_weights",
    )(*d_parts, normed)


REST_COLS = 128 + ITEMS


def back_kernel(
    first_crop, dq0, dk0, dv0, dq1, dk1, dv1, hidden, d_hidden, gains, vectors, entered, d_flow,
    p_own, p_far, q_own, q_far, keep, send, d_image, sums, weights, sem,
):
    copies = []
    for k, (source, row, start, width) in enumerate(
        ((p_own, 0, 0, P_COLS), (p_far, HALF, 0, P_COLS), (q_own, 0, P_COLS, Q_TABLE), (q_far, HALF, P_COLS, Q_TABLE))
    ):
        target = weights.at[pl.ds(row, HALF), pl.ds(start, width)]
        copies.append(pltpu.make_async_copy(source.at[:, pl.ds(0, width)], target, sem.at[k]))
        copies[k].start()
    for copy in copies:
        copy.wait()
    edges, to_gain = [], jnp.zeros((1, D), wide)
    for i, parts in enumerate(((dq0, dk0, dv0), (dq1, dk1, dv1))):
        rows = slice(i * PATCHES, (i + 1) * PATCHES)
        upstream = jnp.zeros((PATCHES, D), wide)
        for s, part in enumerate(parts):
            upstream = upstream + dot(part[...], weights[:, s * D : (s + 1) * D], NT)
        value, scale = norm_parts(hidden[rows, :])
        to_input, gain_part = norm_pull(value, scale, gains[1:2, :], upstream)
        to_gain = to_gain + gain_part
        edges.append((d_hidden[rows, :] + to_input).astype(low).T)
    edge_rows = jnp.concatenate(edges, axis=1)
    sums[...] = jnp.zeros((128, D), wide)
    sums[CH : CH + 8, :] = jnp.where(iota((8, D), 0) == 1, to_gain, vectors[...])
    owner = iota((TOKENS, ITEMS), 1) == first_crop[0] + (iota((TOKENS, ITEMS), 0) >> 8)
    value = (dot(edge_rows, entered[...]) + sums[...].T).astype(low)
    keep[:, :128] = value[:HALF]
    send[:, :128] = value[HALF:]
    value = dot(edge_rows, owner.astype(low)).astype(low)
    keep[:, 128:] = value[:HALF]
    send[:, 128:] = value[HALF:]
    d_shifted = dot(weights[:, QKV:].T, edge_rows)
    lane = iota((CH, PATCHES), 1)
    for i in range(CROPS):
        moved = pltpu.roll(d_shifted[:CH, i * PATCHES : (i + 1) * PATCHES], PATCHES - 1, 1)
        d_image[i] = d_flow[i] + jnp.where(lane == PATCHES - 1, 0.0, moved)


def back(first_crop, d_parts, hidden, d_hidden, gains, vectors, entered, p_own, p_far, q_own, q_far, d_flow):
    near = pl.BlockSpec(memory_space=pltpu.VMEM)
    return pl.pallas_call(
        back_kernel,
        out_shape=(
            jax.ShapeDtypeStruct((HALF, REST_COLS), low),
            jax.ShapeDtypeStruct((HALF, REST_COLS), low),
            jax.ShapeDtypeStruct((CROPS, CH, PATCHES), wide),
        ),
        in_specs=[pl.BlockSpec(memory_space=pltpu.SMEM)] + [near] * 12 + [pl.BlockSpec(memory_space=pl.ANY)] * 4,
        out_specs=(near,) * 3,
        scratch_shapes=[
            pltpu.VMEM((128, D), wide),
            pltpu.VMEM((D, QKV + 128), low),
            pltpu.SemaphoreType.DMA((4,)),
        ],
        compiler_params=pltpu.CompilerParams(vmem_limit_bytes=VMEM_BYTES),
        cost_estimate=COST,
        name="back",
    )(first_crop, *d_parts, hidden, d_hidden, gains, vectors, entered, d_flow, p_own, p_far, q_own, q_far)


WIDTHS = (QKV, D, FF, FF)
PACK_STARTS = (0, A_COLS + M_ATTN, A_COLS, A_COLS + FF)


def pack_kernel(labels, qkv, attn, up, down, entry, vectors, table, out, order, packed, wide_rows):
    wide_rows[...] = jnp.zeros(wide_rows.shape, wide)
    for source, start, width in zip((qkv, attn, up, down), PACK_STARTS, WIDTHS):
        for row in range(ROWS):
            wide_rows[row : row + 1, start : start + width] = source[row]
    start = A_COLS + M_ATTN
    attn_rows = dot(wide_rows[:, start : start + D].astype(low), order[...])
    wide_rows[:, start : start + D] = attn_rows
    wide_rows[:ROWS, A_IN:A_VEC] = entry[...]
    lane = iota((8, 128), 1)
    marks = jnp.zeros((8, 128), wide)
    for i in range(2 * CROPS):
        first = (labels[i] >> 5).astype(wide)
        second = (labels[i] & 31).astype(wide)
        marks = jnp.where(lane == CH + NVEC + i, first, marks)
        marks = jnp.where(lane == CH + NVEC + 2 * CROPS + i, second, marks)
    wide_rows[:, A_IN:A_TABLE] = wide_rows[:, A_IN:A_TABLE] + marks
    same = iota((ROWS, ROWS), 0) == iota((ROWS, ROWS), 1)
    lane = iota((ROWS, 128), 1)
    for k in range(NVEC):
        across = jnp.broadcast_to(vectors[k : k + 1, :], (ROWS, ROWS))
        down_rows = jnp.sum(jnp.where(same, across, 0.0), axis=1, keepdims=True)
        wide_rows[:ROWS, A_IN:A_TABLE] = jnp.where(lane == CH + k, down_rows, wide_rows[:ROWS, A_IN:A_TABLE])
    wide_rows[:ROWS, A_TABLE : A_TABLE + CLASSES] = table[...]
    wide_rows[:ROWS, A_OUT : A_OUT + 2 * CH] = out[...]
    packed[...] = wide_rows[:ROWS, :].astype(low)


def pack(labels, qkv, attn, up, down, entry, vectors, table, out, order):
    near = pl.BlockSpec(memory_space=pltpu.VMEM)
    return pl.pallas_call(
        pack_kernel,
        out_shape=jax.ShapeDtypeStruct((ROWS, A_COLS + M_COLS), low),
        in_specs=[pl.BlockSpec(memory_space=pltpu.SMEM)] + [near] * 9,
        out_specs=near,
        scratch_shapes=[pltpu.VMEM((8, A_COLS + M_COLS), wide)],
        compiler_params=pltpu.CompilerParams(vmem_limit_bytes=VMEM_BYTES),
        cost_estimate=COST,
        name="pack",
    )(labels, qkv, attn, up, down, entry, vectors, table, out, order)


R_ENTRY = 4736
R_ITEM = R_ENTRY + 128
R_RIGHT = R_ITEM + ITEMS
R_OUT = 8832
R_COLS = 9728
R_PIECES = (
    (1, 0, 0, 768),
    (2, 0, 768, 1024),
    (0, 0, 1792, 768),
    (2, 1024, 2560, 1792),
    (0, 768, 4352, 384),
    (2, 2816, 5120, 256),
    (3, 0, 5376, 1536),
    (0, 1152, 6912, 384),
    (3, 1536, 7296, 1536),
    (0, 1536, 8960, 768),
)


def finish_kernel(
    own, one, two, three, places, order, qkv, attn, up, down, entry, table, out, vectors, square, rows
):
    rows[...] = jnp.zeros(rows.shape, wide)
    total = own[...].astype(wide) + one[...].astype(wide) + two[...].astype(wide) + three[...].astype(wide)
    rows[:ROWS, :] = total
    rest = rows[:, :D]
    swapped = jnp.zeros((8, D), wide)
    for _ in range(3):
        part = rest.astype(low)
        swapped = swapped + dot(part, order[...], NT)
        rest = rest - part.astype(wide)
    rows[:, :D] = swapped
    targets = (qkv, attn, up, down)
    for index, first, start, width in R_PIECES:
        for row in range(ROWS):
            targets[index][row, :, first : first + width] = rows[row : row + 1, start : start + width]
    same = iota((ROWS, ROWS), 0) == iota((ROWS, ROWS), 1)
    for k in range(NVEC):
        at = R_ENTRY + CH + k
        down_rows = jnp.broadcast_to(rows[:ROWS, at : at + 1], (ROWS, ROWS))
        vectors[k : k + 1, :] = jnp.sum(jnp.where(same, down_rows, 0.0), axis=0, keepdims=True)
    entry[...] = rows[:ROWS, R_ENTRY : R_ENTRY + CH]
    out[...] = rows[:ROWS, R_OUT : R_OUT + 2 * CH]
    by_class = dot(rows[:, R_ITEM:R_RIGHT].astype(low), places[...])
    table[...] = by_class[:ROWS, :]
    total = jnp.sum(jnp.square(by_class), axis=1, keepdims=True)
    for columns in (slice(0, R_ITEM), slice(R_RIGHT, R_COLS)):
        total = total + jnp.sum(jnp.square(rows[:, columns]), axis=1, keepdims=True)
    square[...] = jnp.broadcast_to(jnp.sum(total, axis=0, keepdims=True), (8, 128))


def finish(own, one, two, three, places, order):
    near = pl.BlockSpec(memory_space=pltpu.VMEM)
    flats = tuple(jax.ShapeDtypeStruct((ROWS, 1, width), wide) for width in WIDTHS)
    return pl.pallas_call(
        finish_kernel,
        out_shape=flats
        + (
            jax.ShapeDtypeStruct((ROWS, CH), wide),
            jax.ShapeDtypeStruct((ROWS, CLASSES), wide),
            jax.ShapeDtypeStruct((ROWS, 2 * CH), wide),
            jax.ShapeDtypeStruct((NVEC, ROWS), wide),
            jax.ShapeDtypeStruct((8, 128), wide),
        ),
        in_specs=[near] * 6,
        out_specs=(near,) * 9,
        scratch_shapes=[pltpu.VMEM((8, R_COLS), wide)],
        compiler_params=pltpu.CompilerParams(vmem_limit_bytes=16 * MIB),
        cost_estimate=COST,
        name="finish",
    )(own, one, two, three, places, order)


def adam_kernel(*refs):
    squares, gradients, states = refs[:4], refs[4:12], refs[12:36]
    results, norm_out = refs[36:60], refs[60]
    norm = jnp.sqrt(squares[0][...] + squares[1][...] + squares[2][...] + squares[3][...])
    norm_out[...] = norm[0:1, 0:1]
    factor = jnp.minimum(1.0, clip_norm / norm)[0:1, 0:1]
    for index in range(8):
        weight, first, second = (ref[...] for ref in states[3 * index : 3 * index + 3])
        gradient = gradients[index][...]
        clipped = gradient * factor.reshape((1,) * gradient.ndim)
        first_new = beta_one * first + (1.0 - beta_one) * clipped
        second_new = beta_two * second + (1.0 - beta_two) * clipped * clipped
        first_hat = first_new / (1.0 - beta_one**STEP)
        second_hat = second_new / (1.0 - beta_two**STEP)
        weight_new = weight - step_rates[index] * (
            first_hat / (jnp.sqrt(second_hat) + adam_eps) + decay_factors[index] * weight
        )
        for k, value in enumerate((first_new, second_new, weight_new)):
            results[3 * index + k][...] = value


def adam(squares, gradients, states):
    near = pl.BlockSpec(memory_space=pltpu.VMEM)
    shapes = tuple(jax.ShapeDtypeStruct(value.shape, wide) for value in states)
    return pl.pallas_call(
        adam_kernel,
        out_shape=shapes + (jax.ShapeDtypeStruct((1, 1), wide),),
        in_specs=[near] * 36,
        out_specs=(near,) * 25,
        compiler_params=pltpu.CompilerParams(vmem_limit_bytes=24 * MIB),
        cost_estimate=COST,
        name="adam",
    )(*squares, *gradients, *states)


ROUTES = (
    ("x", 1, 0, (0, 1792), (0, 768)),
    ("x", 3, 0, (1792, B_CUT), (768, 1152)),
    ("y", 1, 1, (0, 1792), (0, 384)),
    ("y", 3, 1, (1792, B_REST), (384, 1152)),
)
SIDE_QKV = QKV // 2
WIDTHS_OUT = tuple(b[1] - b[0] + a[1] - a[0] for _, _, _, b, a in ROUTES)


def by_place(value):
    return value.reshape(4, 4, 24, value.shape[1])


def both_cores(refs, columns):
    return refs[0][..., columns[0] : columns[1]].astype(wide) + refs[1][..., columns[0] : columns[1]].astype(wide)


def route_specs(m, distance):
    axis, _, side, columns, of_qkv = ROUTES[m]
    if axis == "x":
        index = lambda at: lambda *g: (g[-1][0] ^ distance(g[0]), g[-2], 0, at)
    else:
        index = lambda at: lambda *g: (g[-2], g[-1][1] ^ distance(g[0]), 0, at)
    step = of_qkv[1] - of_qkv[0]
    at = (side * SIDE_QKV + of_qkv[0]) // step
    shape = lambda width: (1, 2, 24, width) if axis == "x" else (2, 1, 24, width)
    return [pl.BlockSpec(shape(1792), index(columns[0] // 1792))] * 2 + [pl.BlockSpec(shape(step), index(at))] * 2


def own_sum(refs, m):
    columns, of_qkv = ROUTES[m][3:]
    width, step = columns[1] - columns[0], of_qkv[1] - of_qkv[0]
    return both_cores(refs[:2], (0, width)).reshape(2, 24, width), both_cores(refs[2:4], (0, step)).reshape(2, 24, step)


def fold_send_kernel(places, *refs):
    for m in range(4):
        sent = refs[16 + m]
        value, of_qkv = own_sum(refs[4 * m : 4 * m + 4], m)
        width = value.shape[-1]
        sent[0, :, :, :width] = value.astype(low)
        sent[0, :, :, width:] = of_qkv.astype(low)


def fold_send(places, left, right, qkv):
    operands, specs, out_specs = [], [], []
    for m in range(4):
        operands += route_operands(m, left, right, qkv)
        start = 1 if ROUTES[m][1] == 1 else 2
        specs += route_specs(m, lambda k, start=start: k + start)
        out_specs.append(pl.BlockSpec((1, 2, 24, WIDTHS_OUT[m]), lambda k, g, places: (k, g, 0, 0)))
    return pl.pallas_call(
        fold_send_kernel,
        grid_spec=pltpu.PrefetchScalarGridSpec(num_scalar_prefetch=1, grid=(2, 2), in_specs=specs, out_specs=out_specs),
        out_shape=[jax.ShapeDtypeStruct((2, 4, 24, width), low) for width in WIDTHS_OUT],
        compiler_params=pltpu.CompilerParams(vmem_limit_bytes=20 * MIB),
        cost_estimate=COST,
        name="fold_send",
    )(places, *operands)


def second_send_kernel(places, *refs):
    for m in range(4):
        came, sent = refs[5 * m + 4], refs[20 + m]
        value, of_qkv = own_sum(refs[5 * m : 5 * m + 4], m)
        width = value.shape[-1]
        sent[:, :, :width] = (value + came[0, :, :, :width].astype(wide)).astype(low)
        sent[:, :, width:] = (of_qkv + came[0, :, :, width:].astype(wide)).astype(low)


def slot_spec(m, here):
    slot = (0 if ROUTES[m][1] == 1 else 1) if here else (1 if ROUTES[m][1] == 1 else 0)
    return pl.BlockSpec((1, 2, 24, WIDTHS_OUT[m]), lambda g, places: (slot, g, 0, 0))


def row_spec(width):
    return pl.BlockSpec((2, 24, width), lambda g, places: (g, 0, 0))


def route_operands(m, left, right, qkv):
    return [by_place(value) for value in ((left, right)[ROUTES[m][2]] + qkv)]


def second_send(places, left, right, qkv, came):
    operands, specs = [], []
    for m in range(4):
        operands += [*route_operands(m, left, right, qkv), came[m]]
        specs += [*route_specs(m, lambda g, d=ROUTES[m][1] ^ 2: d), slot_spec(m, False)]
    return pl.pallas_call(
        second_send_kernel,
        grid_spec=pltpu.PrefetchScalarGridSpec(
            num_scalar_prefetch=1, grid=(2,), in_specs=specs, out_specs=[row_spec(width) for width in WIDTHS_OUT]
        ),
        out_shape=[jax.ShapeDtypeStruct((4, 24, width), low) for width in WIDTHS_OUT],
        compiler_params=pltpu.CompilerParams(vmem_limit_bytes=VMEM_BYTES),
        cost_estimate=COST,
        name="second_send",
    )(places, *operands)


def line_sum_kernel(places, *refs):
    left, right = refs[-2:]
    for m in range(4):
        came, late = refs[6 * m + 4 : 6 * m + 6]
        value, of_qkv = own_sum(refs[6 * m : 6 * m + 4], m)
        target, start = (left, right)[m // 2], (m % 2) * WIDTHS_OUT[m - m % 2]
        width = value.shape[-1]
        value = value + came[0, :, :, :width].astype(wide) + late[:, :, :width].astype(wide)
        target[:, :, start : start + width] = value.astype(low)
        value = of_qkv + came[0, :, :, width:].astype(wide) + late[:, :, width:].astype(wide)
        target[:, :, start + width : start + WIDTHS_OUT[m]] = value.astype(low)
    kept, other, came, late = refs[24:28]
    value = kept[0].astype(wide) + other[0].astype(wide) + came[0].astype(wide) + late[...].astype(wide)
    left[:, :, WIDTHS_OUT[0] + WIDTHS_OUT[1] :] = value.astype(low)


def line_sum(places, left, right, qkv, came, late, rest, came_rest, late_rest):
    operands, specs = [], []
    for m in range(4):
        operands += [*route_operands(m, left, right, qkv), came[m], late[m]]
        specs += [*route_specs(m, lambda g: 0), slot_spec(m, True), row_spec(WIDTHS_OUT[m])]
    operands += [by_place(value) for value in rest] + [came_rest, late_rest]
    specs += [pl.BlockSpec((1, 2, 24, REST_COLS), lambda g, places: (places[0], g, 0, 0))] * 2
    specs += [pl.BlockSpec((1, 2, 24, REST_COLS), lambda g, places: (0, g, 0, 0)), row_spec(REST_COLS)]
    widths = (R_RIGHT, R_COLS - R_RIGHT)
    return pl.pallas_call(
        line_sum_kernel,
        grid_spec=pltpu.PrefetchScalarGridSpec(
            num_scalar_prefetch=1, grid=(2,), in_specs=specs, out_specs=[row_spec(width) for width in widths]
        ),
        out_shape=[jax.ShapeDtypeStruct((4, 24, width), low) for width in widths],
        compiler_params=pltpu.CompilerParams(vmem_limit_bytes=VMEM_BYTES),
        cost_estimate=COST,
        name="line_sum",
    )(places, *operands)


def per_device(
    images,
    labels,
    crop_sizes,
    latent_cotangent,
    logdet_cotangent,
    weight_in,
    moment_in,
    second_in,
    class_table,
    moment_table,
    second_table,
    weight_qkv,
    moment_qkv,
    second_qkv,
    weight_attn,
    moment_attn,
    second_attn,
    weight_up,
    moment_up,
    second_up,
    weight_down,
    moment_down,
    second_down,
    weight_out,
    moment_out,
    second_out,
    vectors,
    moment_vectors,
    second_vectors,
):
    core = lax.axis_index("c")
    chip = lax.axis_index(("x", "y", "z"))
    half = PATCHES // 2

    order = order_matrix()
    rows_of = lambda value: jnp.transpose(value, (1, 0, 2))
    rows_down = lambda value: jnp.transpose(value, (2, 0, 1))
    packed = pack(
        labels, rows_of(weight_qkv), rows_of(weight_attn), rows_of(weight_up), rows_down(weight_down),
        weight_in.T, vectors, class_table.T, weight_out, order,
    )

    inputs = jnp.stack([images, latent_cotangent])
    mine = lax.dynamic_slice_in_dim(inputs, core * CROPS, CROPS, 1)
    theirs = swap(lax.dynamic_slice_in_dim(inputs, (1 - core) * CROPS, CROPS, 1), "c", 1)
    whole = jnp.where(
        core == 0,
        jnp.concatenate([mine, theirs], axis=-1),
        jnp.concatenate([theirs, mine], axis=-1),
    )
    flow = whole[0][:, :, ::-1]
    latent_cot = whole[1]
    logdet_cot = lax.dynamic_slice_in_dim(logdet_cotangent, core * CROPS, CROPS, 0)
    sizes = lax.dynamic_slice_in_dim(crop_sizes, core * CROPS, CROPS, 0)
    my_labels = lax.dynamic_slice_in_dim(labels, core * CROPS, CROPS, 0)

    rows_a = gather_four(packed, "z", 0).reshape(4 * ROWS, A_COLS + M_COLS)
    b_own = lax.all_gather(rows_a[:, A_COLS:], ("x", "y"), axis=0, tiled=True)
    p_own = gather_four(gather_four(rows_a[:, :P_COLS], "y", 0), "x", 0).reshape(HALF, P_COLS)
    q_own = gather_four(gather_four(rows_a[:, P_COLS:A_COLS], "x", 0), "y", 1).reshape(HALF, Q_COLS)
    p_far = swap(p_own, "c", 1)
    q_far = swap(q_own, "c", 1)

    hidden, normed, qkv, gains, entered = front(my_labels, flow, p_own, p_far, q_own, q_far)
    b_own, qkv = together((b_own, qkv))
    b_far = swap(b_own, "c", 1)
    mixed = attend(sizes, qkv)
    label_parts = q_own[::ROWS, Q_X + CH + NVEC : Q_X + CH + NVEC + 8].astype(wide).astype(jnp.int32)
    all_labels = (label_parts[:, :4] * 32 + label_parts[:, 4:]).reshape(ITEMS)
    class_places = (all_labels[:, None] == jnp.arange(CLASSES, dtype=jnp.int32)[None, :]).astype(low)
    mixed, class_places = together((mixed, class_places))
    masked_latent, d_flow, logdet_rows, d_hidden, d_mixed, vector_rows, keep_p, keep_q, send_p, send_q = middle(
        core[None], sizes, logdet_cot, hidden, mixed, gains, order, flow, latent_cot, q_own, q_far, b_own, b_far
    )
    came_p, came_q = swap(send_p, "c", 1), swap(send_q, "c", 1)
    d_parts = (*attend_back(0, sizes, qkv, d_mixed), *attend_back(1, sizes, qkv, d_mixed))
    keep_a, send_a = back_weights(d_parts, normed)
    came_a = swap(send_a, "c", 1)
    places = jnp.stack([lax.axis_index("x"), lax.axis_index("y")])
    sums = ((keep_p, came_p), (keep_q, came_q), (keep_a, came_a))
    sent = fold_send(places, *sums)
    sent, hidden_late = together((sent, hidden))
    came = [swap(value, route[0], route[1]) for value, route in zip(sent, ROUTES)]
    first_crop = (chip * 4 + core * CROPS)[None]
    keep_r, send_r, d_image = back(
        first_crop, d_parts, hidden_late, d_hidden, gains, vector_rows, entered,
        p_own, p_far, q_own, q_far, d_flow,
    )
    came_r = swap(send_r, "c", 1)
    place_x = lax.axis_index("x")

    def rest_block(distance):
        blocks = [lax.dynamic_index_in_dim(by_place(value), place_x ^ distance, 0, keepdims=False) for value in (keep_r, came_r)]
        return blocks[0].astype(wide) + blocks[1].astype(wide)

    came_rest = swap(jnp.stack([rest_block(1).astype(low), rest_block(2).astype(low)]), "x", 1)
    came, came_rest = together((came, came_rest))
    sent = second_send(places, *sums, came)
    sent_rest = (rest_block(3) + came_rest[1].astype(wide)).astype(low)
    sent, sent_rest = together((sent, sent_rest))
    late = [swap(value, route[0], route[1] ^ 2) for value, route in zip(sent, ROUTES)]
    late_rest = swap(sent_rest, "x", 3)
    left, right = line_sum(places, *sums, came, late, (keep_r, came_r), came_rest, late_rest)
    pick = lambda value: lambda place: lax.dynamic_index_in_dim(value, place, 0, keepdims=False)
    left = scatter_four(pick(left), "y").astype(low)
    right = scatter_four(pick(right), "x").astype(low)
    last = jnp.concatenate([left, right], axis=1).reshape(4, ROWS, R_COLS)
    level = lax.axis_index("z")
    parts = [lax.dynamic_index_in_dim(last, level ^ k, 0, keepdims=False) for k in range(4)]
    parts = [parts[0]] + [swap(parts[k], "z", k) for k in (1, 2, 3)]

    image_back = d_image[:, :, ::-1]
    logdet_own = logdet_rows[::8, 0]

    def to_places(value):
        kept = lax.dynamic_slice_in_dim(value, core * half, half, 2)
        came = swap(lax.dynamic_slice_in_dim(value, (1 - core) * half, half, 2), "c", 1)
        return jnp.where(
            core == 0, jnp.concatenate([kept, came], axis=0), jnp.concatenate([came, kept], axis=0)
        )

    latents = to_places(masked_latent)
    image_grad = to_places(image_back)
    came_logdet = swap(logdet_rows, "c", 1)[::8, 0]
    logdet = jnp.where(
        core == 0,
        jnp.concatenate([logdet_own, came_logdet]),
        jnp.concatenate([came_logdet, logdet_own]),
    )

    *grads, grad_entry, grad_table, grad_out, grad_vectors, square = finish(*parts, class_places, order)
    square = square + swap(square, "c", 1)
    for axis in ("z", "y"):
        square = square + swap(square, axis, 1) + swap(square, axis, 2) + swap(square, axis, 3)
    squares = [square] + [swap(square, "x", k) for k in (1, 2, 3)]

    rows_back = lambda value: jnp.transpose(value, (1, 0, 2))
    turned = lambda value: value.T
    same = lambda value: value
    views = (
        (turned, turned, grad_entry),
        (turned, turned, grad_table),
        (rows_of, rows_back, grads[0]),
        (rows_of, rows_back, grads[1]),
        (rows_of, rows_back, grads[2]),
        (rows_down, lambda value: jnp.transpose(value, (1, 2, 0)), grads[3]),
        (same, same, grad_out),
        (same, same, grad_vectors),
    )
    states = (
        (weight_in, moment_in, second_in),
        (class_table, moment_table, second_table),
        (weight_qkv, moment_qkv, second_qkv),
        (weight_attn, moment_attn, second_attn),
        (weight_up, moment_up, second_up),
        (weight_down, moment_down, second_down),
        (weight_out, moment_out, second_out),
        (vectors, moment_vectors, second_vectors),
    )
    entered_states = [view[0](value) for view, group in zip(views, states) for value in group]
    *results, norm = adam(squares, [view[2] for view in views], entered_states)
    updated = [views[k // 3][1](value) for k, value in enumerate(results)]
    return (latents, logdet, image_grad, norm.reshape(()), *updated)


def solution(mesh):
    chips = Mesh(mesh.devices.reshape(4, 4, 4, 2), ("x", "y", "z", "c"))
    dp, every = ("x", "y", "z"), ("x", "y", "z", "c")
    patches = P(dp, None, "c")
    columns, rows, last = P(None, every), P(None, every, None), P(None, None, every)
    parameters = (columns,) * 6 + (rows,) * 9 + (last,) * 3 + (P(every, None),) * 3 + (columns,) * 3
    return jax.shard_map(
        per_device,
        mesh=chips,
        in_specs=(patches, P(dp), P(dp, None), patches, P(dp)) + parameters,
        out_specs=(patches, P(dp), patches, P()) + parameters,
        check_vma=False,
    )
```
